256 devices in a mesh: gx: 16 (over y, x), gy: 8 (over z), gz: 2 (over core).
Axes of the slice: x: 4, y: 4, z: 8, core: 2. Of those that a mesh axis runs over, the one named last changes fastest.
Arguments:
- era5_columns: float32 [128, 1024, 256], P(('gx', 'gy'), None, 'gz'), may hold values from -6 to 6
- column_owner: int32 [128, 1024], P(('gx', 'gy')), may hold values from 0 to 127, as said below
- live_counts: int32 [128], P(('gx', 'gy')), may hold values from 135 to 1024, as said below
- vertical_weights: float32 [32, 32], P('gz'), may hold values from -1 to 1
- stencil_index: int32 [4, 512, 2048], P(None, 'gx', 'gy'), may hold values from 0 to 1023, as said below
- stencil_weight: float32 [4, 512, 2048], P(None, 'gx', 'gy'), may hold values from 0.1 to 1
- terrain_mask: int32 [32, 512, 2048], P('gz', 'gx', 'gy'), may hold values from 0 to 1, as said below
- fuel_start: float32 [3, 512, 2048], P(None, 'gx', 'gy'), may hold values from 0.5 to 3
Outputs:
- potential: float32 [32, 512, 2048], P('gz', 'gx', 'gy')
- wind_field: float32 [3, 32, 512, 2048], P(None, 'gz', 'gx', 'gy')
- fuel_moisture: float32 [3, 512, 2048], P(None, 'gx', 'gy')
The draws below stay inside these ranges and needn't reach their ends.
Inputs may be any that keep to these rules, and one draw needn't show every extreme that they name: `column_owner`: among the first live_counts entries of a device's row, each tile appears at least once and at most 8 times, and one tile, the same for every device, appears exactly 8 times in every row; entries after the live ones carry no meaning. A device's live ERA5 column rows are its first live_counts rows. `stencil_index`: each entry names a row s * 8 + k of the block that its grid column's tile receives, with k below the number of live rows that device s holds for that tile. `terrain_mask`: in each grid column the terrain cells are the lowest ones, at most 16 of them.
All inputs are finite; a program needn't handle non-finite values.
Results may differ from the reference program's by a relative error of at most 0.0003.
Values sent between devices are 32-bit elements; how exact they have to be, the bound alone decides.
No kernel may reach another device: no remote copies, remote signals or barrier semaphores. Data moves between devices by JAX's collectives and lax.ppermute only.
A program may use at most 64 MiB of HBM per device.

```python
import math
import jax
import jax.numpy as jnp
from jax import lax

CX = 32
CY = 256
LZ = 16
ELEV_DEV = 32
COMP = 4
CAP = 8
POINTS = 4
CLASSES = 3
ITERS = 3
PASSES = 4
TILES = 128
COLS_DEV = 1024
NE = 256
NX = 512
NY = 2048
SIGMA_LEVELS = 32
N_GX = 16
N_GY = 8
N_GZ = 2


def pair_loads(key):
    base_key = jax.random.fold_in(key, 11)
    drawn_load = jax.random.randint(jax.random.fold_in(base_key, 1), (TILES, TILES), 1, CAP + 1)
    busiest = jax.random.randint(jax.random.fold_in(base_key, 2), (), 0, TILES)
    full_device = jax.random.randint(jax.random.fold_in(base_key, 3), (), 0, TILES)
    offset_draw = jax.random.randint(jax.random.fold_in(base_key, 4), (), 0, TILES - 1)
    sparse_device = (full_device + 1 + offset_draw) % TILES
    row_ids = jnp.arange(TILES)[:, None]
    drawn_load = jnp.where(row_ids == full_device, CAP, jnp.where(row_ids == sparse_device, 1, drawn_load))
    filled = jnp.arange(TILES)[None, :] == busiest
    return jnp.where(filled, CAP, drawn_load).astype(jnp.int32)


def draw_live_counts(key, part):
    return jnp.sum(pair_loads(key), axis=1).astype(jnp.int32)


def shuffled_owners(row_load, row_key):
    positions = jnp.arange(COLS_DEV, dtype=jnp.int32)
    bounds = jnp.cumsum(row_load).astype(jnp.int32)
    grouped = jnp.searchsorted(bounds, positions, side='right').astype(jnp.int32)
    filler = jax.random.randint(jax.random.fold_in(row_key, 1), (COLS_DEV,), 0, TILES).astype(jnp.int32)
    is_live = positions < bounds[-1]
    grouped = jnp.where(is_live, grouped, filler)
    shuffle = jax.random.permutation(jax.random.fold_in(row_key, 2), COLS_DEV).astype(jnp.int32)
    scores = jnp.where(is_live, shuffle, COLS_DEV + positions)
    ordering = jnp.argsort(scores, stable=True)
    return grouped[ordering].astype(jnp.int32)


def draw_column_owner(key, part):
    row_keys = jax.random.split(jax.random.fold_in(key, 21), TILES)
    return jax.vmap(shuffled_owners)(pair_loads(key), row_keys)


def draw_stencil_index(key, part):
    tile_load = pair_loads(key)
    slot_live = (jnp.arange(CAP)[None, None, :] < tile_load[:, :, None]).astype(jnp.int32)
    per_tile = jnp.transpose(slot_live, (1, 0, 2)).reshape(TILES, TILES * CAP)
    running = jnp.cumsum(per_tile, axis=1).astype(jnp.int32)
    gx_tiles = NX // CX
    gy_tiles = NY // CY
    totals = running[:, -1].reshape(gx_tiles, 1, gy_tiles, 1)
    limits = jnp.broadcast_to(totals[None], (POINTS, gx_tiles, CX, gy_tiles, CY))
    chosen = jax.random.randint(jax.random.fold_in(key, 31), (POINTS, gx_tiles, CX, gy_tiles, CY), 0, limits).astype(jnp.int32)
    chosen = jnp.transpose(chosen, (1, 3, 0, 2, 4)).reshape(TILES, POINTS * CX * CY)
    located = jax.vmap(lambda totals_row, wanted: jnp.searchsorted(totals_row, wanted, side='right'))(running, chosen)
    located = located.reshape(gx_tiles, gy_tiles, POINTS, CX, CY)
    return jnp.transpose(located, (2, 0, 3, 1, 4)).reshape(POINTS, NX, NY).astype(jnp.int32)


def draw_terrain_mask(key, part):
    heights = jax.random.randint(jax.random.fold_in(key, 41), (NX, NY), 0, SIGMA_LEVELS // 2 + 1)
    layer_ids = jnp.arange(SIGMA_LEVELS)[:, None, None]
    return (layer_ids >= heights[None]).astype(jnp.int32)


def levels(own_key, shape, shards, least, largest):
    def one(axis_at, parts):
        draws = jax.random.uniform(jax.random.fold_in(jax.random.fold_in(own_key, 6), axis_at), (parts,), jnp.float32, least / len(shards), largest / len(shards))
        return jnp.repeat(jnp.exp(draws), shape[axis_at] // parts).reshape((-1,) + (1,) * (len(shape) - axis_at - 1))

    loudness = one(*shards[0])
    for cut in shards[1:]:
        loudness = loudness * one(*cut)
    return loudness


def scatter_about(rng, dims, spread, bound, cuts=(), kind=jnp.bfloat16):
    values = jax.random.normal(rng, dims, jnp.float32) * spread
    if len(cuts) > 0:
        values = levels(rng, dims, cuts, -0.22, 0.18) * values
    return jnp.clip(values, min=-bound, max=bound).astype(kind)


def setup_inputs(seed: int = 0) -> dict:
    seeds = jax.random.split(jax.random.key(seed), 9)
    return {
        "era5_columns": scatter_about(seeds[0], (TILES, COLS_DEV, NE), 1.0, 6.0, ((0, 128), (2, 2)), jnp.float32),
        "column_owner": draw_column_owner(jax.random.fold_in(seeds[8], 71), 0),
        "live_counts": draw_live_counts(jax.random.fold_in(seeds[8], 71), 0),
        "vertical_weights": scatter_about(seeds[3], (SIGMA_LEVELS, ELEV_DEV), ELEV_DEV ** -0.5, 1.0, ((0, 2),), jnp.float32),
        "stencil_index": draw_stencil_index(jax.random.fold_in(seeds[8], 71), 0),
        "stencil_weight": jnp.clip(jnp.exp(math.log(1.0) - 2.3025851 * jax.random.uniform(seeds[5], (POINTS, NX, NY), jnp.float32) ** levels(seeds[5], (POINTS, NX, NY), ((1, 16), (2, 8)), -0.2, 0.2)), 0.1, 1.0),
        "terrain_mask": draw_terrain_mask(jax.random.fold_in(seeds[8], 71), 0),
        "fuel_start": jnp.clip(0.5 + 2.5 * jax.random.uniform(seeds[7], (CLASSES, NX, NY), jnp.float32) ** levels(seeds[7], (CLASSES, NX, NY), ((1, 16), (2, 8)), -0.2, 0.2), 0.5, 3.0),
    }


drying_lags = (1.0, 10.0, 100.0)

def smooth_box(padded):
    along_z = 0.5 * padded[:-2] + padded[1:-1] + 0.5 * padded[2:]
    along_x = 0.5 * along_z[:, :-2] + along_z[:, 1:-1] + 0.5 * along_z[:, 2:]
    return 0.5 * along_x[:, :, :-2] + along_x[:, :, 1:-1] + 0.5 * along_x[:, :, 2:]

def operate(field_in, air_mask):
    masked = air_mask * field_in
    nearby = smooth_box(jnp.pad(masked, 1))
    return air_mask * (16.0 * masked - 2.0 * nearby) + (1.0 - air_mask) * field_in

def slot_ranks(owner_list, live_count):
    number = owner_list.shape[0]
    is_live = jnp.arange(number, dtype=jnp.int32) < live_count
    onehot = ((owner_list[:, None] == jnp.arange(TILES, dtype=jnp.int32)[None, :]) & is_live[:, None]).astype(jnp.int32)
    before = jnp.cumsum(onehot, axis=0) - onehot
    return (is_live, lax.optimization_barrier(jnp.sum(before * onehot, axis=1)).astype(jnp.int32))

def reference(era5_columns, column_owner, live_counts, vertical_weights, stencil_index, stencil_weight, terrain_mask, fuel_start):
    feature_count = era5_columns.shape[2]
    is_live, slot_rank = jax.vmap(slot_ranks)(column_owner, live_counts)
    sources = jnp.arange(TILES, dtype=jnp.int32)[:, None]
    flat_rows = jnp.where(is_live, column_owner * (TILES * CAP) + sources * CAP + slot_rank, TILES * TILES * CAP).astype(jnp.int32)
    received = jnp.zeros((TILES * TILES * CAP, feature_count), jnp.float32)
    received = received.at[flat_rows.reshape(-1)].set(era5_columns.reshape(-1, feature_count), mode='drop')
    blocks = vertical_weights.reshape(N_GZ, LZ, ELEV_DEV)

    def tile_fields(tile_no):
        first_row = (tile_no * (TILES * CAP)).astype(jnp.int32)
        buffer_rows = lax.dynamic_slice_in_dim(received, first_row, TILES * CAP, 0).reshape(TILES * CAP, N_GZ, COMP, ELEV_DEV)
        profile = jnp.einsum('sbce,bze->bczs', buffer_rows, blocks, precision=lax.Precision.HIGHEST)
        row_start = (tile_no // N_GY * CX).astype(jnp.int32)
        col_start = (tile_no % N_GY * CY).astype(jnp.int32)
        anchor = (jnp.zeros((), jnp.int32), row_start, col_start)
        indices = lax.dynamic_slice(stencil_index, anchor, (POINTS, CX, CY)).reshape(POINTS, CX * CY)
        weights = lax.dynamic_slice(stencil_weight, anchor, (POINTS, CX, CY)).reshape(POINTS, CX * CY)
        weights = weights / lax.optimization_barrier(jnp.sum(weights, axis=0))
        picked = jnp.take(profile, indices, axis=3)
        return lax.optimization_barrier(jnp.sum(picked * weights, axis=3))
    per_tile = lax.map(tile_fields, jnp.arange(TILES, dtype=jnp.int32))
    gridded_quantities = per_tile.reshape(N_GX, N_GY, N_GZ, COMP, LZ, CX, CY)
    gridded_quantities = jnp.transpose(gridded_quantities, (3, 2, 4, 0, 5, 1, 6)).reshape(COMP, SIGMA_LEVELS, NX, NY)
    zonal_velocity, meridional_velocity, kelvin_reading, saturation_percent = (gridded_quantities[0], gridded_quantities[1], gridded_quantities[2], gridded_quantities[3])
    air_mask = terrain_mask.astype(jnp.float32)
    padded_east = jnp.pad(zonal_velocity, ((0, 0), (1, 1), (0, 0)))
    padded_north = jnp.pad(meridional_velocity, ((0, 0), (0, 0), (1, 1)))
    divergence = 0.5 * (padded_east[:, 2:] - padded_east[:, :-2]) + 0.5 * (padded_north[:, :, 2:] - padded_north[:, :, :-2])
    source = air_mask * divergence
    scaling = 14.0 * air_mask + (1.0 - air_mask)
    potential = jnp.zeros_like(source)
    residual = source
    precond = residual / scaling
    direction = precond
    current = jnp.sum(residual * precond)
    for iteration in range(ITERS):
        applied = operate(direction, air_mask)
        alpha_step = current / jnp.sum(direction * applied)
        potential = potential + alpha_step * direction
        residual = residual - alpha_step * applied
        precond = residual / scaling
        updated = jnp.sum(residual * precond)
        direction = precond + updated / current * direction
        current = updated
    padded = jnp.pad(air_mask * potential, 1)
    slope_east = 0.5 * (padded[1:-1, 2:, 1:-1] - padded[1:-1, :-2, 1:-1])
    slope_north = 0.5 * (padded[1:-1, 1:-1, 2:] - padded[1:-1, 1:-1, :-2])
    slope_up = 0.5 * (padded[2:, 1:-1, 1:-1] - padded[:-2, 1:-1, 1:-1])
    wind_field = jnp.stack([air_mask * (zonal_velocity + slope_east), air_mask * (meridional_velocity + slope_north), air_mask * slope_up])
    flow_speed_norm = jnp.sqrt(lax.optimization_barrier(jnp.sum(wind_field * wind_field, axis=0)))
    profile_means = jnp.stack([lax.optimization_barrier(jnp.sum(flow_speed_norm, axis=0)), lax.optimization_barrier(jnp.sum(kelvin_reading, axis=0)), lax.optimization_barrier(jnp.sum(saturation_percent, axis=0))]) / SIGMA_LEVELS
    speed_mean, temp_mean, humid_mean = (profile_means[0], profile_means[1], profile_means[2])
    balance = 1.2 + 0.5 * jnp.tanh(humid_mean) - 0.3 * jnp.tanh(temp_mean)
    lag_table = jnp.asarray(drying_lags, jnp.float32)[:, None, None]
    decay_rate = jnp.exp(-(1.0 + 0.5 * speed_mean)[None] / lag_table)
    fuel_moisture = fuel_start
    for sweep_no in range(PASSES):
        goal_now = balance + 0.3 * math.cos(2.0 * math.pi * sweep_no / 24.0)
        fuel_moisture = goal_now + (fuel_moisture - goal_now) * decay_rate
    return (potential, wind_field, fuel_moisture)
```

```python
import functools
import math

import jax
import jax.numpy as jnp
from jax import lax
from jax.experimental import pallas as pl
from jax.experimental.pallas import tpu as pltpu
from jax.sharding import PartitionSpec as P

F32 = jnp.float32
BF16 = jnp.bfloat16
PASSES = 4
LAGS = (1.0, 10.0, 100.0)

LZ = 16
DEEP = 3
NF = 40
NS = NF + LZ
XR = 40
YR = 384
VMEM = 56 * 1024 * 1024


def params():
    return pltpu.CompilerParams(vmem_limit_bytes=VMEM)


def split(value):
    high = value.astype(BF16)
    return high, (value - high.astype(F32)).astype(BF16)


def dot_nt(a, b):
    return lax.dot_general(a, b, (((1,), (1,)), ((), ())), preferred_element_type=F32)


def profile_kernel(weights_ref, columns_ref, own_ref, send_ref):
    w_high, w_low = split(weights_ref[...])
    c_high, c_low = split(columns_ref[...])
    result = dot_nt(w_high, c_high) + dot_nt(w_high, c_low) + dot_nt(w_low, c_high)
    own_ref[...] = result[:NF]
    send_ref[...] = result[NF:]


def route_kernel(live_ref, owner_ref, own_ref, other_ref, out_ref, *, tiles, capacity):
    rows = owner_ref.shape[1]
    slots = out_ref.shape[0]
    position = lax.broadcasted_iota(jnp.int32, (1, rows), 1)
    owner = jnp.where(position < live_ref[0], owner_ref[...], -1)
    matches = lax.broadcasted_iota(jnp.int32, (tiles, rows), 0) == owner
    hits = jnp.where(matches, 1.0, 0.0)
    earlier = lax.broadcasted_iota(jnp.int32, (rows, rows), 0) < lax.broadcasted_iota(
        jnp.int32, (rows, rows), 1
    )
    before = jnp.dot(
        hits.astype(BF16), jnp.where(earlier, 1.0, 0.0).astype(BF16), preferred_element_type=F32
    )
    rank = jnp.sum(hits * before, axis=0, keepdims=True).astype(jnp.int32)
    target = jnp.where(owner >= 0, owner * capacity + rank, -1)
    place = lax.broadcasted_iota(jnp.int32, (slots, rows), 0) == target
    profile = jnp.concatenate([own_ref[: NF - 8], own_ref[NF - 8 :] + other_ref[...]], axis=0)
    high, low = split(profile)
    pad = jnp.zeros((64 - NF, rows), BF16)
    both = jnp.concatenate([high, pad, low, pad], axis=0)
    out_ref[...] = dot_nt(jnp.where(place, 1.0, 0.0).astype(BF16), both)


def lane_pick(table, lanes):
    return jnp.take_along_axis(table, lanes, axis=1)


def pick_columns(table_ref, index, weight, blocks):
    total = weight[0] + weight[1] + weight[2] + weight[3]
    acc = [None] * (NF // 8)
    for point in range(len(index)):
        lanes = jnp.broadcast_to(index[point] & 127, (8, 128))
        part = jnp.broadcast_to(index[point] >> 7, (8, 128))
        share = jnp.broadcast_to(weight[point] / total, (8, 128))
        masks = [part == b for b in range(1, blocks)]
        for g in range(NF // 8):
            value = lane_pick(table_ref[0, 8 * g : 8 * g + 8], lanes)
            for b in range(1, blocks):
                other = lane_pick(table_ref[b, 8 * g : 8 * g + 8], lanes)
                value = jnp.where(masks[b - 1], other, value)
            term = value * share
            acc[g] = term if acc[g] is None else acc[g] + term
    return acc


def gather_kernel(
    block_ref, received_ref, index_ref, weight_ref, mask_ref, far_mask_ref,
    grid_ref, low_y_ref, high_y_ref, low_x_ref, high_x_ref,
    table_ref, index_y_ref, weight_y_ref, mask_f_ref, *, blocks
):
    lower = block_ref[2] == 0
    points, rows, cols = index_ref.shape
    for b in range(blocks):
        turned = jnp.transpose(received_ref[128 * b : 128 * b + 128, :])
        table_ref[b] = turned[:NF] + turned[64 : 64 + NF]

    for h in range(cols // 128):
        at = slice(128 * h, 128 * h + 128)
        near = mask_ref[0 : 8 * rows, at]
        mask_f_ref[h, 0 : 8 * rows] = jnp.where(lower, near, far_mask_ref[:, at]).astype(F32)
        mask_f_ref[h, 8 * rows :] = mask_ref[8 * rows :, at].astype(F32)

    lane = lax.broadcasted_iota(jnp.int32, (1, 128), 1)

    for x in range(rows):
        mine = (lane >> 2) == x
        for side in range(2):
            start = 0 if side == 0 else cols - 128
            turn = (4 * x if side == 0 else 4 * x + 4) % 128
            for k in range(points):
                row = index_ref[k, x : x + 1, start : start + 128]
                row = pltpu.roll(row, turn, 1)
                index_y_ref[side, k] = jnp.where(mine, row, index_y_ref[side, k])
                row = weight_ref[k, x : x + 1, start : start + 128]
                row = pltpu.roll(row, turn, 1)
                weight_y_ref[side, k] = jnp.where(mine, row, weight_y_ref[side, k])
            out = low_y_ref if side == 0 else high_y_ref
            for g in range(LZ // 8):
                value = mask_f_ref[start // 128, pl.ds(x + g * 8 * rows, 8, stride=rows), :]
                at = slice(NF + 8 * g, NF + 8 * g + 8)
                out[at] = jnp.where(mine, pltpu.roll(value, turn, 1), out[at])

    for side, out in ((0, low_y_ref), (1, high_y_ref)):
        got = pick_columns(
            table_ref,
            [index_y_ref[side, k] for k in range(points)],
            [weight_y_ref[side, k] for k in range(points)],
            blocks,
        )
        for g in range(NF // 8):
            out[8 * g : 8 * g + 8] = got[g]

    def group_body(group, carry):
        first = pl.multiple_of(8 * group, 8)
        for h in range(cols // 128):
            at = slice(128 * h, 128 * h + 128)
            index = [index_ref[k, pl.ds(first, 8), at] for k in range(points)]
            weight = [weight_ref[k, pl.ds(first, 8), at] for k in range(points)]
            for j in range(8):
                got = pick_columns(
                    table_ref,
                    [value[j : j + 1] for value in index],
                    [value[j : j + 1] for value in weight],
                    blocks,
                )
                for g in range(NF // 8):
                    grid_ref[h, first + j, 8 * g : 8 * g + 8, :] = got[g]
        return carry

    lax.fori_loop(0, rows // 8, group_body, 0)
    for d in range(4):
        for out, x in ((low_x_ref, d), (high_x_ref, rows - 1 - d)):
            if d < 3:
                for h in range(cols // 128):
                    out[NS * d : NS * d + NF, 128 * h : 128 * h + 128] = grid_ref[h, x]
                for g in range(LZ // 8):
                    at = NS * d + NF + 8 * g
                    for h in range(cols // 128):
                        out[at : at + 8, 128 * h : 128 * h + 128] = mask_f_ref[
                            h, pl.ds(x + g * 8 * rows, 8, stride=rows), :
                        ]
            else:
                for h in range(cols // 128):
                    at = slice(128 * h, 128 * h + 128)
                    out[NS * 3 : NS * 3 + 16, at] = grid_ref[h, x, 0:16]
                    out[NS * 3 + 16 : NS * 3 + 24, at] = grid_ref[h, x, 32:40]


def ring_smooth(plane):
    plane = plane + 0.5 * (pltpu.roll(plane, 1, 0) + pltpu.roll(plane, XR - 1, 0))
    return plane + 0.5 * (pltpu.roll(plane, 1, 1) + pltpu.roll(plane, YR - 1, 1))


def basis_kernel(
    block_ref, grid_ref, mask_ref, far_mask_ref,
    right_ref, left_ref, above_ref, above_corner_ref, below_ref, below_corner_ref,
    basis_ref, moments_ref,
    ext_ref, source_ref, air_ref, last_ref, *, last_gx, last_gy
):
    gx, gy, gz = block_ref[0], block_ref[1], block_ref[2]
    lower = gz == 0
    halves, rows = grid_ref.shape[:2]
    cols = 128 * halves
    lane = lax.broadcasted_iota(jnp.int32, (8, 128), 1)

    def own_row(x, carry):
        for h in range(halves):
            ext_ref[h, pl.ds(pl.multiple_of(x * NS, 8), NF), :] = grid_ref[h, x]
        for g in range(NS // 8):
            at = slice(8 * g, 8 * g + 8)
            right = pltpu.roll(right_ref[at], (128 - 4 * x) & 127, 1)
            left = pltpu.roll(left_ref[at], (124 - 4 * x) & 127, 1)
            side = jnp.where(lane < 4, right, jnp.where(lane >= 124, left, 0.0))
            ext_ref[halves, pl.ds(pl.multiple_of(x * NS + 8 * g, 8), 8), :] = side
        return carry

    lax.fori_loop(0, rows, own_row, 0)
    for d in range(4):
        for near_ref, corner_ref, ring, origin in (
            (above_ref, above_corner_ref, rows + d, d),
            (below_ref, below_corner_ref, XR - 1 - d, rows - 1 - d),
        ):
            base = ring * NS
            for h in range(halves):
                at = slice(128 * h, 128 * h + 128)
                if d < 3:
                    ext_ref[h, base : base + NS] = near_ref[NS * d : NS * d + NS, at]
                else:
                    ext_ref[h, base : base + 16] = near_ref[NS * 3 : NS * 3 + 16, at]
                    ext_ref[h, base + 16 : base + 32] = jnp.zeros((16, 128), F32)
                    ext_ref[h, base + 32 : base + 40] = near_ref[NS * 3 + 16 : NS * 3 + 24, at]
                    ext_ref[h, base + 40 : base + NS] = jnp.zeros((LZ, 128), F32)
            for g in range(NS // 8):
                at = slice(8 * g, 8 * g + 8)
                right = pltpu.roll(corner_ref[at, 0:128], (128 - 4 * origin) % 128, 1)
                left = pltpu.roll(corner_ref[at, 128:256], (124 - 4 * origin) % 128, 1)
                side = jnp.where(lane < 4, right, jnp.where(lane >= 124, left, 0.0))
                ext_ref[halves, base + 8 * g : base + 8 * g + 8] = side

    def source_row(x, carry):
        here = pl.multiple_of(x * NS, 8)
        after = pl.multiple_of(jnp.where(x == XR - 1, 0, x + 1) * NS, 8)
        prior = pl.multiple_of(jnp.where(x == 0, XR - 1, x - 1) * NS, 8)

        def row_of(start, f):
            return jnp.concatenate(
                [ext_ref[h, pl.ds(start + f, 8), :] for h in range(halves + 1)], axis=1
            )

        def east(f):
            return row_of(after, f) - row_of(prior, f)

        def north(f):
            value = row_of(here, f)
            return pltpu.roll(value, YR - 1, 1) - pltpu.roll(value, 1, 1)

        out = pl.multiple_of(x * 24, 8)
        values = (
            0.5 * east(0) + 0.5 * north(16),
            0.5 * east(8) + 0.5 * north(24),
            0.5 * east(32) + 0.5 * pltpu.roll(north(32), 5, 0),
        )
        for g, value in enumerate(values):
            for h in range(halves + 1):
                source_ref[h, pl.ds(out + 8 * g, 8), :] = value[:, 128 * h : 128 * h + 128]
        return carry

    lax.fori_loop(0, XR, source_row, 0)

    row_id = lax.broadcasted_iota(jnp.int32, (XR, YR), 0)
    col_id = lax.broadcasted_iota(jnp.int32, (XR, YR), 1)
    row_in = (row_id < 32) | ((row_id < 36) & (gx < last_gx)) | ((row_id >= 36) & (gx > 0))
    col_in = (
        (col_id < 256) | ((col_id < 260) & (gy < last_gy)) | ((col_id >= 380) & (gy > 0))
    )
    inside = jnp.where(row_in & col_in, 1.0, 0.0)
    for layer in range(LZ + DEEP):
        picked = layer if layer < LZ else 23 - layer
        for group in range(XR // 8):
            for h in range(YR // 128):
                at = slice(128 * h, 128 * h + 128)
                x = slice(8 * group, 8 * group + 8)
                if group < 4 and h < 2:
                    if layer < LZ:
                        known = mask_ref[rows * picked + 8 * group : rows * picked + 8 * group + 8, at]
                    else:
                        known = far_mask_ref[rows * picked + 8 * group : rows * picked + 8 * group + 8, at]
                    known = known.astype(F32)
                else:
                    known = ext_ref[h, pl.ds(8 * group * NS + NF + picked, 8, stride=NS), :]
                full = inside[x, at]
                air = jnp.where(lower, known, full) if layer < LZ else jnp.where(lower, full, known)
                air_ref[layer, x, at] = air
                source = air * source_ref[h, pl.ds(8 * group * 24 + layer, 8, stride=24), :]
                value = source / (14.0 * air + (1.0 - air))
                if layer < LZ + 1:
                    basis_ref[0, layer, x, at] = value
                else:
                    last_ref[0, layer - LZ - 1, x, at] = value

    def read(k, layer):
        if layer < LZ + 1:
            return basis_ref[k, layer]
        return last_ref[k, layer - LZ - 1]

    def advance(k, layer):
        here = read(k, layer)
        beside = read(k, layer + 1)
        if layer > 0:
            beside = beside + read(k, layer - 1)
        return air_ref[layer] * (ring_smooth(here + 0.5 * beside) - here) * (1.0 / 7.0)

    sums = [None] * 6

    def add(at, value):
        value = value[:, 0:128] + value[:, 128:256]
        sums[at] = value if sums[at] is None else sums[at] + value

    for layer in range(LZ + 2):
        value = advance(0, layer)
        if layer < LZ + 1:
            basis_ref[1, layer] = value
        else:
            last_ref[1, layer - LZ - 1] = value
    for layer in range(LZ + 1):
        basis_ref[2, layer] = advance(1, layer)
    for layer in range(LZ):
        third = advance(2, layer)[0:rows, 0:cols]
        first, second, zero = (basis_ref[k, layer, 0:rows, 0:cols] for k in (1, 2, 0))
        air = air_ref[layer, 0:rows, 0:cols]
        scaling = 14.0 * air + (1.0 - air)
        zero_s, first_s, second_s = zero * scaling, first * scaling, second * scaling
        add(0, zero_s * zero)
        add(1, zero_s * first)
        add(2, first_s * first)
        add(3, first_s * second)
        add(4, second_s * second)
        add(5, second_s * third)
    rows_out = [jnp.sum(value, axis=0, keepdims=True) for value in sums]
    moments_ref[...] = jnp.concatenate(rows_out + [jnp.zeros((2, 128), F32)], axis=0)


def iterate(nu):
    def inner(a, b):
        total = None
        for i, left in enumerate(a):
            for j, right in enumerate(b):
                term = left * right * nu[i + j]
                total = term if total is None else total + term
        return total

    one = jnp.ones_like(nu[0])
    precond = [one]
    direction = [one]
    potential = []
    current = nu[0]
    for step in range(3):
        applied = (
            [direction[0]]
            + [direction[i] - direction[i - 1] for i in range(1, len(direction))]
            + [-direction[-1]]
        )
        alpha = current / inner(direction, applied)
        potential = [
            (potential[i] + alpha * d) if i < len(potential) else alpha * d
            for i, d in enumerate(direction)
        ]
        if step < 2:
            precond = [
                (precond[i] - alpha * a) if i < len(precond) else -(alpha * a)
                for i, a in enumerate(applied)
            ]
            updated = inner(precond, precond)
            ratio = updated / current
            direction = [
                (p + ratio * direction[i]) if i < len(direction) else p
                for i, p in enumerate(precond)
            ]
            current = updated
    return potential


def wind_kernel(
    block_ref, moments_ref, basis_ref, grid_ref, mask_ref,
    potential_ref, wind_ref, speed_ref, balance_ref, p_ref
):
    gz = block_ref[2]
    rows, cols = speed_ref.shape
    totals = jnp.sum(moments_ref[...], axis=1, keepdims=True)
    factors = iterate([totals[k : k + 1] for k in range(6)])
    factors = [jnp.broadcast_to(c, (8, 128)) for c in factors]
    factors = [jnp.tile(c, (XR // 8, YR // 128)) for c in factors]

    def combine(layer):
        return (
            factors[0] * basis_ref[0, layer]
            + factors[1] * basis_ref[1, layer]
            + factors[2] * basis_ref[2, layer]
        )

    for layer in range(LZ + 1):
        p_ref[layer] = combine(layer)
    upward = jnp.where(gz == 0, 0.5, -0.5)

    def wind_of(layer, below):
        here = p_ref[layer]
        slope_up = p_ref[layer + 1][0:rows, 0:cols]
        if below:
            slope_up = slope_up - p_ref[layer - 1][0:rows, 0:cols]
        slope_up = upward * slope_up
        slope_east = 0.5 * (pltpu.roll(here, XR - 1, 0) - pltpu.roll(here, 1, 0))[0:rows, 0:cols]
        slope_north = 0.5 * (pltpu.roll(here, YR - 1, 1) - pltpu.roll(here, 1, 1))[0:rows, 0:cols]
        out = jnp.where(gz == 0, layer, LZ - 1 - layer)
        potential_ref[out] = here[0:rows, 0:cols]
        for group in range(rows // 8):
            x = slice(8 * group, 8 * group + 8)
            for h in range(cols // 128):
                at = slice(128 * h, 128 * h + 128)
                east = grid_ref[h, pl.ds(8 * group * NF + layer, 8, stride=NF), :]
                north = grid_ref[h, pl.ds(8 * group * NF + LZ + layer, 8, stride=NF), :]
                air = mask_ref[out, x, at].astype(F32)
                a = air * (east + slope_east[x, at])
                b = air * (north + slope_north[x, at])
                c = air * slope_up[x, at]
                wind_ref[0, out, x, at] = a
                wind_ref[1, out, x, at] = b
                wind_ref[2, out, x, at] = c
                speed = jnp.sqrt(a * a + b * b + c * c)
                if below:
                    speed = speed_ref[x, at] + speed
                speed_ref[x, at] = speed

    for layer in range(LZ):
        wind_of(layer, layer > 0)
    for group in range(rows // 8):
        x = slice(8 * group, 8 * group + 8)
        for h in range(cols // 128):
            at = slice(128 * h, 128 * h + 128)
            temp = grid_ref[h, pl.ds(8 * group * NF + NF - 2, 8, stride=NF), :] / 32.0
            humid = grid_ref[h, pl.ds(8 * group * NF + NF - 1, 8, stride=NF), :] / 32.0
            balance_ref[x, at] = 1.2 + 0.5 * jnp.tanh(humid) - 0.3 * jnp.tanh(temp)


def shifted(block, axis, by):
    count = lax.axis_size(axis)
    pairs = [(i, i + by) for i in range(count) if 0 <= i + by < count]
    return lax.ppermute(block, axis, pairs)


def swapped(block, axis, bit):
    count = lax.axis_size(axis)
    return lax.ppermute(block, axis, [(i, i ^ bit) for i in range(count)])


def shards(
    era5_columns,
    column_owner,
    live_counts,
    vertical_weights,
    stencil_index,
    stencil_weight,
    terrain_mask,
    fuel_start,
):
    gx, gy, gz = (lax.axis_index(a).astype(jnp.int32) for a in ("gx", "gy", "gz"))
    block = jnp.stack([gx, gy, gz])
    tiles = lax.axis_size(("gx", "gy"))
    rows_in = column_owner.shape[1]
    capacity = rows_in // tiles
    slots = tiles * capacity
    blocks = slots // 128
    layers, rows, cols = terrain_mask.shape
    points = stencil_index.shape[0]
    levels = vertical_weights.shape[1]
    vmem = pl.BlockSpec(memory_space=pltpu.VMEM)
    smem = pl.BlockSpec(memory_space=pltpu.SMEM)

    weights = jnp.where(gz == 0, vertical_weights, vertical_weights[::-1])
    total = jnp.sum(vertical_weights, axis=0, keepdims=True)
    edge = weights[: -DEEP - 1 : -1]

    def at_field(value, field):
        return jnp.pad(value, ((0, 0), (field * levels, (3 - field) * levels)))

    rows_of_weights = jnp.concatenate(
        [
            at_field(weights, 0),
            at_field(weights, 1),
            jnp.zeros((2 * DEEP, 4 * levels), F32),
            at_field(total, 2),
            at_field(total, 3),
            at_field(edge, 0),
            at_field(edge, 1),
            at_field(total, 2),
            at_field(total, 3),
        ],
        axis=0,
    )
    own, leaving = pl.pallas_call(
        profile_kernel,
        out_shape=(
            jax.ShapeDtypeStruct((NF, rows_in), F32),
            jax.ShapeDtypeStruct((8, rows_in), F32),
        ),
        in_specs=[vmem] * 2,
        out_specs=(vmem, vmem),
        compiler_params=params(),
        name="profile",
    )(rows_of_weights, era5_columns[0])
    other = swapped(leaving, "gz", 1)
    far_mask = swapped(terrain_mask[8:], "gz", 1).reshape(8 * rows, cols)
    near_mask = terrain_mask.reshape(layers * rows, cols)

    outgoing = pl.pallas_call(
        functools.partial(route_kernel, tiles=tiles, capacity=capacity),
        out_shape=jax.ShapeDtypeStruct((slots, 128), F32),
        in_specs=[smem, vmem, vmem, vmem],
        out_specs=vmem,
        compiler_params=params(),
        name="route",
    )(live_counts, column_owner, own, other)
    received = lax.all_to_all(
        outgoing.reshape(tiles, capacity, 128), ("gx", "gy"), split_axis=0, concat_axis=0, tiled=True
    ).reshape(slots, 128)

    strip_rows = NS * 3 + 24
    grid, low_y, high_y, low_x, high_x = pl.pallas_call(
        functools.partial(gather_kernel, blocks=blocks),
        out_shape=(
            jax.ShapeDtypeStruct((cols // 128, rows, NF, 128), F32),
            jax.ShapeDtypeStruct((NS, 128), F32),
            jax.ShapeDtypeStruct((NS, 128), F32),
            jax.ShapeDtypeStruct((strip_rows, cols), F32),
            jax.ShapeDtypeStruct((strip_rows, cols), F32),
        ),
        in_specs=[smem] + [vmem] * 5,
        out_specs=(vmem,) * 5,
        scratch_shapes=[
            pltpu.VMEM((blocks, NF, 128), F32),
            pltpu.VMEM((2, points, 1, 128), jnp.int32),
            pltpu.VMEM((2, points, 1, 128), F32),
            pltpu.VMEM((cols // 128, layers * rows, 128), F32),
        ],
        compiler_params=params(),
        name="gather",
    )(block, received, stencil_index, stencil_weight, near_mask, far_mask)

    right = shifted(low_y, "gy", -1)
    left = shifted(high_y, "gy", 1)
    above = shifted(low_x, "gx", -1)
    below = shifted(high_x, "gx", 1)
    corners = jnp.concatenate([right, left], axis=1)
    above_corner = shifted(corners, "gx", -1)
    below_corner = shifted(corners, "gx", 1)

    basis, moments = pl.pallas_call(
        functools.partial(
            basis_kernel, last_gx=lax.axis_size("gx") - 1, last_gy=lax.axis_size("gy") - 1
        ),
        out_shape=(
            jax.ShapeDtypeStruct((3, LZ + 1, XR, YR), F32),
            jax.ShapeDtypeStruct((8, 128), F32),
        ),
        in_specs=[smem] + [vmem] * 9,
        out_specs=(vmem, vmem),
        scratch_shapes=[
            pltpu.VMEM((YR // 128, XR * NS, 128), F32),
            pltpu.VMEM((YR // 128, XR * 24, 128), F32),
            pltpu.VMEM((LZ + DEEP, XR, YR), F32),
            pltpu.VMEM((2, DEEP - 1, XR, YR), F32),
        ],
        compiler_params=params(),
        name="basis",
    )(
        block, grid, near_mask, far_mask,
        right, left, above, above_corner, below, below_corner,
    )

    moments = moments + swapped(moments, "gz", 1)
    for axis in ("gy", "gx"):
        bit = 1
        while bit < lax.axis_size(axis):
            moments = moments + swapped(moments, axis, bit)
            bit *= 2

    potential, wind_field, speed, balance = pl.pallas_call(
        wind_kernel,
        out_shape=(
            jax.ShapeDtypeStruct((layers, rows, cols), F32),
            jax.ShapeDtypeStruct((3, layers, rows, cols), F32),
            jax.ShapeDtypeStruct((rows, cols), F32),
            jax.ShapeDtypeStruct((rows, cols), F32),
        ),
        in_specs=[smem] + [vmem] * 4,
        out_specs=(vmem,) * 4,
        scratch_shapes=[pltpu.VMEM((LZ + 1, XR, YR), F32)],
        compiler_params=params(),
        name="wind",
    )(block, moments, basis, grid.reshape(cols // 128, rows * NF, 128), terrain_mask)

    speed_mean = (speed + swapped(speed, "gz", 1)) / 32.0
    lags = jnp.asarray(LAGS, F32)[:, None, None]
    decay_rate = jnp.exp(-(1.0 + 0.5 * speed_mean)[None] / lags)
    fuel_moisture = fuel_start
    for hour in range(PASSES):
        goal = balance + 0.3 * math.cos(2.0 * math.pi * hour / 24.0)
        fuel_moisture = goal + (fuel_moisture - goal) * decay_rate
    return (potential, wind_field, fuel_moisture)


def solution(mesh):
    placed = (
        P(("gx", "gy"), None, "gz"),
        P(("gx", "gy"), None),
        P(("gx", "gy")),
        P("gz", None),
        P(None, "gx", "gy"),
        P(None, "gx", "gy"),
        P("gz", "gx", "gy"),
        P(None, "gx", "gy"),
    )
    return jax.shard_map(
        shards,
        mesh=mesh,
        in_specs=placed,
        out_specs=(P("gz", "gx", "gy"), P(None, "gz", "gx", "gy"), P(None, "gx", "gy")),
        check_vma=False,
    )
```

```python
import functools
import math

import jax
import jax.numpy as jnp
from jax import lax
from jax.experimental import pallas as pl
from jax.experimental.pallas import tpu as pltpu
from jax.sharding import PartitionSpec as P

F32 = jnp.float32
BF16 = jnp.bfloat16
PASSES = 4
LAGS = (1.0, 10.0, 100.0)

LZ = 16
DEEP = 3
NF = 40
NS = NF + LZ
STRIP = NS * 3 + 24
XR = 40
YR = 384
VMEM = 56 * 1024 * 1024


def params():
    return pltpu.CompilerParams(vmem_limit_bytes=VMEM)


def split(value):
    high = value.astype(BF16)
    return high, (value - high.astype(F32)).astype(BF16)


def dot_nt(a, b):
    return lax.dot_general(a, b, (((1,), (1,)), ((), ())), preferred_element_type=F32)


def profile_kernel(block_ref, weights_ref, columns_ref, own_ref, send_ref):
    plain = weights_ref[...]
    turned = jnp.concatenate([plain[LZ - 1 - i : LZ - i] for i in range(LZ)], axis=0)
    weights = jnp.where(block_ref[2] == 0, plain, turned)
    total = jnp.sum(plain, axis=0, keepdims=True)
    edge = jnp.concatenate([weights[LZ - 1 - i : LZ - i] for i in range(DEEP)], axis=0)

    def at_field(value, field):
        blank = jnp.zeros_like(value)
        return jnp.concatenate([value if f == field else blank for f in range(4)], axis=1)

    sums = [at_field(total, 2), at_field(total, 3)]
    stack = jnp.concatenate(
        [at_field(weights, 0), at_field(weights, 1), jnp.zeros((2 * DEEP, columns_ref.shape[1]), F32)]
        + sums
        + [at_field(edge, 0), at_field(edge, 1)]
        + sums,
        axis=0,
    )
    w_high, w_low = split(stack)
    c_high, c_low = split(columns_ref[...])
    result = dot_nt(w_high, c_high) + dot_nt(w_high, c_low) + dot_nt(w_low, c_high)
    own_ref[...] = result[:NF]
    send_ref[...] = result[NF:]


def route_kernel(live_ref, owner_ref, own_ref, other_ref, out_ref, *, tiles, capacity):
    rows = owner_ref.shape[1]
    slots = out_ref.shape[0]
    position = lax.broadcasted_iota(jnp.int32, (1, rows), 1)
    owner = jnp.where(position < live_ref[0], owner_ref[...], -1)
    matches = lax.broadcasted_iota(jnp.int32, (tiles, rows), 0) == owner
    hits = jnp.where(matches, 1.0, 0.0)
    earlier = lax.broadcasted_iota(jnp.int32, (rows, rows), 0) < lax.broadcasted_iota(
        jnp.int32, (rows, rows), 1
    )
    before = jnp.dot(
        hits.astype(BF16), jnp.where(earlier, 1.0, 0.0).astype(BF16), preferred_element_type=F32
    )
    rank = jnp.sum(hits * before, axis=0, keepdims=True).astype(jnp.int32)
    target = jnp.where(owner >= 0, owner * capacity + rank, -1)
    place = lax.broadcasted_iota(jnp.int32, (slots, rows), 0) == target
    profile = jnp.concatenate([own_ref[: NF - 8], own_ref[NF - 8 :] + other_ref[...]], axis=0)
    high, low = split(profile)
    pad = jnp.zeros((64 - NF, rows), BF16)
    both = jnp.concatenate([high, pad, low, pad], axis=0)
    out_ref[...] = dot_nt(jnp.where(place, 1.0, 0.0).astype(BF16), both)


def fill_table(received_ref, table_ref):
    parts = received_ref.shape[0] // 256
    turned = [jnp.transpose(received_ref[256 * p : 256 * p + 256, :]) for p in range(parts)]
    for g in range(NF // 8):
        for half, start in ((0, 0), (1, 64)):
            rows = slice(start + 8 * g, start + 8 * g + 8)
            value = jnp.concatenate([turned[p][rows] for p in range(parts)], axis=0)
            table_ref[8 * parts * g : 8 * parts * (g + 1), 256 * half : 256 * half + 256] = (
                value.astype(BF16)
            )


def pick_columns(table_ref, index, weight):
    parts = table_ref.shape[0] // NF
    total = weight[0] + weight[1] + weight[2] + weight[3]
    slot = lax.broadcasted_iota(jnp.int32, (256, 256), 0).astype(F32).astype(BF16)
    acc = [None] * (NF // 8)
    for point in range(len(index)):
        low = jnp.broadcast_to((index[point] & 255).astype(F32), (16, 256)).astype(BF16)
        low = jnp.concatenate([low] * 16, axis=0)
        chosen = jnp.where(slot == low, jnp.ones((256, 256), BF16), jnp.zeros((256, 256), BF16))
        chosen = jnp.concatenate([chosen, chosen], axis=0)
        found = jnp.dot(table_ref[...], chosen, preferred_element_type=F32)
        part = jnp.broadcast_to(index[point] >> 8, (8, 256))
        share = jnp.broadcast_to(weight[point] / total, (8, 256))
        for g in range(NF // 8):
            values = [
                found[8 * (parts * g + p) : 8 * (parts * g + p) + 8] for p in range(parts)
            ]
            bit = 1
            while len(values) > 1:
                odd = (part & bit) != 0
                values = [
                    jnp.where(odd, values[i + 1], values[i]) for i in range(0, len(values), 2)
                ]
                bit *= 2
            term = values[0] * share
            acc[g] = term if acc[g] is None else acc[g] + term
    return acc


def pick_rows(table_ref, index_ref, weight_ref, first, steps, out_ref, base):
    points, _, cols = index_ref.shape
    index = [index_ref[k, pl.ds(first, 8), :] for k in range(points)]
    weight = [weight_ref[k, pl.ds(first, 8), :] for k in range(points)]
    for j in steps:
        got = pick_columns(
            table_ref, [value[j : j + 1] for value in index], [value[j : j + 1] for value in weight]
        )
        for g in range(NF // 8):
            for h in range(cols // 128):
                out_ref[h, base + j, 8 * g : 8 * g + 8, :] = got[g][:, 128 * h : 128 * h + 128]


def edge_kernel(
    block_ref, received_ref, index_ref, weight_ref, mask_ref, far_mask_ref,
    table_ref, edge_ref, low_y_ref, high_y_ref, low_x_ref, high_x_ref, mask_f_ref
):
    lower = block_ref[2] == 0
    points, rows, cols = index_ref.shape
    fill_table(received_ref, table_ref)
    for h in range(cols // 128):
        at = slice(128 * h, 128 * h + 128)
        near = mask_ref[0 : 8 * rows, at]
        mask_f_ref[h, 0 : 8 * rows] = jnp.where(lower, near, far_mask_ref[:, at]).astype(F32)
        mask_f_ref[h, 8 * rows :] = mask_ref[8 * rows :, at].astype(F32)

    lane = lax.broadcasted_iota(jnp.int32, (8, 128), 1)
    row = lax.broadcasted_iota(jnp.int32, (8, 128), 0)

    def packed(value_ref, k):
        sides = []
        for start, turn in ((0, 0), (cols - 128, 4)):
            total = None
            for group in range(rows // 8):
                value = value_ref[k, 8 * group : 8 * group + 8, start : start + 128]
                value = pltpu.roll(value, 32 * group + turn, 1, stride=4, stride_axis=0)
                value = jnp.where((lane >> 2) == row + 8 * group, value, jnp.zeros_like(value))
                total = value if total is None else total + value
            sides.append(jnp.sum(total, axis=0, keepdims=True))
        return jnp.concatenate(sides, axis=1)

    got = pick_columns(
        table_ref,
        [packed(index_ref, k) for k in range(points)],
        [packed(weight_ref, k) for k in range(points)],
    )
    for out, start, turn in ((low_y_ref, 0, 0), (high_y_ref, cols - 128, 4)):
        half = 0 if start == 0 else 1
        for g in range(NF // 8):
            out[8 * g : 8 * g + 8] = got[g][:, 128 * half : 128 * half + 128]
        for g in range(LZ // 8):
            total = None
            for x in range(rows):
                value = mask_f_ref[start // 128, pl.ds(x + g * 8 * rows, 8, stride=rows), :]
                value = pltpu.roll(value, (4 * x + turn) % 128, 1)
                total = value if total is None else jnp.where((lane >> 2) == x, value, total)
            out[NF + 8 * g : NF + 8 * g + 8] = total

    pick_rows(table_ref, index_ref, weight_ref, 0, range(4), edge_ref, 0)
    pick_rows(table_ref, index_ref, weight_ref, rows - 8, range(4, 8), edge_ref, 0)
    for d in range(4):
        for out, x, kept in ((low_x_ref, d, d), (high_x_ref, rows - 1 - d, 7 - d)):
            for h in range(cols // 128):
                at = slice(128 * h, 128 * h + 128)
                if d < 3:
                    out[NS * d : NS * d + NF, at] = edge_ref[h, kept]
                    for g in range(LZ // 8):
                        first = NS * d + NF + 8 * g
                        out[first : first + 8, at] = mask_f_ref[
                            h, pl.ds(x + g * 8 * rows, 8, stride=rows), :
                        ]
                else:
                    out[NS * 3 : NS * 3 + 16, at] = edge_ref[h, kept, 0:16]
                    out[NS * 3 + 16 : NS * 3 + 24, at] = edge_ref[h, kept, 32:40]


def middle_kernel(table_ref, index_ref, weight_ref, middle_ref):
    rows = index_ref.shape[1]
    pick_rows(table_ref, index_ref, weight_ref, 0, range(4, 8), middle_ref, -4)

    def body(group, carry):
        first = pl.multiple_of(8 * group, 8)
        pick_rows(table_ref, index_ref, weight_ref, first, range(8), middle_ref, first - 4)
        return carry

    lax.fori_loop(1, rows // 8 - 1, body, 0)
    pick_rows(table_ref, index_ref, weight_ref, rows - 8, range(4), middle_ref, rows - 12)


def ring_smooth(plane):
    plane = plane + 0.5 * (pltpu.roll(plane, 1, 0) + pltpu.roll(plane, XR - 1, 0))
    return plane + 0.5 * (pltpu.roll(plane, 1, 1) + pltpu.roll(plane, YR - 1, 1))


def basis_kernel(
    block_ref, edge_ref, middle_ref, mask_ref, far_mask_ref,
    right_ref, left_ref, above_ref, below_ref,
    basis_ref, moments_ref,
    ext_ref, source_ref, air_ref, last_ref, *, last_gx, last_gy
):
    gx, gy, gz = block_ref[0], block_ref[1], block_ref[2]
    lower = gz == 0
    halves, rows = middle_ref.shape[0], middle_ref.shape[1] + 8
    cols = 128 * halves
    lane = lax.broadcasted_iota(jnp.int32, (8, 128), 1)

    for h in range(halves):
        for j in range(8):
            x = j if j < 4 else rows - 8 + j
            ext_ref[h, NS * x : NS * x + NF] = edge_ref[h, j]

    def middle_row(x, carry):
        for h in range(halves):
            ext_ref[h, pl.ds(pl.multiple_of(x * NS, 8), NF), :] = middle_ref[h, x - 4]
        return carry

    lax.fori_loop(4, rows - 4, middle_row, 0)

    def own_row(x, carry):
        for g in range(NS // 8):
            at = slice(8 * g, 8 * g + 8)
            right = pltpu.roll(right_ref[at], (128 - 4 * x) & 127, 1)
            left = pltpu.roll(left_ref[at], (124 - 4 * x) & 127, 1)
            side = jnp.where(lane < 4, right, jnp.where(lane >= 124, left, 0.0))
            ext_ref[halves, pl.ds(pl.multiple_of(x * NS + 8 * g, 8), 8), :] = side
        return carry

    lax.fori_loop(0, rows, own_row, 0)
    for d in range(4):
        for near_ref, ring, origin in (
            (above_ref, rows + d, d),
            (below_ref, XR - 1 - d, rows - 1 - d),
        ):
            base = ring * NS
            for h in range(halves):
                at = slice(128 * h, 128 * h + 128)
                if d < 3:
                    ext_ref[h, base : base + NS] = near_ref[NS * d : NS * d + NS, at]
                else:
                    ext_ref[h, base : base + 16] = near_ref[NS * 3 : NS * 3 + 16, at]
                    ext_ref[h, base + 16 : base + 32] = jnp.zeros((16, 128), F32)
                    ext_ref[h, base + 32 : base + 40] = near_ref[NS * 3 + 16 : NS * 3 + 24, at]
                    ext_ref[h, base + 40 : base + NS] = jnp.zeros((LZ, 128), F32)
            for g in range(NS // 8):
                at = slice(STRIP + 8 * g, STRIP + 8 * g + 8)
                right = pltpu.roll(near_ref[at, 0:128], (128 - 4 * origin) % 128, 1)
                left = pltpu.roll(near_ref[at, 128:256], (124 - 4 * origin) % 128, 1)
                side = jnp.where(lane < 4, right, jnp.where(lane >= 124, left, 0.0))
                ext_ref[halves, base + 8 * g : base + 8 * g + 8] = side

    def source_row(x, carry):
        here = pl.multiple_of(x * NS, 8)
        after = pl.multiple_of(jnp.where(x == XR - 1, 0, x + 1) * NS, 8)
        prior = pl.multiple_of(jnp.where(x == 0, XR - 1, x - 1) * NS, 8)

        def row_of(start, f):
            return jnp.concatenate(
                [ext_ref[h, pl.ds(start + f, 8), :] for h in range(halves + 1)], axis=1
            )

        def east(f):
            return row_of(after, f) - row_of(prior, f)

        def north(f):
            value = row_of(here, f)
            return pltpu.roll(value, YR - 1, 1) - pltpu.roll(value, 1, 1)

        out = pl.multiple_of(x * 24, 8)
        values = (
            0.5 * east(0) + 0.5 * north(16),
            0.5 * east(8) + 0.5 * north(24),
            0.5 * east(32) + 0.5 * pltpu.roll(north(32), 5, 0),
        )
        for g, value in enumerate(values):
            for h in range(halves + 1):
                source_ref[h, pl.ds(out + 8 * g, 8), :] = value[:, 128 * h : 128 * h + 128]
        return carry

    lax.fori_loop(0, XR, source_row, 0)

    row_id = lax.broadcasted_iota(jnp.int32, (XR, YR), 0)
    col_id = lax.broadcasted_iota(jnp.int32, (XR, YR), 1)
    row_in = (row_id < 32) | ((row_id < 36) & (gx < last_gx)) | ((row_id >= 36) & (gx > 0))
    col_in = (
        (col_id < 256) | ((col_id < 260) & (gy < last_gy)) | ((col_id >= 380) & (gy > 0))
    )
    inside = jnp.where(row_in & col_in, 1.0, 0.0)
    for layer in range(LZ + DEEP):
        picked = layer if layer < LZ else 23 - layer
        for group in range(XR // 8):
            for h in range(YR // 128):
                at = slice(128 * h, 128 * h + 128)
                x = slice(8 * group, 8 * group + 8)
                if group < 4 and h < 2:
                    if layer < LZ:
                        known = mask_ref[rows * picked + 8 * group : rows * picked + 8 * group + 8, at]
                    else:
                        known = far_mask_ref[rows * picked + 8 * group : rows * picked + 8 * group + 8, at]
                    known = known.astype(F32)
                else:
                    known = ext_ref[h, pl.ds(8 * group * NS + NF + picked, 8, stride=NS), :]
                full = inside[x, at]
                air = jnp.where(lower, known, full) if layer < LZ else jnp.where(lower, full, known)
                air_ref[layer, x, at] = air
                source = air * source_ref[h, pl.ds(8 * group * 24 + layer, 8, stride=24), :]
                value = source / (14.0 * air + (1.0 - air))
                if layer < LZ + 1:
                    basis_ref[0, layer, x, at] = value
                else:
                    last_ref[0, layer - LZ - 1, x, at] = value

    def read(k, layer):
        if layer < LZ + 1:
            return basis_ref[k, layer]
        return last_ref[k, layer - LZ - 1]

    def advance(k, layer):
        here = read(k, layer)
        beside = read(k, layer + 1)
        if layer > 0:
            beside = beside + read(k, layer - 1)
        return air_ref[layer] * (ring_smooth(here + 0.5 * beside) - here) * (1.0 / 7.0)

    sums = [None] * 6

    def add(at, value):
        value = value[:, 0:128] + value[:, 128:256]
        sums[at] = value if sums[at] is None else sums[at] + value

    for layer in range(LZ + 2):
        value = advance(0, layer)
        if layer < LZ + 1:
            basis_ref[1, layer] = value
        else:
            last_ref[1, layer - LZ - 1] = value
    for layer in range(LZ + 1):
        basis_ref[2, layer] = advance(1, layer)
    for layer in range(LZ):
        third = advance(2, layer)[0:rows, 0:cols]
        first, second, zero = (basis_ref[k, layer, 0:rows, 0:cols] for k in (1, 2, 0))
        air = air_ref[layer, 0:rows, 0:cols]
        scaling = 14.0 * air + (1.0 - air)
        zero_s, first_s, second_s = zero * scaling, first * scaling, second * scaling
        add(0, zero_s * zero)
        add(1, zero_s * first)
        add(2, first_s * first)
        add(3, first_s * second)
        add(4, second_s * second)
        add(5, second_s * third)
    lane_id = lax.broadcasted_iota(jnp.int32, (1, 128), 1)
    packed = jnp.zeros((1, 128), F32)
    for k, value in enumerate(sums):
        value = jnp.sum(jnp.sum(value, axis=0, keepdims=True), axis=1, keepdims=True)
        packed = jnp.where(lane_id == k, value, packed)
    moments_ref[...] = jnp.broadcast_to(packed, moments_ref.shape)


def iterate(nu):
    def inner(a, b):
        total = None
        for i, left in enumerate(a):
            for j, right in enumerate(b):
                term = left * right * nu[i + j]
                total = term if total is None else total + term
        return total

    one = jnp.ones_like(nu[0])
    precond = [one]
    direction = [one]
    potential = []
    current = nu[0]
    for step in range(3):
        applied = (
            [direction[0]]
            + [direction[i] - direction[i - 1] for i in range(1, len(direction))]
            + [-direction[-1]]
        )
        alpha = current / inner(direction, applied)
        potential = [
            (potential[i] + alpha * d) if i < len(potential) else alpha * d
            for i, d in enumerate(direction)
        ]
        if step < 2:
            precond = [
                (precond[i] - alpha * a) if i < len(precond) else -(alpha * a)
                for i, a in enumerate(applied)
            ]
            updated = inner(precond, precond)
            ratio = updated / current
            direction = [
                (p + ratio * direction[i]) if i < len(direction) else p
                for i, p in enumerate(precond)
            ]
            current = updated
    return potential


def wind_kernel(
    block_ref, moments_ref, basis_ref, edge_ref, middle_ref, mask_ref,
    potential_ref, wind_ref, speed_ref, balance_ref, p_ref, grid_ref
):
    gz = block_ref[2]
    rows, cols = speed_ref.shape
    near = 4 * NF
    for h in range(cols // 128):
        grid_ref[h, 0:near] = edge_ref[h, 0:near]
        grid_ref[h, near : (rows - 4) * NF] = middle_ref[h]
        grid_ref[h, (rows - 4) * NF :] = edge_ref[h, near:]
    totals = jnp.sum(moments_ref[...], axis=0, keepdims=True)
    factors = iterate([totals[:, k : k + 1] for k in range(6)])
    factors = [jnp.broadcast_to(c, (8, 128)) for c in factors]
    factors = [jnp.tile(c, (XR // 8, YR // 128)) for c in factors]

    def combine(layer):
        return (
            factors[0] * basis_ref[0, layer]
            + factors[1] * basis_ref[1, layer]
            + factors[2] * basis_ref[2, layer]
        )

    for layer in range(LZ + 1):
        p_ref[layer] = combine(layer)
    upward = jnp.where(gz == 0, 0.5, -0.5)

    def wind_of(layer, below):
        here = p_ref[layer]
        slope_up = p_ref[layer + 1][0:rows, 0:cols]
        if below:
            slope_up = slope_up - p_ref[layer - 1][0:rows, 0:cols]
        slope_up = upward * slope_up
        slope_east = 0.5 * (pltpu.roll(here, XR - 1, 0) - pltpu.roll(here, 1, 0))[0:rows, 0:cols]
        slope_north = 0.5 * (pltpu.roll(here, YR - 1, 1) - pltpu.roll(here, 1, 1))[0:rows, 0:cols]
        out = jnp.where(gz == 0, layer, LZ - 1 - layer)
        potential_ref[out] = here[0:rows, 0:cols]
        for group in range(rows // 8):
            x = slice(8 * group, 8 * group + 8)
            for h in range(cols // 128):
                at = slice(128 * h, 128 * h + 128)
                east = grid_ref[h, pl.ds(8 * group * NF + layer, 8, stride=NF), :]
                north = grid_ref[h, pl.ds(8 * group * NF + LZ + layer, 8, stride=NF), :]
                air = mask_ref[out, x, at].astype(F32)
                a = air * (east + slope_east[x, at])
                b = air * (north + slope_north[x, at])
                c = air * slope_up[x, at]
                wind_ref[0, out, x, at] = a
                wind_ref[1, out, x, at] = b
                wind_ref[2, out, x, at] = c
                speed = jnp.sqrt(a * a + b * b + c * c)
                if below:
                    speed = speed_ref[x, at] + speed
                speed_ref[x, at] = speed

    for layer in range(LZ):
        wind_of(layer, layer > 0)
    for group in range(rows // 8):
        x = slice(8 * group, 8 * group + 8)
        for h in range(cols // 128):
            at = slice(128 * h, 128 * h + 128)
            temp = grid_ref[h, pl.ds(8 * group * NF + NF - 2, 8, stride=NF), :] / 32.0
            humid = grid_ref[h, pl.ds(8 * group * NF + NF - 1, 8, stride=NF), :] / 32.0
            balance_ref[x, at] = 1.2 + 0.5 * jnp.tanh(humid) - 0.3 * jnp.tanh(temp)


def fuel_kernel(speed_ref, other_ref, balance_ref, start_ref, out_ref):
    speed_mean = (speed_ref[...] + other_ref[...]) / 32.0
    balance = balance_ref[...]
    for kind, lag in enumerate(LAGS):
        decay_rate = jnp.exp(-(1.0 + 0.5 * speed_mean) / lag)
        moisture = start_ref[kind]
        for hour in range(PASSES):
            goal = balance + 0.3 * math.cos(2.0 * math.pi * hour / 24.0)
            moisture = goal + (moisture - goal) * decay_rate
        out_ref[kind] = moisture


def shifted(block, axis, by):
    count = lax.axis_size(axis)
    pairs = [(i, i + by) for i in range(count) if 0 <= i + by < count]
    return lax.ppermute(block, axis, pairs)


def swapped(block, axis, bit):
    count = lax.axis_size(axis)
    return lax.ppermute(block, axis, [(i, i ^ bit) for i in range(count)])


def shards(
    era5_columns,
    column_owner,
    live_counts,
    vertical_weights,
    stencil_index,
    stencil_weight,
    terrain_mask,
    fuel_start,
):
    gx, gy, gz = (lax.axis_index(a).astype(jnp.int32) for a in ("gx", "gy", "gz"))
    block = jnp.stack([gx, gy, gz])
    tiles = lax.axis_size(("gx", "gy"))
    rows_in = column_owner.shape[1]
    capacity = rows_in // tiles
    slots = tiles * capacity
    layers, rows, cols = terrain_mask.shape
    halves = cols // 128
    vmem = pl.BlockSpec(memory_space=pltpu.VMEM)
    smem = pl.BlockSpec(memory_space=pltpu.SMEM)

    def kernel(body, name, outs, operands, scratch=(), in_smem=0, cost=None):
        shapes = [jax.ShapeDtypeStruct(shape, dtype) for shape, dtype in outs]
        return pl.pallas_call(
            body,
            out_shape=tuple(shapes),
            in_specs=[smem] * in_smem + [vmem] * (len(operands) - in_smem),
            out_specs=(vmem,) * len(outs),
            scratch_shapes=[pltpu.VMEM(shape, dtype) for shape, dtype in scratch],
            compiler_params=params(),
            cost_estimate=cost,
            name=name,
        )(*operands)

    own, leaving = kernel(
        profile_kernel,
        "profile",
        [((NF, rows_in), F32), ((8, rows_in), F32)],
        [block, vertical_weights, era5_columns[0]],
        in_smem=1,
    )
    other = swapped(leaving, "gz", 1)
    far_mask = swapped(terrain_mask[8:], "gz", 1).reshape(8 * rows, cols)
    near_mask = terrain_mask.reshape(layers * rows, cols)
    (outgoing,) = kernel(
        functools.partial(route_kernel, tiles=tiles, capacity=capacity),
        "route",
        [((slots, 128), F32)],
        [live_counts, column_owner, own, other],
        in_smem=1,
    )
    outgoing, far_mask, block = lax.optimization_barrier((outgoing, far_mask, block))
    received = lax.all_to_all(
        outgoing.reshape(tiles, capacity, 128), ("gx", "gy"), split_axis=0, concat_axis=0, tiled=True
    ).reshape(slots, 128)

    table, edge, low_y, high_y, low_x, high_x = kernel(
        edge_kernel,
        "edge",
        [
            ((slots // 256 * NF, 512), BF16),
            ((halves, 8, NF, 128), F32),
            ((NS, 128), F32),
            ((NS, 128), F32),
            ((STRIP + NS, cols), F32),
            ((STRIP + NS, cols), F32),
        ],
        [block, received, stencil_index, stencil_weight, near_mask, far_mask],
        scratch=[((halves, layers * rows, 128), F32)],
        in_smem=1,
    )
    right = shifted(low_y, "gy", -1)
    left = shifted(high_y, "gy", 1)
    (middle,) = kernel(
        middle_kernel,
        "middle",
        [((halves, rows - 8, NF, 128), F32)],
        [table, stencil_index, stencil_weight],
        cost=pl.CostEstimate(flops=4_000_000_000, bytes_accessed=1_600_000, transcendentals=0),
    )
    corners = jnp.concatenate([right, left], axis=1)
    above = shifted(low_x.at[STRIP:].set(corners), "gx", -1)
    below = shifted(high_x.at[STRIP:].set(corners), "gx", 1)

    devices = tiles * lax.axis_size("gz")
    basis, moments = kernel(
        functools.partial(
            basis_kernel, last_gx=lax.axis_size("gx") - 1, last_gy=lax.axis_size("gy") - 1
        ),
        "basis",
        [((3, LZ + 1, XR, YR), F32), ((devices, 128), F32)],
        [block, edge, middle, near_mask, far_mask, right, left, above, below],
        scratch=[
            ((YR // 128, XR * NS, 128), F32),
            ((YR // 128, XR * 24, 128), F32),
            ((LZ + DEEP, XR, YR), F32),
            ((2, DEEP - 1, XR, YR), F32),
        ],
        in_smem=1,
    )
    moments = lax.all_to_all(
        moments, ("gx", "gy", "gz"), split_axis=0, concat_axis=0, tiled=True
    )
    potential, wind_field, speed, balance = kernel(
        wind_kernel,
        "wind",
        [
            ((layers, rows, cols), F32),
            ((3, layers, rows, cols), F32),
            ((rows, cols), F32),
            ((rows, cols), F32),
        ],
        [
            block,
            moments,
            basis,
            edge.reshape(halves, 8 * NF, 128),
            middle.reshape(halves, (rows - 8) * NF, 128),
            terrain_mask,
        ],
        scratch=[((LZ + 1, XR, YR), F32), ((halves, rows * NF, 128), F32)],
        in_smem=1,
    )
    (fuel_moisture,) = kernel(
        fuel_kernel,
        "fuel",
        [((len(LAGS), rows, cols), F32)],
        [speed, swapped(speed, "gz", 1), balance, fuel_start],
    )
    return (potential, wind_field, fuel_moisture)


def solution(mesh):
    placed = (
        P(("gx", "gy"), None, "gz"),
        P(("gx", "gy"), None),
        P(("gx", "gy")),
        P("gz", None),
        P(None, "gx", "gy"),
        P(None, "gx", "gy"),
        P("gz", "gx", "gy"),
        P(None, "gx", "gy"),
    )
    return jax.shard_map(
        shards,
        mesh=mesh,
        in_specs=placed,
        out_specs=(P("gz", "gx", "gy"), P(None, "gz", "gx", "gy"), P(None, "gx", "gy")),
        check_vma=False,
    )
```

```python
import functools
import math

import jax
import jax.numpy as jnp
from jax import lax
from jax.experimental import pallas as pl
from jax.experimental.pallas import tpu as pltpu
from jax.sharding import PartitionSpec as P

F32 = jnp.float32
BF16 = jnp.bfloat16
PASSES = 4
LAGS = (1.0, 10.0, 100.0)

LZ = 16
DEEP = 3
NF = 40
NS = NF + LZ
STRIP = NS * 3 + 24
XR = 40
YR = 384
VMEM = 56 * 1024 * 1024


def params():
    return pltpu.CompilerParams(vmem_limit_bytes=VMEM)


def split(value):
    high = value.astype(BF16)
    return high, (value - high.astype(F32)).astype(BF16)


def dot_nt(a, b):
    return lax.dot_general(a, b, (((1,), (1,)), ((), ())), preferred_element_type=F32)


def profile_kernel(gz_ref, weights_ref, columns_ref, own_ref, send_ref):
    plain = weights_ref[...]
    turned = jnp.concatenate([plain[LZ - 1 - i : LZ - i] for i in range(LZ)], axis=0)
    weights = jnp.where(gz_ref[0] == 0, plain, turned)
    total = jnp.sum(plain, axis=0, keepdims=True)
    edge = jnp.concatenate([weights[LZ - 1 - i : LZ - i] for i in range(DEEP)], axis=0)

    def at_field(value, field):
        blank = jnp.zeros_like(value)
        return jnp.concatenate([value if f == field else blank for f in range(4)], axis=1)

    sums = [at_field(total, 2), at_field(total, 3)]
    stack = jnp.concatenate(
        [at_field(weights, 0), at_field(weights, 1), jnp.zeros((2 * DEEP, columns_ref.shape[1]), F32)]
        + sums
        + [at_field(edge, 0), at_field(edge, 1)]
        + sums,
        axis=0,
    )
    w_high, w_low = split(stack)
    c_high, c_low = split(columns_ref[...])
    result = dot_nt(w_high, c_high) + dot_nt(w_high, c_low) + dot_nt(w_low, c_high)
    own_ref[...] = result[:NF]
    send_ref[...] = result[NF:]


def route_kernel(live_ref, owner_ref, own_ref, other_ref, out_ref, *, tiles, capacity):
    rows = owner_ref.shape[1]
    slots = tiles * capacity
    half = capacity // 2
    position = lax.broadcasted_iota(jnp.int32, (1, rows), 1)
    owner = jnp.where(position < live_ref[0], owner_ref[...], -1)
    matches = lax.broadcasted_iota(jnp.int32, (tiles, rows), 0) == owner
    hits = jnp.where(matches, 1.0, 0.0)
    earlier = lax.broadcasted_iota(jnp.int32, (rows, rows), 0) < lax.broadcasted_iota(
        jnp.int32, (rows, rows), 1
    )
    before = jnp.dot(
        hits.astype(BF16), jnp.where(earlier, 1.0, 0.0).astype(BF16), preferred_element_type=F32
    )
    rank = jnp.sum(hits * before, axis=0, keepdims=True).astype(jnp.int32)
    upper = jnp.where(rank >= half, 1, 0)
    target = jnp.where(owner >= 0, owner * half + rank + upper * (slots // 2 - half), -1)
    place = lax.broadcasted_iota(jnp.int32, (slots, rows), 0) == target
    profile = jnp.concatenate([own_ref[: NF - 8], own_ref[NF - 8 :] + other_ref[...]], axis=0)
    high, low = split(profile)
    pad = jnp.zeros((64 - NF, rows), BF16)
    both = jnp.concatenate([high, pad, low, pad], axis=0)
    placed = dot_nt(jnp.where(place, 1.0, 0.0).astype(BF16), both)
    placed = placed + pltpu.roll(placed, 64, 1)
    lane = lax.broadcasted_iota(jnp.int32, (slots // 2, 128), 1)
    out_ref[...] = jnp.where(lane < 64, placed[: slots // 2], placed[slots // 2 :])


def fill_table(received_ref, table_ref):
    blocks = received_ref.shape[0] // 256
    turned = [jnp.transpose(received_ref[256 * p : 256 * p + 256, :]) for p in range(blocks)]
    parts = 2 * blocks
    for g in range(NF // 8):
        value = jnp.concatenate(
            [
                turned[p][64 * side + 8 * g : 64 * side + 8 * g + 8]
                for side in range(2)
                for p in range(blocks)
            ],
            axis=0,
        )
        rows = slice(8 * parts * g, 8 * parts * (g + 1))
        table_ref[rows, 0:256], table_ref[rows, 256:512] = split(value)


def place_of(slot, capacity):
    half = capacity // 2
    bits = half.bit_length() - 1
    row = ((slot >> (bits + 1)) << bits) | (slot & (half - 1))
    return row, (slot >> bits) & 1


def pick_columns(table_ref, index, weight, capacity):
    parts = table_ref.shape[0] // NF
    total = weight[0] + weight[1] + weight[2] + weight[3]
    slot = lax.broadcasted_iota(jnp.int32, (256, 256), 0).astype(F32).astype(BF16)
    acc = [None] * (NF // 8)
    for point in range(len(index)):
        row, side = place_of(index[point], capacity)
        low = jnp.broadcast_to((row & 255).astype(F32), (16, 256)).astype(BF16)
        low = jnp.concatenate([low] * 16, axis=0)
        chosen = jnp.where(slot == low, jnp.ones((256, 256), BF16), jnp.zeros((256, 256), BF16))
        chosen = jnp.concatenate([chosen, chosen], axis=0)
        found = jnp.dot(table_ref[...], chosen, preferred_element_type=F32)
        part = jnp.broadcast_to((row >> 8) + side * (parts // 2), (8, 256))
        share = jnp.broadcast_to(weight[point] / total, (8, 256))
        for g in range(NF // 8):
            values = [
                found[8 * (parts * g + p) : 8 * (parts * g + p) + 8] for p in range(parts)
            ]
            bit = 1
            while len(values) > 1:
                odd = (part & bit) != 0
                values = [
                    jnp.where(odd, values[i + 1], values[i]) for i in range(0, len(values), 2)
                ]
                bit *= 2
            term = values[0] * share
            acc[g] = term if acc[g] is None else acc[g] + term
    return acc


def pick_rows(table_ref, index_ref, weight_ref, chosen, out_ref, capacity):
    points, _, cols = index_ref.shape
    for at, x in enumerate(chosen):
        got = pick_columns(
            table_ref,
            [index_ref[k, x : x + 1, :] for k in range(points)],
            [weight_ref[k, x : x + 1, :] for k in range(points)],
            capacity,
        )
        for g in range(NF // 8):
            for h in range(cols // 128):
                out_ref[h, at, 8 * g : 8 * g + 8, :] = got[g][:, 128 * h : 128 * h + 128]


def mask_kernel(gz_ref, mask_ref, far_mask_ref, mask_y_ref, mask_x_ref, mask_f_ref):
    lower = gz_ref[0] == 0
    halves = mask_f_ref.shape[0]
    rows = mask_f_ref.shape[1] // LZ
    cols = 128 * halves
    lane = lax.broadcasted_iota(jnp.int32, (8, 128), 1)
    for h in range(halves):
        at = slice(128 * h, 128 * h + 128)
        near = mask_ref[0 : 8 * rows, at]
        mask_f_ref[h, 0 : 8 * rows] = jnp.where(lower, near, far_mask_ref[:, at]).astype(F32)
        mask_f_ref[h, 8 * rows :] = mask_ref[8 * rows :, at].astype(F32)
    for side, start, turn in ((0, 0, 0), (1, cols - 128, 4)):
        for g in range(LZ // 8):
            total = None
            for x in range(rows):
                value = mask_f_ref[start // 128, pl.ds(x + g * 8 * rows, 8, stride=rows), :]
                value = pltpu.roll(value, (4 * x + turn) % 128, 1)
                total = value if total is None else jnp.where((lane >> 2) == x, value, total)
            mask_y_ref[side, 8 * g : 8 * g + 8] = total
            for d in range(3):
                x = d if side == 0 else rows - 1 - d
                for h in range(halves):
                    mask_x_ref[
                        side, LZ * d + 8 * g : LZ * d + 8 * g + 8, 128 * h : 128 * h + 128
                    ] = mask_f_ref[h, pl.ds(x + g * 8 * rows, 8, stride=rows), :]


def table_kernel(
    received_ref, index_ref, weight_ref, mask_y_ref, table_ref, low_y_ref, high_y_ref, *, capacity
):
    points, rows, cols = index_ref.shape
    fill_table(received_ref, table_ref)
    lane = lax.broadcasted_iota(jnp.int32, (8, 128), 1)
    row = lax.broadcasted_iota(jnp.int32, (8, 128), 0)

    def packed(value_ref, k):
        sides = []
        for start, turn in ((0, 0), (cols - 128, 4)):
            total = None
            for group in range(rows // 8):
                value = value_ref[k, 8 * group : 8 * group + 8, start : start + 128]
                value = pltpu.roll(value, 32 * group + turn, 1, stride=4, stride_axis=0)
                value = jnp.where((lane >> 2) == row + 8 * group, value, jnp.zeros_like(value))
                total = value if total is None else total + value
            sides.append(jnp.sum(total, axis=0, keepdims=True))
        return jnp.concatenate(sides, axis=1)

    got = pick_columns(
        table_ref,
        [packed(index_ref, k) for k in range(points)],
        [packed(weight_ref, k) for k in range(points)],
        capacity,
    )
    for side, out in ((0, low_y_ref), (1, high_y_ref)):
        for g in range(NF // 8):
            out[8 * g : 8 * g + 8] = got[g][:, 128 * side : 128 * side + 128]
        out[NF:] = mask_y_ref[side]


def edge_kernel(
    table_ref, index_ref, weight_ref, mask_x_ref, edge_ref, low_x_ref, high_x_ref, *, capacity
):
    _, rows, cols = index_ref.shape
    chosen = [0, 1, 2, 3] + [rows - 4 + j for j in range(4)]
    pick_rows(table_ref, index_ref, weight_ref, chosen, edge_ref, capacity)
    for d in range(4):
        for side, out, kept in ((0, low_x_ref, d), (1, high_x_ref, 7 - d)):
            for h in range(cols // 128):
                at = slice(128 * h, 128 * h + 128)
                if d < 3:
                    out[NS * d : NS * d + NF, at] = edge_ref[h, kept]
                    out[NS * d + NF : NS * d + NS, at] = mask_x_ref[side, LZ * d : LZ * d + LZ, at]
                else:
                    out[NS * 3 : NS * 3 + 16, at] = edge_ref[h, kept, 0:16]
                    out[NS * 3 + 16 : NS * 3 + 24, at] = edge_ref[h, kept, 32:40]


def middle_kernel(table_ref, index_ref, weight_ref, middle_ref, *, first, capacity):
    chosen = list(range(first, first + 8))
    pick_rows(table_ref, index_ref, weight_ref, chosen, middle_ref, capacity)


def holder(x, rows, edge_ref, middle_refs):
    if x < 4:
        return edge_ref, x
    if x >= rows - 4:
        return edge_ref, x - rows + 8
    return middle_refs[(x - 4) // 8], (x - 4) % 8


def ring_smooth(plane):
    plane = plane + 0.5 * (pltpu.roll(plane, 1, 0) + pltpu.roll(plane, XR - 1, 0))
    return plane + 0.5 * (pltpu.roll(plane, 1, 1) + pltpu.roll(plane, YR - 1, 1))


def basis_kernel(
    gx_ref, gy_ref, gz_ref, edge_ref, middle_0_ref, middle_1_ref, middle_2_ref, mask_ref, far_mask_ref,
    right_ref, left_ref, above_ref, below_ref,
    basis_ref, moments_ref,
    ext_ref, source_ref, air_ref, last_ref, *, last_gx, last_gy
):
    gx, gy = gx_ref[0], gy_ref[0]
    lower = gz_ref[0] == 0
    halves, rows = edge_ref.shape[0], mask_ref.shape[0] // LZ
    cols = 128 * halves
    lane = lax.broadcasted_iota(jnp.int32, (8, 128), 1)

    for x in range(rows):
        held_ref, j = holder(x, rows, edge_ref, (middle_0_ref, middle_1_ref, middle_2_ref))
        for h in range(halves):
            ext_ref[h, NS * x : NS * x + NF] = held_ref[h, j]
        for g in range(NS // 8):
            at = slice(8 * g, 8 * g + 8)
            right = pltpu.roll(right_ref[at], (128 - 4 * x) % 128, 1)
            left = pltpu.roll(left_ref[at], (124 - 4 * x) % 128, 1)
            side = jnp.where(lane < 4, right, jnp.where(lane >= 124, left, 0.0))
            ext_ref[halves, NS * x + 8 * g : NS * x + 8 * g + 8] = side

    for d in range(4):
        for near_ref, ring, origin in (
            (above_ref, rows + d, d),
            (below_ref, XR - 1 - d, rows - 1 - d),
        ):
            base = ring * NS
            for h in range(halves):
                at = slice(128 * h, 128 * h + 128)
                if d < 3:
                    ext_ref[h, base : base + NS] = near_ref[NS * d : NS * d + NS, at]
                else:
                    ext_ref[h, base : base + 16] = near_ref[NS * 3 : NS * 3 + 16, at]
                    ext_ref[h, base + 16 : base + 32] = jnp.zeros((16, 128), F32)
                    ext_ref[h, base + 32 : base + 40] = near_ref[NS * 3 + 16 : NS * 3 + 24, at]
                    ext_ref[h, base + 40 : base + NS] = jnp.zeros((LZ, 128), F32)
            for g in range(NS // 8):
                at = slice(STRIP + 8 * g, STRIP + 8 * g + 8)
                right = pltpu.roll(near_ref[at, 0:128], (128 - 4 * origin) % 128, 1)
                left = pltpu.roll(near_ref[at, 128:256], (124 - 4 * origin) % 128, 1)
                side = jnp.where(lane < 4, right, jnp.where(lane >= 124, left, 0.0))
                ext_ref[halves, base + 8 * g : base + 8 * g + 8] = side

    def source_row(x):
        here, after, prior = x * NS, (x + 1) % XR * NS, (x - 1) % XR * NS

        def row_of(start, f):
            return jnp.concatenate(
                [ext_ref[h, start + f : start + f + 8, :] for h in range(halves + 1)], axis=1
            )

        def east(f):
            return row_of(after, f) - row_of(prior, f)

        def north(f):
            value = row_of(here, f)
            return pltpu.roll(value, YR - 1, 1) - pltpu.roll(value, 1, 1)

        out = x * 24
        values = (
            0.5 * east(0) + 0.5 * north(16),
            0.5 * east(8) + 0.5 * north(24),
            0.5 * east(32) + 0.5 * pltpu.roll(north(32), 5, 0),
        )
        for g, value in enumerate(values):
            for h in range(halves + 1):
                source_ref[h, out + 8 * g : out + 8 * g + 8, :] = value[
                    :, 128 * h : 128 * h + 128
                ]

    for x in range(XR):
        source_row(x)

    row_id = lax.broadcasted_iota(jnp.int32, (XR, YR), 0)
    col_id = lax.broadcasted_iota(jnp.int32, (XR, YR), 1)
    row_in = (row_id < 32) | ((row_id < 36) & (gx < last_gx)) | ((row_id >= 36) & (gx > 0))
    col_in = (
        (col_id < 256) | ((col_id < 260) & (gy < last_gy)) | ((col_id >= 380) & (gy > 0))
    )
    inside = jnp.where(row_in & col_in, 1.0, 0.0)
    for layer in range(LZ + DEEP):
        picked = layer if layer < LZ else 23 - layer
        for group in range(XR // 8):
            for h in range(YR // 128):
                at = slice(128 * h, 128 * h + 128)
                x = slice(8 * group, 8 * group + 8)
                if group < 4 and h < 2:
                    if layer < LZ:
                        known = mask_ref[rows * picked + 8 * group : rows * picked + 8 * group + 8, at]
                    else:
                        known = far_mask_ref[rows * picked + 8 * group : rows * picked + 8 * group + 8, at]
                    known = known.astype(F32)
                else:
                    known = ext_ref[h, pl.ds(8 * group * NS + NF + picked, 8, stride=NS), :]
                full = inside[x, at]
                air = jnp.where(lower, known, full) if layer < LZ else jnp.where(lower, full, known)
                air_ref[layer, x, at] = air
                source = air * source_ref[h, pl.ds(8 * group * 24 + layer, 8, stride=24), :]
                value = source / (14.0 * air + (1.0 - air))
                if layer < LZ + 1:
                    basis_ref[0, layer, x, at] = value
                else:
                    last_ref[0, layer - LZ - 1, x, at] = value

    def read(k, layer):
        if layer < LZ + 1:
            return basis_ref[k, layer]
        return last_ref[k, layer - LZ - 1]

    def advance(k, layer):
        here = read(k, layer)
        beside = read(k, layer + 1)
        if layer > 0:
            beside = beside + read(k, layer - 1)
        return air_ref[layer] * (ring_smooth(here + 0.5 * beside) - here) * (1.0 / 7.0)

    sums = [None] * 6

    def add(at, value):
        value = value[:, 0:128] + value[:, 128:256]
        sums[at] = value if sums[at] is None else sums[at] + value

    for layer in range(LZ + 2):
        value = advance(0, layer)
        if layer < LZ + 1:
            basis_ref[1, layer] = value
        else:
            last_ref[1, layer - LZ - 1] = value
    for layer in range(LZ + 1):
        basis_ref[2, layer] = advance(1, layer)
    for layer in range(LZ):
        third = advance(2, layer)[0:rows, 0:cols]
        first, second, zero = (basis_ref[k, layer, 0:rows, 0:cols] for k in (1, 2, 0))
        air = air_ref[layer, 0:rows, 0:cols]
        scaling = 14.0 * air + (1.0 - air)
        zero_s, first_s, second_s = zero * scaling, first * scaling, second * scaling
        add(0, zero_s * zero)
        add(1, zero_s * first)
        add(2, first_s * first)
        add(3, first_s * second)
        add(4, second_s * second)
        add(5, second_s * third)
    lane_id = lax.broadcasted_iota(jnp.int32, (1, 128), 1)
    packed = jnp.zeros((1, 128), F32)
    for k, value in enumerate(sums):
        value = jnp.sum(jnp.sum(value, axis=0, keepdims=True), axis=1, keepdims=True)
        packed = jnp.where(lane_id == k, value, packed)
    moments_ref[...] = jnp.broadcast_to(packed, moments_ref.shape)


def iterate(nu):
    def inner(a, b):
        total = None
        for i, left in enumerate(a):
            for j, right in enumerate(b):
                term = left * right * nu[i + j]
                total = term if total is None else total + term
        return total

    one = jnp.ones_like(nu[0])
    precond = [one]
    direction = [one]
    potential = []
    current = nu[0]
    for step in range(3):
        applied = (
            [direction[0]]
            + [direction[i] - direction[i - 1] for i in range(1, len(direction))]
            + [-direction[-1]]
        )
        alpha = current / inner(direction, applied)
        potential = [
            (potential[i] + alpha * d) if i < len(potential) else alpha * d
            for i, d in enumerate(direction)
        ]
        if step < 2:
            precond = [
                (precond[i] - alpha * a) if i < len(precond) else -(alpha * a)
                for i, a in enumerate(applied)
            ]
            updated = inner(precond, precond)
            ratio = updated / current
            direction = [
                (p + ratio * direction[i]) if i < len(direction) else p
                for i, p in enumerate(precond)
            ]
            current = updated
    return potential


def wind_kernel(
    gz_ref, moments_ref, basis_ref, edge_ref, middle_0_ref, middle_1_ref, middle_2_ref, mask_ref,
    potential_ref, wind_ref, speed_ref, balance_ref, p_ref, grid_ref
):
    gz = gz_ref[0]
    rows, cols = speed_ref.shape
    near = 4 * NF
    for h in range(cols // 128):
        grid_ref[h, 0:near] = edge_ref[h, 0:near]
        for i, held_ref in enumerate((middle_0_ref, middle_1_ref, middle_2_ref)):
            grid_ref[h, near + 8 * NF * i : near + 8 * NF * (i + 1)] = held_ref[h]
        grid_ref[h, (rows - 4) * NF :] = edge_ref[h, near:]
    totals = jnp.sum(moments_ref[...], axis=0, keepdims=True)
    factors = iterate([totals[:, k : k + 1] for k in range(6)])
    factors = [jnp.broadcast_to(c, (8, 128)) for c in factors]
    factors = [jnp.tile(c, (XR // 8, YR // 128)) for c in factors]

    def combine(layer):
        return (
            factors[0] * basis_ref[0, layer]
            + factors[1] * basis_ref[1, layer]
            + factors[2] * basis_ref[2, layer]
        )

    for layer in range(LZ + 1):
        p_ref[layer] = combine(layer)
    upward = jnp.where(gz == 0, 0.5, -0.5)

    def wind_of(layer, below):
        here = p_ref[layer]
        slope_up = p_ref[layer + 1][0:rows, 0:cols]
        if below:
            slope_up = slope_up - p_ref[layer - 1][0:rows, 0:cols]
        slope_up = upward * slope_up
        slope_east = 0.5 * (pltpu.roll(here, XR - 1, 0) - pltpu.roll(here, 1, 0))[0:rows, 0:cols]
        slope_north = 0.5 * (pltpu.roll(here, YR - 1, 1) - pltpu.roll(here, 1, 1))[0:rows, 0:cols]
        out = jnp.where(gz == 0, layer, LZ - 1 - layer)
        potential_ref[out] = here[0:rows, 0:cols]
        for group in range(rows // 8):
            x = slice(8 * group, 8 * group + 8)
            for h in range(cols // 128):
                at = slice(128 * h, 128 * h + 128)
                east = grid_ref[h, pl.ds(8 * group * NF + layer, 8, stride=NF), :]
                north = grid_ref[h, pl.ds(8 * group * NF + LZ + layer, 8, stride=NF), :]
                air = mask_ref[out, x, at].astype(F32)
                a = air * (east + slope_east[x, at])
                b = air * (north + slope_north[x, at])
                c = air * slope_up[x, at]
                wind_ref[0, out, x, at] = a
                wind_ref[1, out, x, at] = b
                wind_ref[2, out, x, at] = c
                speed = jnp.sqrt(a * a + b * b + c * c)
                if below:
                    speed = speed_ref[x, at] + speed
                speed_ref[x, at] = speed

    for layer in range(LZ):
        wind_of(layer, layer > 0)
    for group in range(rows // 8):
        x = slice(8 * group, 8 * group + 8)
        for h in range(cols // 128):
            at = slice(128 * h, 128 * h + 128)
            temp = grid_ref[h, pl.ds(8 * group * NF + NF - 2, 8, stride=NF), :] / 32.0
            humid = grid_ref[h, pl.ds(8 * group * NF + NF - 1, 8, stride=NF), :] / 32.0
            balance_ref[x, at] = 1.2 + 0.5 * jnp.tanh(humid) - 0.3 * jnp.tanh(temp)


def fuel_kernel(speed_ref, other_ref, balance_ref, start_ref, out_ref):
    speed_mean = (speed_ref[...] + other_ref[...]) / 32.0
    balance = balance_ref[...]
    for kind, lag in enumerate(LAGS):
        decay_rate = jnp.exp(-(1.0 + 0.5 * speed_mean) / lag)
        moisture = start_ref[kind]
        for hour in range(PASSES):
            goal = balance + 0.3 * math.cos(2.0 * math.pi * hour / 24.0)
            moisture = goal + (moisture - goal) * decay_rate
        out_ref[kind] = moisture


def shifted(block, axis, by):
    count = lax.axis_size(axis)
    pairs = [(i, i + by) for i in range(count) if 0 <= i + by < count]
    return lax.ppermute(block, axis, pairs)


def swapped(block, axis, bit):
    count = lax.axis_size(axis)
    return lax.ppermute(block, axis, [(i, i ^ bit) for i in range(count)])


def shards(
    era5_columns,
    column_owner,
    live_counts,
    vertical_weights,
    stencil_index,
    stencil_weight,
    terrain_mask,
    fuel_start,
):
    gx, gy, gz = (lax.axis_index(a).astype(jnp.int32) for a in ("gx", "gy", "gz"))
    gx, gy, gz = gx.reshape(1), gy.reshape(1), gz.reshape(1)
    tiles = lax.axis_size(("gx", "gy"))
    rows_in = column_owner.shape[1]
    capacity = rows_in // tiles
    slots = tiles * capacity
    layers, rows, cols = terrain_mask.shape
    halves = cols // 128
    vmem = pl.BlockSpec(memory_space=pltpu.VMEM)
    smem = pl.BlockSpec(memory_space=pltpu.SMEM)

    def kernel(body, name, outs, operands, scratch=(), in_smem=0, cost=None):
        shapes = [jax.ShapeDtypeStruct(shape, dtype) for shape, dtype in outs]
        return pl.pallas_call(
            body,
            out_shape=tuple(shapes),
            in_specs=[smem] * in_smem + [vmem] * (len(operands) - in_smem),
            out_specs=(vmem,) * len(outs),
            scratch_shapes=[pltpu.VMEM(shape, dtype) for shape, dtype in scratch],
            compiler_params=params(),
            cost_estimate=cost,
            name=name,
        )(*operands)

    own, leaving = kernel(
        profile_kernel,
        "profile",
        [((NF, rows_in), F32), ((8, rows_in), F32)],
        [gz, vertical_weights, era5_columns[0]],
        in_smem=1,
    )
    other = swapped(leaving, "gz", 1)
    far_mask = swapped(terrain_mask[8:], "gz", 1).reshape(8 * rows, cols)
    near_mask = terrain_mask.reshape(layers * rows, cols)
    mask_y, mask_x = kernel(
        mask_kernel,
        "mask",
        [((2, LZ, 128), F32), ((2, 3 * LZ, cols), F32)],
        [gz, near_mask, far_mask],
        scratch=[((halves, layers * rows, 128), F32)],
        in_smem=1,
        cost=pl.CostEstimate(flops=3_000_000, bytes_accessed=3_000_000, transcendentals=0),
    )
    other, mask_y, mask_x = lax.optimization_barrier((other, mask_y, mask_x))
    (outgoing,) = kernel(
        functools.partial(route_kernel, tiles=tiles, capacity=capacity),
        "route",
        [((slots // 2, 128), F32)],
        [live_counts, column_owner, own, other],
        in_smem=1,
    )
    outgoing, far_mask, mask_y, mask_x, gx, gy, gz = lax.optimization_barrier(
        (outgoing, far_mask, mask_y, mask_x, gx, gy, gz)
    )
    received = lax.all_to_all(
        outgoing.reshape(tiles, capacity // 2, 128),
        ("gx", "gy"),
        split_axis=0,
        concat_axis=0,
        tiled=True,
    ).reshape(slots // 2, 128)

    def middle(table, first):
        return kernel(
            functools.partial(middle_kernel, first=first, capacity=capacity),
            "middle" + str(first),
            [((halves, 8, NF, 128), F32)],
            [table, stencil_index, stencil_weight],
            cost=pl.CostEstimate(flops=1_500_000_000, bytes_accessed=1_000_000, transcendentals=0),
        )[0]

    table, low_y, high_y = kernel(
        functools.partial(table_kernel, capacity=capacity),
        "table",
        [((slots // 256 * NF, 512), BF16), ((NS, 128), F32), ((NS, 128), F32)],
        [received, stencil_index, stencil_weight, mask_y],
    )
    right = shifted(low_y, "gy", -1)
    edge, low_x, high_x = kernel(
        functools.partial(edge_kernel, capacity=capacity),
        "edge",
        [
            ((halves, 8, NF, 128), F32),
            ((STRIP + NS, cols), F32),
            ((STRIP + NS, cols), F32),
        ],
        [table, stencil_index, stencil_weight, mask_x],
        cost=pl.CostEstimate(flops=1_500_000_000, bytes_accessed=1_500_000, transcendentals=0),
    )
    edge, high_y = lax.optimization_barrier((edge, high_y))
    left = shifted(high_y, "gy", 1)
    table, right = lax.optimization_barrier((table, right))
    middle_0 = middle(table, 4)
    middle_0, low_x, high_x = lax.optimization_barrier((middle_0, low_x, high_x))
    corners = jnp.concatenate([right, left], axis=1)
    low_x, high_x = low_x.at[STRIP:].set(corners), high_x.at[STRIP:].set(corners)
    table, low_x, high_x = lax.optimization_barrier((table, low_x, high_x))
    above = shifted(low_x, "gx", -1)
    middle_1 = middle(table, 12)
    middle_1, table, high_x = lax.optimization_barrier((middle_1, table, high_x))
    below = shifted(high_x, "gx", 1)
    middle_2 = middle(table, 20)
    middles = (middle_0, middle_1, middle_2)

    devices = tiles * lax.axis_size("gz")
    basis, moments = kernel(
        functools.partial(
            basis_kernel, last_gx=lax.axis_size("gx") - 1, last_gy=lax.axis_size("gy") - 1
        ),
        "basis",
        [((3, LZ + 1, XR, YR), F32), ((devices, 128), F32)],
        [gx, gy, gz, edge, *middles, near_mask, far_mask, right, left, above, below],
        scratch=[
            ((YR // 128, XR * NS, 128), F32),
            ((YR // 128, XR * 24, 128), F32),
            ((LZ + DEEP, XR, YR), F32),
            ((2, DEEP - 1, XR, YR), F32),
        ],
        in_smem=3,
    )
    moments = lax.all_to_all(
        moments, ("gx", "gy", "gz"), split_axis=0, concat_axis=0, tiled=True
    )
    potential, wind_field, speed, balance = kernel(
        wind_kernel,
        "wind",
        [
            ((layers, rows, cols), F32),
            ((3, layers, rows, cols), F32),
            ((rows, cols), F32),
            ((rows, cols), F32),
        ],
        [
            gz,
            moments,
            basis,
            *(piece.reshape(halves, 8 * NF, 128) for piece in (edge, *middles)),
            terrain_mask,
        ],
        scratch=[((LZ + 1, XR, YR), F32), ((halves, rows * NF, 128), F32)],
        in_smem=1,
    )
    (fuel_moisture,) = kernel(
        fuel_kernel,
        "fuel",
        [((len(LAGS), rows, cols), F32)],
        [speed, swapped(speed, "gz", 1), balance, fuel_start],
    )
    return (potential, wind_field, fuel_moisture)


def solution(mesh):
    placed = (
        P(("gx", "gy"), None, "gz"),
        P(("gx", "gy"), None),
        P(("gx", "gy")),
        P("gz", None),
        P(None, "gx", "gy"),
        P(None, "gx", "gy"),
        P("gz", "gx", "gy"),
        P(None, "gx", "gy"),
    )
    return jax.shard_map(
        shards,
        mesh=mesh,
        in_specs=placed,
        out_specs=(P("gz", "gx", "gy"), P(None, "gz", "gx", "gy"), P(None, "gx", "gy")),
        check_vma=False,
    )
```

```python
import functools
import math

import jax
import jax.numpy as jnp
from jax import lax
from jax.experimental import pallas as pl
from jax.experimental.pallas import tpu as pltpu
from jax.sharding import PartitionSpec as P

F32 = jnp.float32
BF16 = jnp.bfloat16
PASSES = 4
LAGS = (1.0, 10.0, 100.0)

LZ = 16
DEEP = 3
NF = 40
NS = NF + LZ
STRIP = NS * 3 + 24
XR = 40
YR = 384
VMEM = 28 * 1024 * 1024


def params():
    return pltpu.CompilerParams(vmem_limit_bytes=VMEM)


def split(value):
    high = value.astype(BF16)
    return high, (value - high.astype(F32)).astype(BF16)


def dot_nt(a, b):
    return lax.dot_general(a, b, (((1,), (1,)), ((), ())), preferred_element_type=F32)


def route_kernel(
    gz_ref, live_ref, weights_ref, columns_ref, owner_ref, out_ref, *, tiles, capacity
):
    plain = weights_ref[...]
    turned = jnp.concatenate([plain[LZ - 1 - i : LZ - i] for i in range(LZ)], axis=0)
    weights = jnp.where(gz_ref[0] == 0, plain, turned)
    total = jnp.sum(plain, axis=0, keepdims=True)
    edge = jnp.concatenate([weights[LZ - 1 - i : LZ - i] for i in range(DEEP)], axis=0)

    def at_field(value, field):
        blank = jnp.zeros_like(value)
        return jnp.concatenate([value if f == field else blank for f in range(4)], axis=1)

    sums = [at_field(total, 2), at_field(total, 3)]
    stack = jnp.concatenate(
        [at_field(weights, 0), at_field(weights, 1), jnp.zeros((2 * DEEP, columns_ref.shape[1]), F32)]
        + sums
        + [at_field(edge, 0), at_field(edge, 1)]
        + sums,
        axis=0,
    )
    w_high, w_low = split(stack)
    c_high, c_low = split(columns_ref[...])
    profile = dot_nt(w_high, c_high) + dot_nt(w_high, c_low) + dot_nt(w_low, c_high)

    rows = owner_ref.shape[1]
    slots = tiles * capacity
    half = capacity // 2
    position = lax.broadcasted_iota(jnp.int32, (1, rows), 1)
    owner = jnp.where(position < live_ref[0], owner_ref[...], -1)
    matches = lax.broadcasted_iota(jnp.int32, (tiles, rows), 0) == owner
    hits = jnp.where(matches, 1.0, 0.0)
    earlier = lax.broadcasted_iota(jnp.int32, (rows, rows), 0) < lax.broadcasted_iota(
        jnp.int32, (rows, rows), 1
    )
    before = jnp.dot(
        hits.astype(BF16), jnp.where(earlier, 1.0, 0.0).astype(BF16), preferred_element_type=F32
    )
    rank = jnp.sum(hits * before, axis=0, keepdims=True).astype(jnp.int32)
    upper = jnp.where(rank >= half, 1, 0)
    target = jnp.where(owner >= 0, owner * half + rank + upper * (slots // 2 - half), -1)
    place = lax.broadcasted_iota(jnp.int32, (slots, rows), 0) == target
    high, low = split(profile)
    pad = jnp.zeros((64 - NF - 8, rows), BF16)
    both = jnp.concatenate([high, pad, low, pad], axis=0)
    placed = dot_nt(jnp.where(place, 1.0, 0.0).astype(BF16), both)
    placed = placed + pltpu.roll(placed, 64, 1)
    lane = lax.broadcasted_iota(jnp.int32, (slots // 2, 128), 1)
    out_ref[...] = jnp.where(lane < 64, placed[: slots // 2], placed[slots // 2 :])


def fill_table(received_ref, other_ref, table_ref):
    blocks = received_ref.shape[0] // 256
    turned = [jnp.transpose(received_ref[256 * p : 256 * p + 256, :]) for p in range(blocks)]
    beyond = [jnp.transpose(other_ref[256 * p : 256 * p + 256, :]) for p in range(blocks)]
    parts = 2 * blocks
    for g in range(NF // 8):
        value = jnp.concatenate(
            [
                turned[p][64 * side + 8 * g : 64 * side + 8 * g + 8]
                for side in range(2)
                for p in range(blocks)
            ],
            axis=0,
        )
        if g == NF // 8 - 1:
            value = value + jnp.concatenate(
                [
                    beyond[p][64 * side + NF : 64 * side + NF + 8]
                    for side in range(2)
                    for p in range(blocks)
                ],
                axis=0,
            )
        rows = slice(8 * parts * g, 8 * parts * (g + 1))
        table_ref[rows, 0:256], table_ref[rows, 256:512] = split(value)


def place_of(slot, capacity):
    half = capacity // 2
    bits = half.bit_length() - 1
    row = ((slot >> (bits + 1)) << bits) | (slot & (half - 1))
    return row, (slot >> bits) & 1


def pick_columns(table_ref, index, weight, capacity):
    parts = table_ref.shape[0] // NF
    total = weight[0] + weight[1] + weight[2] + weight[3]
    slot = lax.broadcasted_iota(jnp.int32, (256, 256), 0).astype(F32).astype(BF16)
    acc = [None] * (NF // 8)
    for point in range(len(index)):
        row, side = place_of(index[point], capacity)
        low = jnp.broadcast_to((row & 255).astype(F32), (16, 256)).astype(BF16)
        low = jnp.concatenate([low] * 16, axis=0)
        chosen = jnp.where(slot == low, jnp.ones((256, 256), BF16), jnp.zeros((256, 256), BF16))
        chosen = jnp.concatenate([chosen, chosen], axis=0)
        found = jnp.dot(table_ref[...], chosen, preferred_element_type=F32)
        part = jnp.broadcast_to((row >> 8) + side * (parts // 2), (8, 256))
        share = jnp.broadcast_to(weight[point] / total, (8, 256))
        for g in range(NF // 8):
            values = [
                found[8 * (parts * g + p) : 8 * (parts * g + p) + 8] for p in range(parts)
            ]
            bit = 1
            while len(values) > 1:
                odd = (part & bit) != 0
                values = [
                    jnp.where(odd, values[i + 1], values[i]) for i in range(0, len(values), 2)
                ]
                bit *= 2
            term = values[0] * share
            acc[g] = term if acc[g] is None else acc[g] + term
    return acc


def pick_rows(table_ref, index_ref, weight_ref, chosen, out_ref, capacity):
    points, _, cols = index_ref.shape
    for at, x in enumerate(chosen):
        got = pick_columns(
            table_ref,
            [index_ref[k, x : x + 1, :] for k in range(points)],
            [weight_ref[k, x : x + 1, :] for k in range(points)],
            capacity,
        )
        for g in range(NF // 8):
            for h in range(cols // 128):
                out_ref[h, at, 8 * g : 8 * g + 8, :] = got[g][:, 128 * h : 128 * h + 128]


def fill_mask(lower, mask_ref, far_mask_ref, mask_f_ref):
    first = mask_ref.shape[0] // 2 - far_mask_ref.shape[0]
    last = first + far_mask_ref.shape[0]
    for h in range(mask_f_ref.shape[0]):
        at = slice(128 * h, 128 * h + 128)
        mask_f_ref[h, 0:first] = mask_ref[0:first, at].astype(F32)
        mask_f_ref[h, first:last] = jnp.where(
            lower, mask_ref[first:last, at], far_mask_ref[:, at]
        ).astype(F32)
        mask_f_ref[h, last:] = mask_ref[last:, at].astype(F32)


def table_kernel(
    gz_ref, received_ref, other_ref, index_ref, weight_ref, mask_ref, far_mask_ref,
    table_ref, low_y_ref, high_y_ref, mask_f_ref, *, capacity
):
    points, rows, cols = index_ref.shape
    fill_table(received_ref, other_ref, table_ref)
    fill_mask(gz_ref[0] == 0, mask_ref, far_mask_ref, mask_f_ref)
    lane = lax.broadcasted_iota(jnp.int32, (8, 128), 1)
    row = lax.broadcasted_iota(jnp.int32, (8, 128), 0)

    def packed(value_ref, k):
        sides = []
        for start, turn in ((0, 0), (cols - 128, 4)):
            total = None
            for group in range(rows // 8):
                value = value_ref[k, 8 * group : 8 * group + 8, start : start + 128]
                value = pltpu.roll(value, 32 * group + turn, 1, stride=4, stride_axis=0)
                value = jnp.where((lane >> 2) == row + 8 * group, value, jnp.zeros_like(value))
                total = value if total is None else total + value
            sides.append(jnp.sum(total, axis=0, keepdims=True))
        return jnp.concatenate(sides, axis=1)

    got = pick_columns(
        table_ref,
        [packed(index_ref, k) for k in range(points)],
        [packed(weight_ref, k) for k in range(points)],
        capacity,
    )
    for side, out in ((0, low_y_ref), (1, high_y_ref)):
        for g in range(NF // 8):
            out[8 * g : 8 * g + 8] = got[g][:, 128 * side : 128 * side + 128]
        start, turn = ((0, 0), (cols - 128, 4))[side]
        for g in range(LZ // 8):
            total = None
            for x in range(rows):
                value = mask_f_ref[start // 128, pl.ds(x + g * 8 * rows, 8, stride=rows), :]
                value = pltpu.roll(value, (4 * x + turn) % 128, 1)
                total = value if total is None else jnp.where((lane >> 2) == x, value, total)
            out[NF + 8 * g : NF + 8 * g + 8] = total


def edge_kernel(
    gz_ref, table_ref, index_ref, weight_ref, mask_ref, far_mask_ref,
    edge_ref, middle_ref, low_x_ref, high_x_ref, mask_f_ref, *, capacity
):
    _, rows, cols = index_ref.shape
    chosen = [0, 1, 2, 3] + [rows - 4 + j for j in range(4)]
    pick_rows(table_ref, index_ref, weight_ref, chosen, edge_ref, capacity)
    fill_mask(gz_ref[0] == 0, mask_ref, far_mask_ref, mask_f_ref)
    for d in range(4):
        for out, x, kept in ((low_x_ref, d, d), (high_x_ref, rows - 1 - d, 7 - d)):
            for h in range(cols // 128):
                at = slice(128 * h, 128 * h + 128)
                if d < 3:
                    out[NS * d : NS * d + NF, at] = edge_ref[h, kept]
                    for g in range(LZ // 8):
                        first = NS * d + NF + 8 * g
                        out[first : first + 8, at] = mask_f_ref[
                            h, pl.ds(x + g * 8 * rows, 8, stride=rows), :
                        ]
                else:
                    out[NS * 3 : NS * 3 + 16, at] = edge_ref[h, kept, 0:16]
                    out[NS * 3 + 16 : NS * 3 + 24, at] = edge_ref[h, kept, 32:40]
    pick_rows(table_ref, index_ref, weight_ref, list(range(4, 12)), middle_ref, capacity)


def middle_kernel(table_ref, index_ref, weight_ref, middle_ref, *, first, capacity):
    chosen = list(range(first, first + middle_ref.shape[1]))
    pick_rows(table_ref, index_ref, weight_ref, chosen, middle_ref, capacity)


def holder(x, rows, edge_ref, middle_refs):
    if x < 4:
        return edge_ref, x
    if x >= rows - 4:
        return edge_ref, x - rows + 8
    return (middle_refs[0], x - 4) if x < 12 else (middle_refs[1], x - 12)


def ring_smooth(plane):
    plane = plane + 0.5 * (pltpu.roll(plane, 1, 0) + pltpu.roll(plane, XR - 1, 0))
    return plane + 0.5 * (pltpu.roll(plane, 1, 1) + pltpu.roll(plane, YR - 1, 1))


def basis_kernel(
    gx_ref, gy_ref, gz_ref, edge_ref, middle_0_ref, middle_1_ref, mask_ref, far_mask_ref,
    right_ref, left_ref, above_ref, below_ref,
    basis_ref, moments_ref,
    ext_ref, source_ref, air_ref, last_ref, *, last_gx, last_gy
):
    gx, gy = gx_ref[0], gy_ref[0]
    lower = gz_ref[0] == 0
    halves, rows = edge_ref.shape[0], mask_ref.shape[0] // LZ
    cols = 128 * halves
    lane = lax.broadcasted_iota(jnp.int32, (8, 128), 1)

    for x in range(rows):
        held_ref, j = holder(x, rows, edge_ref, (middle_0_ref, middle_1_ref))
        for h in range(halves):
            ext_ref[h, NS * x : NS * x + NF] = held_ref[h, j]
        for g in range(NS // 8):
            at = slice(8 * g, 8 * g + 8)
            right = pltpu.roll(right_ref[at], (128 - 4 * x) % 128, 1)
            left = pltpu.roll(left_ref[at], (124 - 4 * x) % 128, 1)
            side = jnp.where(lane < 4, right, jnp.where(lane >= 124, left, 0.0))
            ext_ref[halves, NS * x + 8 * g : NS * x + 8 * g + 8] = side

    for d in range(4):
        for near_ref, ring, origin in (
            (above_ref, rows + d, d),
            (below_ref, XR - 1 - d, rows - 1 - d),
        ):
            base = ring * NS
            for h in range(halves):
                at = slice(128 * h, 128 * h + 128)
                if d < 3:
                    ext_ref[h, base : base + NS] = near_ref[NS * d : NS * d + NS, at]
                else:
                    ext_ref[h, base : base + 16] = near_ref[NS * 3 : NS * 3 + 16, at]
                    ext_ref[h, base + 16 : base + 32] = jnp.zeros((16, 128), F32)
                    ext_ref[h, base + 32 : base + 40] = near_ref[NS * 3 + 16 : NS * 3 + 24, at]
                    ext_ref[h, base + 40 : base + NS] = jnp.zeros((LZ, 128), F32)
            for g in range(NS // 8):
                at = slice(STRIP + 8 * g, STRIP + 8 * g + 8)
                right = pltpu.roll(near_ref[at, 0:128], (128 - 4 * origin) % 128, 1)
                left = pltpu.roll(near_ref[at, 128:256], (124 - 4 * origin) % 128, 1)
                side = jnp.where(lane < 4, right, jnp.where(lane >= 124, left, 0.0))
                ext_ref[halves, base + 8 * g : base + 8 * g + 8] = side

    def source_row(x):
        here, after, prior = x * NS, (x + 1) % XR * NS, (x - 1) % XR * NS

        def row_of(start, f):
            return jnp.concatenate(
                [ext_ref[h, start + f : start + f + 8, :] for h in range(halves + 1)], axis=1
            )

        def east(f):
            return row_of(after, f) - row_of(prior, f)

        def north(f):
            value = row_of(here, f)
            return pltpu.roll(value, YR - 1, 1) - pltpu.roll(value, 1, 1)

        out = x * 24
        values = (
            0.5 * east(0) + 0.5 * north(16),
            0.5 * east(8) + 0.5 * north(24),
            0.5 * east(32) + 0.5 * pltpu.roll(north(32), 5, 0),
        )
        for g, value in enumerate(values):
            for h in range(halves + 1):
                source_ref[h, out + 8 * g : out + 8 * g + 8, :] = value[
                    :, 128 * h : 128 * h + 128
                ]

    for x in range(XR):
        source_row(x)

    row_id = lax.broadcasted_iota(jnp.int32, (XR, YR), 0)
    col_id = lax.broadcasted_iota(jnp.int32, (XR, YR), 1)
    row_in = (row_id < 32) | ((row_id < 36) & (gx < last_gx)) | ((row_id >= 36) & (gx > 0))
    col_in = (
        (col_id < 256) | ((col_id < 260) & (gy < last_gy)) | ((col_id >= 380) & (gy > 0))
    )
    inside = jnp.where(row_in & col_in, 1.0, 0.0)
    for layer in range(LZ + DEEP):
        picked = layer if layer < LZ else 23 - layer
        for group in range(XR // 8):
            for h in range(YR // 128):
                at = slice(128 * h, 128 * h + 128)
                x = slice(8 * group, 8 * group + 8)
                if group < 4 and h < 2:
                    if layer < LZ:
                        known = mask_ref[rows * picked + 8 * group : rows * picked + 8 * group + 8, at]
                    else:
                        first = rows * (picked - 5) + 8 * group
                        known = far_mask_ref[first : first + 8, at]
                    known = known.astype(F32)
                else:
                    known = ext_ref[h, pl.ds(8 * group * NS + NF + picked, 8, stride=NS), :]
                full = inside[x, at]
                air = jnp.where(lower, known, full) if layer < LZ else jnp.where(lower, full, known)
                air_ref[layer, x, at] = air
                source = air * source_ref[h, pl.ds(8 * group * 24 + layer, 8, stride=24), :]
                value = source / (14.0 * air + (1.0 - air))
                if layer < LZ + 1:
                    basis_ref[0, layer, x, at] = value
                else:
                    last_ref[0, layer - LZ - 1, x, at] = value

    def read(k, layer):
        if layer < LZ + 1:
            return basis_ref[k, layer]
        return last_ref[k, layer - LZ - 1]

    def advance(k, layer):
        here = read(k, layer)
        beside = read(k, layer + 1)
        if layer > 0:
            beside = beside + read(k, layer - 1)
        return air_ref[layer] * (ring_smooth(here + 0.5 * beside) - here) * (1.0 / 7.0)

    sums = [None] * 6

    def add(at, value):
        value = value[:, 0:128] + value[:, 128:256]
        sums[at] = value if sums[at] is None else sums[at] + value

    for layer in range(LZ + 2):
        value = advance(0, layer)
        if layer < LZ + 1:
            basis_ref[1, layer] = value
        else:
            last_ref[1, layer - LZ - 1] = value
    for layer in range(LZ + 1):
        basis_ref[2, layer] = advance(1, layer)
    for layer in range(LZ):
        third = advance(2, layer)[0:rows, 0:cols]
        first, second, zero = (basis_ref[k, layer, 0:rows, 0:cols] for k in (1, 2, 0))
        air = air_ref[layer, 0:rows, 0:cols]
        scaling = 14.0 * air + (1.0 - air)
        zero_s, first_s, second_s = zero * scaling, first * scaling, second * scaling
        add(0, zero_s * zero)
        add(1, zero_s * first)
        add(2, first_s * first)
        add(3, first_s * second)
        add(4, second_s * second)
        add(5, second_s * third)
    lane_id = lax.broadcasted_iota(jnp.int32, (1, 128), 1)
    packed = jnp.zeros((1, 128), F32)
    for k, value in enumerate(sums):
        value = jnp.sum(jnp.sum(value, axis=0, keepdims=True), axis=1, keepdims=True)
        packed = jnp.where(lane_id == k, value, packed)
    moments_ref[...] = jnp.broadcast_to(packed, moments_ref.shape)


def iterate(nu):
    def inner(a, b):
        total = None
        for i, left in enumerate(a):
            for j, right in enumerate(b):
                term = left * right * nu[i + j]
                total = term if total is None else total + term
        return total

    one = jnp.ones_like(nu[0])
    precond = [one]
    direction = [one]
    potential = []
    current = nu[0]
    for step in range(3):
        applied = (
            [direction[0]]
            + [direction[i] - direction[i - 1] for i in range(1, len(direction))]
            + [-direction[-1]]
        )
        alpha = current / inner(direction, applied)
        potential = [
            (potential[i] + alpha * d) if i < len(potential) else alpha * d
            for i, d in enumerate(direction)
        ]
        if step < 2:
            precond = [
                (precond[i] - alpha * a) if i < len(precond) else -(alpha * a)
                for i, a in enumerate(applied)
            ]
            updated = inner(precond, precond)
            ratio = updated / current
            direction = [
                (p + ratio * direction[i]) if i < len(direction) else p
                for i, p in enumerate(precond)
            ]
            current = updated
    return potential


def wind_kernel(
    gz_ref, moments_ref, basis_ref, edge_ref, middle_0_ref, middle_1_ref, mask_ref,
    potential_ref, wind_ref, speed_ref, balance_ref, p_ref, grid_ref
):
    gz = gz_ref[0]
    rows, cols = speed_ref.shape
    near = 4 * NF
    for h in range(cols // 128):
        grid_ref[h, 0:near] = edge_ref[h, 0:near]
        grid_ref[h, near : near + 8 * NF] = middle_0_ref[h]
        grid_ref[h, near + 8 * NF : (rows - 4) * NF] = middle_1_ref[h]
        grid_ref[h, (rows - 4) * NF :] = edge_ref[h, near:]
    totals = jnp.sum(moments_ref[...], axis=0, keepdims=True)
    factors = iterate([totals[:, k : k + 1] for k in range(6)])
    factors = [jnp.broadcast_to(c, (8, 128)) for c in factors]
    factors = [jnp.tile(c, (XR // 8, YR // 128)) for c in factors]

    def combine(layer):
        return (
            factors[0] * basis_ref[0, layer]
            + factors[1] * basis_ref[1, layer]
            + factors[2] * basis_ref[2, layer]
        )

    for layer in range(LZ + 1):
        p_ref[layer] = combine(layer)
    upward = jnp.where(gz == 0, 0.5, -0.5)

    def wind_of(layer, below):
        here = p_ref[layer]
        slope_up = p_ref[layer + 1][0:rows, 0:cols]
        if below:
            slope_up = slope_up - p_ref[layer - 1][0:rows, 0:cols]
        slope_up = upward * slope_up
        slope_east = 0.5 * (pltpu.roll(here, XR - 1, 0) - pltpu.roll(here, 1, 0))[0:rows, 0:cols]
        slope_north = 0.5 * (pltpu.roll(here, YR - 1, 1) - pltpu.roll(here, 1, 1))[0:rows, 0:cols]
        out = jnp.where(gz == 0, layer, LZ - 1 - layer)
        potential_ref[out] = here[0:rows, 0:cols]
        for group in range(rows // 8):
            x = slice(8 * group, 8 * group + 8)
            for h in range(cols // 128):
                at = slice(128 * h, 128 * h + 128)
                east = grid_ref[h, pl.ds(8 * group * NF + layer, 8, stride=NF), :]
                north = grid_ref[h, pl.ds(8 * group * NF + LZ + layer, 8, stride=NF), :]
                air = mask_ref[out, x, at].astype(F32)
                a = air * (east + slope_east[x, at])
                b = air * (north + slope_north[x, at])
                c = air * slope_up[x, at]
                wind_ref[0, out, x, at] = a
                wind_ref[1, out, x, at] = b
                wind_ref[2, out, x, at] = c
                speed = jnp.sqrt(a * a + b * b + c * c)
                if below:
                    speed = speed_ref[x, at] + speed
                speed_ref[x, at] = speed

    for layer in range(LZ):
        wind_of(layer, layer > 0)
    for group in range(rows // 8):
        x = slice(8 * group, 8 * group + 8)
        for h in range(cols // 128):
            at = slice(128 * h, 128 * h + 128)
            temp = grid_ref[h, pl.ds(8 * group * NF + NF - 2, 8, stride=NF), :] / 32.0
            humid = grid_ref[h, pl.ds(8 * group * NF + NF - 1, 8, stride=NF), :] / 32.0
            balance_ref[x, at] = 1.2 + 0.5 * jnp.tanh(humid) - 0.3 * jnp.tanh(temp)


def fuel_kernel(speed_ref, other_ref, balance_ref, start_ref, out_ref):
    speed_mean = (speed_ref[...] + other_ref[...]) / 32.0
    balance = balance_ref[...]
    for kind, lag in enumerate(LAGS):
        decay_rate = jnp.exp(-(1.0 + 0.5 * speed_mean) / lag)
        moisture = start_ref[kind]
        for hour in range(PASSES):
            goal = balance + 0.3 * math.cos(2.0 * math.pi * hour / 24.0)
            moisture = goal + (moisture - goal) * decay_rate
        out_ref[kind] = moisture


def shifted(block, axis, by):
    count = lax.axis_size(axis)
    pairs = [(i, i + by) for i in range(count) if 0 <= i + by < count]
    return lax.ppermute(block, axis, pairs)


def swapped(block, axis, bit):
    count = lax.axis_size(axis)
    return lax.ppermute(block, axis, [(i, i ^ bit) for i in range(count)])


def shards(
    era5_columns,
    column_owner,
    live_counts,
    vertical_weights,
    stencil_index,
    stencil_weight,
    terrain_mask,
    fuel_start,
):
    gx, gy, gz = (lax.axis_index(a).astype(jnp.int32) for a in ("gx", "gy", "gz"))
    gx, gy, gz = gx.reshape(1), gy.reshape(1), gz.reshape(1)
    tiles = lax.axis_size(("gx", "gy"))
    rows_in = column_owner.shape[1]
    capacity = rows_in // tiles
    slots = tiles * capacity
    layers, rows, cols = terrain_mask.shape
    halves = cols // 128
    vmem = pl.BlockSpec(memory_space=pltpu.VMEM)
    smem = pl.BlockSpec(memory_space=pltpu.SMEM)

    def kernel(body, name, outs, operands, scratch=(), in_smem=0, anywhere=(), cost=None):
        inputs = len(operands)
        own_refs = inputs + len(outs) + len(scratch)

        def whole(*refs):
            refs, extra = list(refs[:own_refs]), refs[own_refs:]
            copies = []
            for i, at in enumerate(anywhere):
                copies.append(pltpu.make_async_copy(refs[at], extra[2 * i], extra[2 * i + 1]))
                refs[at] = extra[2 * i]
            for copy in copies:
                copy.start()
            for copy in copies:
                copy.wait()
            body(*refs)

        specs = [smem if at < in_smem else vmem for at in range(inputs)]
        more = []
        for at in anywhere:
            specs[at] = pl.BlockSpec(memory_space=pl.ANY)
            more.append(pltpu.VMEM(operands[at].shape, operands[at].dtype))
            more.append(pltpu.SemaphoreType.DMA)
        return pl.pallas_call(
            whole,
            out_shape=tuple(jax.ShapeDtypeStruct(shape, dtype) for shape, dtype in outs),
            in_specs=specs,
            out_specs=(vmem,) * len(outs),
            scratch_shapes=[pltpu.VMEM(shape, dtype) for shape, dtype in scratch] + more,
            compiler_params=params(),
            cost_estimate=cost,
            name=name,
        )(*operands)

    near_mask = terrain_mask.reshape(layers * rows, cols)
    far_mask = swapped(terrain_mask[LZ - DEEP :], "gz", 1).reshape(DEEP * rows, cols)
    (outgoing,) = kernel(
        functools.partial(route_kernel, tiles=tiles, capacity=capacity),
        "route",
        [((slots // 2, 128), F32)],
        [gz, live_counts, vertical_weights, era5_columns[0], column_owner],
        in_smem=2,
        cost=pl.CostEstimate(flops=1_000_000_000, bytes_accessed=1_000_000, transcendentals=0),
    )
    outgoing, far_mask, gx, gy, gz = lax.optimization_barrier((outgoing, far_mask, gx, gy, gz))
    received = lax.all_to_all(
        outgoing.reshape(tiles, capacity // 2, 128),
        ("gx", "gy"),
        split_axis=0,
        concat_axis=0,
        tiled=True,
    ).reshape(slots // 2, 128)
    other = swapped(received, "gz", 1)

    table, low_y, high_y = kernel(
        functools.partial(table_kernel, capacity=capacity),
        "table",
        [((slots // 256 * NF, 512), BF16), ((NS, 128), F32), ((NS, 128), F32)],
        [gz, received, other, stencil_index, stencil_weight, near_mask, far_mask],
        scratch=[((halves, layers * rows, 128), F32)],
        in_smem=1,
        anywhere=(2, 6),
    )
    right = shifted(low_y, "gy", -1)
    left = shifted(high_y, "gy", 1)
    edge, middle_0, low_x, high_x = kernel(
        functools.partial(edge_kernel, capacity=capacity),
        "edge",
        [
            ((halves, 8, NF, 128), F32),
            ((halves, 8, NF, 128), F32),
            ((STRIP + NS, cols), F32),
            ((STRIP + NS, cols), F32),
        ],
        [gz, table, stencil_index, stencil_weight, near_mask, far_mask],
        scratch=[((halves, layers * rows, 128), F32)],
        in_smem=1,
        anywhere=(5,),
        cost=pl.CostEstimate(flops=3_000_000_000, bytes_accessed=2_500_000, transcendentals=0),
    )
    corners = jnp.concatenate([right, left], axis=1)
    low_x, high_x = low_x.at[STRIP:].set(corners), high_x.at[STRIP:].set(corners)
    table, low_x, high_x = lax.optimization_barrier((table, low_x, high_x))
    above = shifted(low_x, "gx", -1)
    below = shifted(high_x, "gx", 1)
    (middle_1,) = kernel(
        functools.partial(middle_kernel, first=12, capacity=capacity),
        "middle",
        [((halves, rows - 16, NF, 128), F32)],
        [table, stencil_index, stencil_weight],
        cost=pl.CostEstimate(flops=3_000_000_000, bytes_accessed=1_600_000, transcendentals=0),
    )
    middles = (middle_0, middle_1)

    devices = tiles * lax.axis_size("gz")
    basis, moments = kernel(
        functools.partial(
            basis_kernel, last_gx=lax.axis_size("gx") - 1, last_gy=lax.axis_size("gy") - 1
        ),
        "basis",
        [((3, LZ + 1, XR, YR), F32), ((devices, 128), F32)],
        [gx, gy, gz, edge, *middles, near_mask, far_mask, right, left, above, below],
        scratch=[
            ((YR // 128, XR * NS, 128), F32),
            ((YR // 128, XR * 24, 128), F32),
            ((LZ + DEEP, XR, YR), F32),
            ((2, DEEP - 1, XR, YR), F32),
        ],
        in_smem=3,
        anywhere=(7, 8, 9, 10, 11),
    )
    moments = lax.all_to_all(
        moments, ("gx", "gy", "gz"), split_axis=0, concat_axis=0, tiled=True
    )
    potential, wind_field, speed, balance = kernel(
        wind_kernel,
        "wind",
        [
            ((layers, rows, cols), F32),
            ((3, layers, rows, cols), F32),
            ((rows, cols), F32),
            ((rows, cols), F32),
        ],
        [
            gz,
            moments,
            basis,
            *(piece.reshape(halves, -1, 128) for piece in (edge, *middles)),
            terrain_mask,
        ],
        scratch=[((LZ + 1, XR, YR), F32), ((halves, rows * NF, 128), F32)],
        in_smem=1,
    )
    (fuel_moisture,) = kernel(
        fuel_kernel,
        "fuel",
        [((len(LAGS), rows, cols), F32)],
        [speed, swapped(speed, "gz", 1), balance, fuel_start],
        anywhere=(1,),
    )
    return (potential, wind_field, fuel_moisture)


def solution(mesh):
    placed = (
        P(("gx", "gy"), None, "gz"),
        P(("gx", "gy"), None),
        P(("gx", "gy")),
        P("gz", None),
        P(None, "gx", "gy"),
        P(None, "gx", "gy"),
        P("gz", "gx", "gy"),
        P(None, "gx", "gy"),
    )
    return jax.shard_map(
        shards,
        mesh=mesh,
        in_specs=placed,
        out_specs=(P("gz", "gx", "gy"), P(None, "gz", "gx", "gy"), P(None, "gx", "gy")),
        check_vma=False,
    )
```

```python
import functools
import math

import jax
import jax.numpy as jnp
from jax import lax
from jax.experimental import pallas as pl
from jax.experimental.pallas import tpu as pltpu
from jax.sharding import PartitionSpec as P

F32 = jnp.float32
BF16 = jnp.bfloat16
PASSES = 4
LAGS = (1.0, 10.0, 100.0)

LZ = 16
DEEP = 3
NF = 40
NS = NF + LZ
STRIP = NS * 3 + 24
XR = 40
YR = 384


GY = ("zh", "zl")


def split(value):
    high = value.astype(BF16)
    return high, (value - high.astype(F32)).astype(BF16)


def dot_nt(a, b):
    return lax.dot_general(a, b, (((1,), (1,)), ((), ())), preferred_element_type=F32)


def route_kernel(
    gz_ref, live_ref, weights_ref, columns_ref, owner_ref, out_ref, *, tiles, capacity
):
    plain = weights_ref[...]
    turned = jnp.concatenate([plain[LZ - 1 - i : LZ - i] for i in range(LZ)], axis=0)
    weights = jnp.where(gz_ref[0] == 0, plain, turned)
    total = jnp.sum(plain, axis=0, keepdims=True)
    edge = jnp.concatenate([weights[LZ - 1 - i : LZ - i] for i in range(DEEP)], axis=0)

    def at_field(value, field):
        blank = jnp.zeros_like(value)
        return jnp.concatenate([value if f == field else blank for f in range(4)], axis=1)

    sums = [at_field(total, 2), at_field(total, 3)]
    stack = jnp.concatenate(
        [at_field(weights, 0), at_field(weights, 1), jnp.zeros((2 * DEEP, columns_ref.shape[1]), F32)]
        + sums
        + [at_field(edge, 0), at_field(edge, 1)]
        + sums,
        axis=0,
    )
    w_high, w_low = split(stack)
    c_high, c_low = split(columns_ref[...])
    profile = dot_nt(w_high, c_high) + dot_nt(w_high, c_low) + dot_nt(w_low, c_high)

    rows = owner_ref.shape[1]
    slots = tiles * capacity
    half = capacity // 2
    position = lax.broadcasted_iota(jnp.int32, (1, rows), 1)
    owner = jnp.where(position < live_ref[0], owner_ref[...], -1)
    matches = lax.broadcasted_iota(jnp.int32, (tiles, rows), 0) == owner
    hits = jnp.where(matches, 1.0, 0.0)
    earlier = lax.broadcasted_iota(jnp.int32, (rows, rows), 0) < lax.broadcasted_iota(
        jnp.int32, (rows, rows), 1
    )
    before = jnp.dot(
        hits.astype(BF16), jnp.where(earlier, 1.0, 0.0).astype(BF16), preferred_element_type=F32
    )
    rank = jnp.sum(hits * before, axis=0, keepdims=True).astype(jnp.int32)
    upper = jnp.where(rank >= half, 1, 0)
    target = jnp.where(owner >= 0, owner * half + rank + upper * (slots // 2 - half), -1)
    place = lax.broadcasted_iota(jnp.int32, (slots, rows), 0) == target
    high, low = split(profile)
    pad = jnp.zeros((64 - NF - 8, rows), BF16)
    both = jnp.concatenate([high, pad, low, pad], axis=0)
    placed = dot_nt(jnp.where(place, 1.0, 0.0).astype(BF16), both)
    placed = placed + pltpu.roll(placed, 64, 1)
    lane = lax.broadcasted_iota(jnp.int32, (slots // 2, 128), 1)
    out_ref[...] = jnp.where(lane < 64, placed[: slots // 2], placed[slots // 2 :])


def fill_table(received_ref, other_ref, table_ref):
    blocks = received_ref.shape[0] // 256
    turned = [jnp.transpose(received_ref[256 * p : 256 * p + 256, :]) for p in range(blocks)]
    beyond = [jnp.transpose(other_ref[256 * p : 256 * p + 256, :]) for p in range(blocks)]
    parts = 2 * blocks
    for g in range(NF // 8):
        value = jnp.concatenate(
            [
                turned[p][64 * side + 8 * g : 64 * side + 8 * g + 8]
                for side in range(2)
                for p in range(blocks)
            ],
            axis=0,
        )
        if g == NF // 8 - 1:
            value = value + jnp.concatenate(
                [
                    beyond[p][64 * side + NF : 64 * side + NF + 8]
                    for side in range(2)
                    for p in range(blocks)
                ],
                axis=0,
            )
        rows = slice(8 * parts * g, 8 * parts * (g + 1))
        table_ref[rows, 0:256], table_ref[rows, 256:512] = split(value)


def place_of(slot, capacity):
    half = capacity // 2
    bits = half.bit_length() - 1
    row = ((slot >> (bits + 1)) << bits) | (slot & (half - 1))
    return row, (slot >> bits) & 1


def pick_columns(table_ref, index, weight, capacity):
    parts = table_ref.shape[0] // NF
    total = weight[0] + weight[1] + weight[2] + weight[3]
    slot = lax.broadcasted_iota(jnp.int32, (256, 256), 0).astype(F32).astype(BF16)
    acc = [None] * (NF // 8)
    for point in range(len(index)):
        row, side = place_of(index[point], capacity)
        low = jnp.broadcast_to((row & 255).astype(F32), (16, 256)).astype(BF16)
        low = jnp.concatenate([low] * 16, axis=0)
        chosen = jnp.where(slot == low, jnp.ones((256, 256), BF16), jnp.zeros((256, 256), BF16))
        chosen = jnp.concatenate([chosen, chosen], axis=0)
        found = jnp.dot(table_ref[...], chosen, preferred_element_type=F32)
        part = jnp.broadcast_to((row >> 8) + side * (parts // 2), (8, 256))
        share = jnp.broadcast_to(weight[point] / total, (8, 256))
        for g in range(NF // 8):
            values = [
                found[8 * (parts * g + p) : 8 * (parts * g + p) + 8] for p in range(parts)
            ]
            bit = 1
            while len(values) > 1:
                odd = (part & bit) != 0
                values = [
                    jnp.where(odd, values[i + 1], values[i]) for i in range(0, len(values), 2)
                ]
                bit *= 2
            term = values[0] * share
            acc[g] = term if acc[g] is None else acc[g] + term
    return acc


def pick_rows(table_ref, index_ref, weight_ref, chosen, out_ref, capacity):
    points, _, cols = index_ref.shape
    for at, x in enumerate(chosen):
        got = pick_columns(
            table_ref,
            [index_ref[k, x : x + 1, :] for k in range(points)],
            [weight_ref[k, x : x + 1, :] for k in range(points)],
            capacity,
        )
        for g in range(NF // 8):
            for h in range(cols // 128):
                out_ref[h, at, 8 * g : 8 * g + 8, :] = got[g][:, 128 * h : 128 * h + 128]


def fill_mask(lower, mask_ref, far_mask_ref, mask_f_ref):
    first = mask_ref.shape[0] // 2 - far_mask_ref.shape[0]
    last = first + far_mask_ref.shape[0]
    for h in range(mask_f_ref.shape[0]):
        at = slice(128 * h, 128 * h + 128)
        mask_f_ref[h, 0:first] = mask_ref[0:first, at].astype(F32)
        mask_f_ref[h, first:last] = jnp.where(
            lower, mask_ref[first:last, at], far_mask_ref[:, at]
        ).astype(F32)
        mask_f_ref[h, last:] = mask_ref[last:, at].astype(F32)


def table_kernel(
    gz_ref, received_ref, other_ref, index_ref, weight_ref, mask_ref, far_mask_ref,
    table_ref, low_y_ref, high_y_ref, mask_f_ref, *, capacity
):
    points, rows, cols = index_ref.shape
    fill_table(received_ref, other_ref, table_ref)
    fill_mask(gz_ref[0] == 0, mask_ref, far_mask_ref, mask_f_ref)
    lane = lax.broadcasted_iota(jnp.int32, (8, 128), 1)
    row = lax.broadcasted_iota(jnp.int32, (8, 128), 0)

    def packed(value_ref, k):
        sides = []
        for start, turn in ((0, 0), (cols - 128, 4)):
            total = None
            for group in range(rows // 8):
                value = value_ref[k, 8 * group : 8 * group + 8, start : start + 128]
                value = pltpu.roll(value, 32 * group + turn, 1, stride=4, stride_axis=0)
                value = jnp.where((lane >> 2) == row + 8 * group, value, jnp.zeros_like(value))
                total = value if total is None else total + value
            sides.append(jnp.sum(total, axis=0, keepdims=True))
        return jnp.concatenate(sides, axis=1)

    got = pick_columns(
        table_ref,
        [packed(index_ref, k) for k in range(points)],
        [packed(weight_ref, k) for k in range(points)],
        capacity,
    )
    for side, out in ((0, low_y_ref), (1, high_y_ref)):
        for g in range(NF // 8):
            out[8 * g : 8 * g + 8] = got[g][:, 128 * side : 128 * side + 128]
        start, turn = ((0, 0), (cols - 128, 4))[side]
        for g in range(LZ // 8):
            total = None
            for x in range(rows):
                value = mask_f_ref[start // 128, pl.ds(x + g * 8 * rows, 8, stride=rows), :]
                value = pltpu.roll(value, (4 * x + turn) % 128, 1)
                total = value if total is None else jnp.where((lane >> 2) == x, value, total)
            out[NF + 8 * g : NF + 8 * g + 8] = total


def edge_kernel(
    gz_ref, table_ref, index_ref, weight_ref, mask_ref, far_mask_ref,
    edge_ref, middle_ref, low_x_ref, high_x_ref, mask_f_ref, *, capacity
):
    _, rows, cols = index_ref.shape
    chosen = [0, 1, 2, 3] + [rows - 4 + j for j in range(4)]
    pick_rows(table_ref, index_ref, weight_ref, chosen, edge_ref, capacity)
    fill_mask(gz_ref[0] == 0, mask_ref, far_mask_ref, mask_f_ref)
    for d in range(4):
        for out, x, kept in ((low_x_ref, d, d), (high_x_ref, rows - 1 - d, 7 - d)):
            for h in range(cols // 128):
                at = slice(128 * h, 128 * h + 128)
                if d < 3:
                    out[NS * d : NS * d + NF, at] = edge_ref[h, kept]
                    for g in range(LZ // 8):
                        first = NS * d + NF + 8 * g
                        out[first : first + 8, at] = mask_f_ref[
                            h, pl.ds(x + g * 8 * rows, 8, stride=rows), :
                        ]
                else:
                    out[NS * 3 : NS * 3 + 16, at] = edge_ref[h, kept, 0:16]
                    out[NS * 3 + 16 : NS * 3 + 24, at] = edge_ref[h, kept, 32:40]
    pick_rows(table_ref, index_ref, weight_ref, list(range(4, 12)), middle_ref, capacity)


def middle_kernel(table_ref, index_ref, weight_ref, middle_ref, *, first, capacity):
    chosen = list(range(first, first + middle_ref.shape[1]))
    pick_rows(table_ref, index_ref, weight_ref, chosen, middle_ref, capacity)


def holder(x, rows, edge_ref, middle_refs):
    if x < 4:
        return edge_ref, x
    if x >= rows - 4:
        return edge_ref, x - rows + 8
    return (middle_refs[0], x - 4) if x < 12 else (middle_refs[1], x - 12)


def ring_smooth(plane):
    plane = plane + 0.5 * (pltpu.roll(plane, 1, 0) + pltpu.roll(plane, XR - 1, 0))
    return plane + 0.5 * (pltpu.roll(plane, 1, 1) + pltpu.roll(plane, YR - 1, 1))


def basis_kernel(
    gx_ref, gy_ref, gz_ref, edge_ref, middle_0_ref, middle_1_ref, mask_ref, far_mask_ref,
    right_ref, left_ref, above_ref, below_ref,
    basis_ref, moments_ref,
    ext_ref, source_ref, air_ref, last_ref, *, last_gx, last_gy
):
    gx, gy = gx_ref[0], gy_ref[0]
    lower = gz_ref[0] == 0
    halves, rows = edge_ref.shape[0], mask_ref.shape[0] // LZ
    cols = 128 * halves
    lane = lax.broadcasted_iota(jnp.int32, (8, 128), 1)

    for x in range(rows):
        held_ref, j = holder(x, rows, edge_ref, (middle_0_ref, middle_1_ref))
        for h in range(halves):
            ext_ref[h, NS * x : NS * x + NF] = held_ref[h, j]
        for g in range(NS // 8):
            at = slice(8 * g, 8 * g + 8)
            right = pltpu.roll(right_ref[at], (128 - 4 * x) % 128, 1)
            left = pltpu.roll(left_ref[at], (124 - 4 * x) % 128, 1)
            side = jnp.where(lane < 4, right, jnp.where(lane >= 124, left, 0.0))
            ext_ref[halves, NS * x + 8 * g : NS * x + 8 * g + 8] = side

    for d in range(4):
        for near_ref, ring, origin in (
            (above_ref, rows + d, d),
            (below_ref, XR - 1 - d, rows - 1 - d),
        ):
            base = ring * NS
            for h in range(halves):
                at = slice(128 * h, 128 * h + 128)
                if d < 3:
                    ext_ref[h, base : base + NS] = near_ref[NS * d : NS * d + NS, at]
                else:
                    ext_ref[h, base : base + 16] = near_ref[NS * 3 : NS * 3 + 16, at]
                    ext_ref[h, base + 16 : base + 32] = jnp.zeros((16, 128), F32)
                    ext_ref[h, base + 32 : base + 40] = near_ref[NS * 3 + 16 : NS * 3 + 24, at]
                    ext_ref[h, base + 40 : base + NS] = jnp.zeros((LZ, 128), F32)
            for g in range(NS // 8):
                at = slice(STRIP + 8 * g, STRIP + 8 * g + 8)
                right = pltpu.roll(near_ref[at, 0:128], (128 - 4 * origin) % 128, 1)
                left = pltpu.roll(near_ref[at, 128:256], (124 - 4 * origin) % 128, 1)
                side = jnp.where(lane < 4, right, jnp.where(lane >= 124, left, 0.0))
                ext_ref[halves, base + 8 * g : base + 8 * g + 8] = side

    def source_row(x):
        here, after, prior = x * NS, (x + 1) % XR * NS, (x - 1) % XR * NS

        def row_of(start, f):
            return jnp.concatenate(
                [ext_ref[h, start + f : start + f + 8, :] for h in range(halves + 1)], axis=1
            )

        def east(f):
            return row_of(after, f) - row_of(prior, f)

        def north(f):
            value = row_of(here, f)
            return pltpu.roll(value, YR - 1, 1) - pltpu.roll(value, 1, 1)

        out = x * 24
        values = (
            0.5 * east(0) + 0.5 * north(16),
            0.5 * east(8) + 0.5 * north(24),
            0.5 * east(32) + 0.5 * pltpu.roll(north(32), 5, 0),
        )
        for g, value in enumerate(values):
            for h in range(halves + 1):
                source_ref[h, out + 8 * g : out + 8 * g + 8, :] = value[
                    :, 128 * h : 128 * h + 128
                ]

    for x in range(XR):
        source_row(x)

    row_id = lax.broadcasted_iota(jnp.int32, (XR, YR), 0)
    col_id = lax.broadcasted_iota(jnp.int32, (XR, YR), 1)
    row_in = (row_id < 32) | ((row_id < 36) & (gx < last_gx)) | ((row_id >= 36) & (gx > 0))
    col_in = (
        (col_id < 256) | ((col_id < 260) & (gy < last_gy)) | ((col_id >= 380) & (gy > 0))
    )
    inside = jnp.where(row_in & col_in, 1.0, 0.0)
    for layer in range(LZ + DEEP):
        picked = layer if layer < LZ else 23 - layer
        for group in range(XR // 8):
            for h in range(YR // 128):
                at = slice(128 * h, 128 * h + 128)
                x = slice(8 * group, 8 * group + 8)
                if group < 4 and h < 2:
                    if layer < LZ:
                        known = mask_ref[rows * picked + 8 * group : rows * picked + 8 * group + 8, at]
                    else:
                        first = rows * (picked - 5) + 8 * group
                        known = far_mask_ref[first : first + 8, at]
                    known = known.astype(F32)
                else:
                    known = ext_ref[h, pl.ds(8 * group * NS + NF + picked, 8, stride=NS), :]
                full = inside[x, at]
                air = jnp.where(lower, known, full) if layer < LZ else jnp.where(lower, full, known)
                air_ref[layer, x, at] = air
                source = air * source_ref[h, pl.ds(8 * group * 24 + layer, 8, stride=24), :]
                value = source / (14.0 * air + (1.0 - air))
                if layer < LZ + 1:
                    basis_ref[0, layer, x, at] = value
                else:
                    last_ref[0, layer - LZ - 1, x, at] = value

    def read(k, layer):
        if layer < LZ + 1:
            return basis_ref[k, layer]
        return last_ref[k, layer - LZ - 1]

    def advance(k, layer):
        here = read(k, layer)
        beside = read(k, layer + 1)
        if layer > 0:
            beside = beside + read(k, layer - 1)
        return air_ref[layer] * (ring_smooth(here + 0.5 * beside) - here) * (1.0 / 7.0)

    sums = [None] * 6

    def add(at, value):
        value = value[:, 0:128] + value[:, 128:256]
        sums[at] = value if sums[at] is None else sums[at] + value

    for layer in range(LZ + 2):
        value = advance(0, layer)
        if layer < LZ + 1:
            basis_ref[1, layer] = value
        else:
            last_ref[1, layer - LZ - 1] = value
    for layer in range(LZ + 1):
        basis_ref[2, layer] = advance(1, layer)
    for layer in range(LZ):
        third = advance(2, layer)[0:rows, 0:cols]
        first, second, zero = (basis_ref[k, layer, 0:rows, 0:cols] for k in (1, 2, 0))
        air = air_ref[layer, 0:rows, 0:cols]
        scaling = 14.0 * air + (1.0 - air)
        zero_s, first_s, second_s = zero * scaling, first * scaling, second * scaling
        add(0, zero_s * zero)
        add(1, zero_s * first)
        add(2, first_s * first)
        add(3, first_s * second)
        add(4, second_s * second)
        add(5, second_s * third)
    lane_id = lax.broadcasted_iota(jnp.int32, (1, 128), 1)
    packed = jnp.zeros((1, 128), F32)
    for k, value in enumerate(sums):
        value = jnp.sum(jnp.sum(value, axis=0, keepdims=True), axis=1, keepdims=True)
        packed = jnp.where(lane_id == k, value, packed)
    moments_ref[...] = jnp.broadcast_to(packed, moments_ref.shape)


def iterate(nu):
    def inner(a, b):
        total = None
        for i, left in enumerate(a):
            for j, right in enumerate(b):
                term = left * right * nu[i + j]
                total = term if total is None else total + term
        return total

    one = jnp.ones_like(nu[0])
    precond = [one]
    direction = [one]
    potential = []
    current = nu[0]
    for step in range(3):
        applied = (
            [direction[0]]
            + [direction[i] - direction[i - 1] for i in range(1, len(direction))]
            + [-direction[-1]]
        )
        alpha = current / inner(direction, applied)
        potential = [
            (potential[i] + alpha * d) if i < len(potential) else alpha * d
            for i, d in enumerate(direction)
        ]
        if step < 2:
            precond = [
                (precond[i] - alpha * a) if i < len(precond) else -(alpha * a)
                for i, a in enumerate(applied)
            ]
            updated = inner(precond, precond)
            ratio = updated / current
            direction = [
                (p + ratio * direction[i]) if i < len(direction) else p
                for i, p in enumerate(precond)
            ]
            current = updated
    return potential


def wind_kernel(
    gz_ref, moments_ref, other_moments_ref, basis_ref, edge_ref, middle_0_ref, middle_1_ref, mask_ref,
    potential_ref, wind_ref, speed_ref, balance_ref, p_ref, grid_ref
):
    gz = gz_ref[0]
    rows, cols = speed_ref.shape
    near = 4 * NF
    for h in range(cols // 128):
        grid_ref[h, 0:near] = edge_ref[h, 0:near]
        grid_ref[h, near : near + 8 * NF] = middle_0_ref[h]
        grid_ref[h, near + 8 * NF : (rows - 4) * NF] = middle_1_ref[h]
        grid_ref[h, (rows - 4) * NF :] = edge_ref[h, near:]
    totals = moments_ref[...] + other_moments_ref[...]
    factors = iterate([totals[:, k : k + 1] for k in range(6)])
    factors = [jnp.broadcast_to(c, (8, 128)) for c in factors]
    factors = [jnp.tile(c, (XR // 8, YR // 128)) for c in factors]

    def combine(layer):
        return (
            factors[0] * basis_ref[0, layer]
            + factors[1] * basis_ref[1, layer]
            + factors[2] * basis_ref[2, layer]
        )

    for layer in range(LZ + 1):
        p_ref[layer] = combine(layer)
    upward = jnp.where(gz == 0, 0.5, -0.5)

    def wind_of(layer, below):
        here = p_ref[layer]
        slope_up = p_ref[layer + 1][0:rows, 0:cols]
        if below:
            slope_up = slope_up - p_ref[layer - 1][0:rows, 0:cols]
        slope_up = upward * slope_up
        slope_east = 0.5 * (pltpu.roll(here, XR - 1, 0) - pltpu.roll(here, 1, 0))[0:rows, 0:cols]
        slope_north = 0.5 * (pltpu.roll(here, YR - 1, 1) - pltpu.roll(here, 1, 1))[0:rows, 0:cols]
        out = jnp.where(gz == 0, layer, LZ - 1 - layer)
        potential_ref[out] = here[0:rows, 0:cols]
        for group in range(rows // 8):
            x = slice(8 * group, 8 * group + 8)
            for h in range(cols // 128):
                at = slice(128 * h, 128 * h + 128)
                east = grid_ref[h, pl.ds(8 * group * NF + layer, 8, stride=NF), :]
                north = grid_ref[h, pl.ds(8 * group * NF + LZ + layer, 8, stride=NF), :]
                air = mask_ref[out, x, at].astype(F32)
                a = air * (east + slope_east[x, at])
                b = air * (north + slope_north[x, at])
                c = air * slope_up[x, at]
                wind_ref[0, out, x, at] = a
                wind_ref[1, out, x, at] = b
                wind_ref[2, out, x, at] = c
                speed = jnp.sqrt(a * a + b * b + c * c)
                if below:
                    speed = speed_ref[x, at] + speed
                speed_ref[x, at] = speed

    for layer in range(LZ):
        wind_of(layer, layer > 0)
    for group in range(rows // 8):
        x = slice(8 * group, 8 * group + 8)
        for h in range(cols // 128):
            at = slice(128 * h, 128 * h + 128)
            temp = grid_ref[h, pl.ds(8 * group * NF + NF - 2, 8, stride=NF), :] / 32.0
            humid = grid_ref[h, pl.ds(8 * group * NF + NF - 1, 8, stride=NF), :] / 32.0
            balance_ref[x, at] = 1.2 + 0.5 * jnp.tanh(humid) - 0.3 * jnp.tanh(temp)


def fuel_kernel(speed_ref, other_ref, balance_ref, start_ref, out_ref):
    speed_mean = (speed_ref[...] + other_ref[...]) / 32.0
    balance = balance_ref[...]
    for kind, lag in enumerate(LAGS):
        decay_rate = jnp.exp(-(1.0 + 0.5 * speed_mean) / lag)
        moisture = start_ref[kind]
        for hour in range(PASSES):
            goal = balance + 0.3 * math.cos(2.0 * math.pi * hour / 24.0)
            moisture = goal + (moisture - goal) * decay_rate
        out_ref[kind] = moisture


def shifted(block, axis, by):
    count = lax.axis_size(axis)
    pairs = [(i, i + by) for i in range(count) if 0 <= i + by < count]
    return lax.ppermute(block, axis, pairs)


def swapped(block, axis, bit):
    count = lax.axis_size(axis)
    return lax.ppermute(block, axis, [(i, i ^ bit) for i in range(count)])


def shards(
    era5_columns,
    column_owner,
    live_counts,
    vertical_weights,
    stencil_index,
    stencil_weight,
    terrain_mask,
    fuel_start,
):
    gx, gy, gz = (lax.axis_index(a).astype(jnp.int32) for a in ("gx", GY, "gz"))
    gx, gy, gz = gx.reshape(1), gy.reshape(1), gz.reshape(1)
    tiles = lax.axis_size(("gx", *GY))
    rows_in = column_owner.shape[1]
    capacity = rows_in // tiles
    slots = tiles * capacity
    layers, rows, cols = terrain_mask.shape
    halves = cols // 128
    vmem = pl.BlockSpec(memory_space=pltpu.VMEM)
    smem = pl.BlockSpec(memory_space=pltpu.SMEM)

    def kernel(
        body, name, outs, operands, scratch=(), in_smem=0, anywhere=(), tail=None, vmem_mib=28, cost=None
    ):
        inputs = len(operands)
        own_refs = inputs + len(outs) + len(scratch)

        def whole(*refs):
            refs, extra = list(refs[:own_refs]), refs[own_refs:]
            copies = []
            for i, at in enumerate(anywhere):
                from_ref = refs[at]
                if at == tail:
                    from_ref = from_ref.at[pl.ds(from_ref.shape[0] - far_rows, far_rows)]
                copies.append(pltpu.make_async_copy(from_ref, extra[2 * i], extra[2 * i + 1]))
                refs[at] = extra[2 * i]
            for copy in copies:
                copy.start()
            for copy in copies:
                copy.wait()
            body(*refs)

        specs = [smem if at < in_smem else vmem for at in range(inputs)]
        more = []
        for at in anywhere:
            specs[at] = pl.BlockSpec(memory_space=pl.ANY)
            shape = (far_rows, cols) if at == tail else operands[at].shape
            more.append(pltpu.VMEM(shape, operands[at].dtype))
            more.append(pltpu.SemaphoreType.DMA)
        return pl.pallas_call(
            whole,
            out_shape=tuple(jax.ShapeDtypeStruct(shape, dtype) for shape, dtype in outs),
            in_specs=specs,
            out_specs=(vmem,) * len(outs),
            scratch_shapes=[pltpu.VMEM(shape, dtype) for shape, dtype in scratch] + more,
            compiler_params=pltpu.CompilerParams(vmem_limit_bytes=vmem_mib * 1024 * 1024),
            cost_estimate=cost,
            name=name,
        )(*operands)

    near_mask = terrain_mask.reshape(layers * rows, cols)
    far_mask = swapped(terrain_mask, "gz", 1).reshape(layers * rows, cols)
    far_rows = DEEP * rows
    (outgoing,) = kernel(
        functools.partial(route_kernel, tiles=tiles, capacity=capacity),
        "route",
        [((slots // 2, 128), F32)],
        [gz, live_counts, vertical_weights, era5_columns[0], column_owner],
        in_smem=2,
        vmem_mib=60,
        cost=pl.CostEstimate(flops=1_000_000_000, bytes_accessed=1_000_000, transcendentals=0),
    )
    outgoing, far_mask, gx, gy, gz = lax.optimization_barrier((outgoing, far_mask, gx, gy, gz))
    received = lax.all_to_all(
        outgoing.reshape(tiles, capacity // 2, 128),
        ("gx", *GY),
        split_axis=0,
        concat_axis=0,
        tiled=True,
    ).reshape(slots // 2, 128)
    other = swapped(received, "gz", 1)

    table, low_y, high_y = kernel(
        functools.partial(table_kernel, capacity=capacity),
        "table",
        [((slots // 256 * NF, 512), BF16), ((NS, 128), F32), ((NS, 128), F32)],
        [gz, received, other, stencil_index, stencil_weight, near_mask, far_mask],
        scratch=[((halves, layers * rows, 128), F32)],
        in_smem=1,
        anywhere=(2, 6),
        tail=6,
    )
    right = shifted(low_y, GY, -1)
    left = shifted(high_y, GY, 1)
    edge, middle_0, low_x, high_x = kernel(
        functools.partial(edge_kernel, capacity=capacity),
        "edge",
        [
            ((halves, 8, NF, 128), F32),
            ((halves, 8, NF, 128), F32),
            ((STRIP + NS, cols), F32),
            ((STRIP + NS, cols), F32),
        ],
        [gz, table, stencil_index, stencil_weight, near_mask, far_mask],
        scratch=[((halves, layers * rows, 128), F32)],
        in_smem=1,
        anywhere=(5,),
        tail=5,
        cost=pl.CostEstimate(flops=3_000_000_000, bytes_accessed=2_500_000, transcendentals=0),
    )
    corners = jnp.concatenate([right, left], axis=1)
    low_x, high_x = low_x.at[STRIP:].set(corners), high_x.at[STRIP:].set(corners)
    table, low_x, high_x = lax.optimization_barrier((table, low_x, high_x))
    above = shifted(low_x, "gx", -1)
    below = shifted(high_x, "gx", 1)
    (middle_1,) = kernel(
        functools.partial(middle_kernel, first=12, capacity=capacity),
        "middle",
        [((halves, rows - 16, NF, 128), F32)],
        [table, stencil_index, stencil_weight],
        cost=pl.CostEstimate(flops=3_000_000_000, bytes_accessed=1_600_000, transcendentals=0),
    )
    middles = (middle_0, middle_1)

    near_group = lax.axis_size(("gx", "zl"))
    basis, moments = kernel(
        functools.partial(
            basis_kernel, last_gx=lax.axis_size("gx") - 1, last_gy=lax.axis_size(GY) - 1
        ),
        "basis",
        [((3, LZ + 1, XR, YR), F32), ((near_group, 128), F32)],
        [gx, gy, gz, edge, *middles, near_mask, far_mask, right, left, above, below],
        scratch=[
            ((YR // 128, XR * NS, 128), F32),
            ((YR // 128, XR * 24, 128), F32),
            ((LZ + DEEP, XR, YR), F32),
            ((2, DEEP - 1, XR, YR), F32),
        ],
        in_smem=3,
        anywhere=(7, 8, 9, 10, 11),
        tail=7,
    )
    moments = lax.all_to_all(
        moments, ("gx", "zl"), split_axis=0, concat_axis=0, tiled=True
    )
    moments = jnp.sum(moments, axis=0, keepdims=True)
    bit = 1
    while bit < lax.axis_size("zh"):
        moments = moments + swapped(moments, "zh", bit)
        bit *= 2
    other_moments = swapped(moments, "gz", 1)
    potential, wind_field, speed, balance = kernel(
        wind_kernel,
        "wind",
        [
            ((layers, rows, cols), F32),
            ((3, layers, rows, cols), F32),
            ((rows, cols), F32),
            ((rows, cols), F32),
        ],
        [
            gz,
            moments,
            other_moments,
            basis,
            *(piece.reshape(halves, -1, 128) for piece in (edge, *middles)),
            terrain_mask,
        ],
        scratch=[((LZ + 1, XR, YR), F32), ((halves, rows * NF, 128), F32)],
        in_smem=1,
    )
    (fuel_moisture,) = kernel(
        fuel_kernel,
        "fuel",
        [((len(LAGS), rows, cols), F32)],
        [speed, swapped(speed, "gz", 1), balance, fuel_start],
        anywhere=(1,),
    )
    return (potential, wind_field, fuel_moisture)


def solution(mesh):
    count_gx, count_gy, count_gz = mesh.devices.shape
    near = math.gcd(count_gy, 4)
    finer = jax.sharding.Mesh(
        mesh.devices.reshape(count_gx, count_gy // near, near, count_gz), ("gx", *GY, "gz")
    )
    placed = (
        P(("gx", *GY), None, "gz"),
        P(("gx", *GY), None),
        P(("gx", *GY)),
        P("gz", None),
        P(None, "gx", GY),
        P(None, "gx", GY),
        P("gz", "gx", GY),
        P(None, "gx", GY),
    )
    return jax.shard_map(
        shards,
        mesh=finer,
        in_specs=placed,
        out_specs=(P("gz", "gx", GY), P(None, "gz", "gx", GY), P(None, "gx", GY)),
        check_vma=False,
    )
```

```python
import functools
import math

import jax
import jax.numpy as jnp
from jax import lax
from jax.experimental import pallas as pl
from jax.experimental.pallas import tpu as pltpu
from jax.sharding import PartitionSpec as P

F32 = jnp.float32
BF16 = jnp.bfloat16
PASSES = 4
LAGS = (1.0, 10.0, 100.0)

LZ = 16
DEEP = 3
NF = 40
NS = NF + LZ
STRIP = NS * 3 + 24
XR = 40
YR = 384


SPLIT = 8
PROFILE = 60
GY = ("gy",)


def split(value):
    high = value.astype(BF16)
    return high, (value - high.astype(F32)).astype(BF16)


def dot_nt(a, b):
    return lax.dot_general(a, b, (((1,), (1,)), ((), ())), preferred_element_type=F32)


def profile_kernel(gz_ref, weights_ref, columns_ref, own_ref, leaving_ref):
    plain = weights_ref[...]
    turned = jnp.concatenate([plain[LZ - 1 - i : LZ - i] for i in range(LZ)], axis=0)
    weights = jnp.where(gz_ref[0] == 0, plain, turned)
    total = jnp.sum(plain, axis=0, keepdims=True)
    edge = jnp.concatenate([weights[LZ - 1 - i : LZ - i] for i in range(DEEP)], axis=0)

    def at_field(value, field):
        blank = jnp.zeros_like(value)
        return jnp.concatenate([value if f == field else blank for f in range(4)], axis=1)

    sums = [at_field(total, 2), at_field(total, 3)]
    stack = jnp.concatenate(
        [at_field(weights, 0), at_field(weights, 1), jnp.zeros((2 * DEEP, columns_ref.shape[1]), F32)]
        + sums
        + [at_field(edge, 0), at_field(edge, 1)]
        + sums,
        axis=0,
    )
    w_high, w_low = split(stack)
    c_high, c_low = split(columns_ref[...])
    profile = dot_nt(w_high, c_high) + dot_nt(w_high, c_low) + dot_nt(w_low, c_high)
    own_ref[...] = profile[:NF]
    leaving_ref[...] = profile[NF:]


def rank_kernel(live_ref, owner_ref, target_ref, *, tiles, capacity):
    rows = owner_ref.shape[1]
    slots = tiles * capacity
    half = capacity // 2
    position = lax.broadcasted_iota(jnp.int32, (1, rows), 1)
    owner = jnp.where(position < live_ref[0], owner_ref[...], -1)
    matches = lax.broadcasted_iota(jnp.int32, (tiles, rows), 0) == owner
    hits = jnp.where(matches, 1.0, 0.0)
    earlier = lax.broadcasted_iota(jnp.int32, (rows, rows), 0) < lax.broadcasted_iota(
        jnp.int32, (rows, rows), 1
    )
    before = jnp.dot(
        hits.astype(BF16), jnp.where(earlier, 1.0, 0.0).astype(BF16), preferred_element_type=F32
    )
    rank = jnp.sum(hits * before, axis=0, keepdims=True).astype(jnp.int32)
    upper = jnp.where(rank >= half, 1, 0)
    target_ref[...] = jnp.where(
        owner >= 0, owner * half + rank + upper * (slots // 2 - half), -1
    )


def place_kernel(target_ref, own_ref, other_ref, out_ref):
    slots = 2 * out_ref.shape[0]
    rows = target_ref.shape[1]
    profile = jnp.concatenate([own_ref[: NF - 8], own_ref[NF - 8 :] + other_ref[...]], axis=0)
    target = target_ref[...]
    place = lax.broadcasted_iota(jnp.int32, (slots, rows), 0) == target
    high, low = split(profile)
    pad = jnp.zeros((64 - NF, rows), BF16)
    both = jnp.concatenate([high, pad, low, pad], axis=0)
    placed = dot_nt(jnp.where(place, 1.0, 0.0).astype(BF16), both)
    placed = placed + pltpu.roll(placed, 64, 1)
    lane = lax.broadcasted_iota(jnp.int32, (slots // 2, 128), 1)
    out_ref[...] = jnp.where(lane < 64, placed[: slots // 2], placed[slots // 2 :])


def fill_table(received_ref, table_ref):
    blocks = received_ref.shape[0] // 256
    turned = [jnp.transpose(received_ref[256 * p : 256 * p + 256, :]) for p in range(blocks)]
    parts = 2 * blocks
    for g in range(NF // 8):
        value = jnp.concatenate(
            [
                turned[p][64 * side + 8 * g : 64 * side + 8 * g + 8]
                for side in range(2)
                for p in range(blocks)
            ],
            axis=0,
        )
        rows = slice(8 * parts * g, 8 * parts * (g + 1))
        table_ref[rows, 0:256], table_ref[rows, 256:512] = split(value)


def place_of(slot, capacity):
    half = capacity // 2
    bits = half.bit_length() - 1
    row = ((slot >> (bits + 1)) << bits) | (slot & (half - 1))
    return row, (slot >> bits) & 1


def pick_columns(table_ref, index, weight, capacity):
    parts = table_ref.shape[0] // NF
    total = weight[0] + weight[1] + weight[2] + weight[3]
    slot = lax.broadcasted_iota(jnp.int32, (256, 256), 0).astype(F32).astype(BF16)
    acc = [None] * (NF // 8)
    for point in range(len(index)):
        row, side = place_of(index[point], capacity)
        low = jnp.broadcast_to((row & 255).astype(F32), (16, 256)).astype(BF16)
        low = jnp.concatenate([low] * 16, axis=0)
        chosen = jnp.where(slot == low, jnp.ones((256, 256), BF16), jnp.zeros((256, 256), BF16))
        chosen = jnp.concatenate([chosen, chosen], axis=0)
        found = jnp.dot(table_ref[...], chosen, preferred_element_type=F32)
        part = jnp.broadcast_to((row >> 8) + side * (parts // 2), (8, 256))
        share = jnp.broadcast_to(weight[point] / total, (8, 256))
        for g in range(NF // 8):
            values = [
                found[8 * (parts * g + p) : 8 * (parts * g + p) + 8] for p in range(parts)
            ]
            bit = 1
            while len(values) > 1:
                odd = (part & bit) != 0
                values = [
                    jnp.where(odd, values[i + 1], values[i]) for i in range(0, len(values), 2)
                ]
                bit *= 2
            term = values[0] * share
            acc[g] = term if acc[g] is None else acc[g] + term
    return acc


def pick_rows(table_ref, index_ref, weight_ref, chosen, out_ref, capacity):
    points, _, cols = index_ref.shape
    for at, x in enumerate(chosen):
        got = pick_columns(
            table_ref,
            [index_ref[k, x : x + 1, :] for k in range(points)],
            [weight_ref[k, x : x + 1, :] for k in range(points)],
            capacity,
        )
        for g in range(NF // 8):
            for h in range(cols // 128):
                out_ref[h, at, 8 * g : 8 * g + 8, :] = got[g][:, 128 * h : 128 * h + 128]


def fill_mask(lower, mask_ref, far_mask_ref, mask_f_ref):
    first = mask_ref.shape[0] // 2 - far_mask_ref.shape[0]
    last = first + far_mask_ref.shape[0]
    for h in range(mask_f_ref.shape[0]):
        at = slice(128 * h, 128 * h + 128)
        mask_f_ref[h, 0:first] = mask_ref[0:first, at].astype(F32)
        mask_f_ref[h, first:last] = jnp.where(
            lower, mask_ref[first:last, at], far_mask_ref[:, at]
        ).astype(F32)
        mask_f_ref[h, last:] = mask_ref[last:, at].astype(F32)


def table_kernel(
    gz_ref, received_ref, index_ref, weight_ref, mask_ref, far_mask_ref,
    table_ref, low_y_ref, high_y_ref, mask_f_ref, *, capacity
):
    points, rows, cols = index_ref.shape
    fill_table(received_ref, table_ref)
    fill_mask(gz_ref[0] == 0, mask_ref, far_mask_ref, mask_f_ref)
    lane = lax.broadcasted_iota(jnp.int32, (8, 128), 1)
    row = lax.broadcasted_iota(jnp.int32, (8, 128), 0)

    def packed(value_ref, k):
        sides = []
        for start, turn in ((0, 0), (cols - 128, 4)):
            total = None
            for group in range(rows // 8):
                value = value_ref[k, 8 * group : 8 * group + 8, start : start + 128]
                value = pltpu.roll(value, 32 * group + turn, 1, stride=4, stride_axis=0)
                value = jnp.where((lane >> 2) == row + 8 * group, value, jnp.zeros_like(value))
                total = value if total is None else total + value
            sides.append(jnp.sum(total, axis=0, keepdims=True))
        return jnp.concatenate(sides, axis=1)

    got = pick_columns(
        table_ref,
        [packed(index_ref, k) for k in range(points)],
        [packed(weight_ref, k) for k in range(points)],
        capacity,
    )
    for side, out in ((0, low_y_ref), (1, high_y_ref)):
        for g in range(NF // 8):
            out[8 * g : 8 * g + 8] = got[g][:, 128 * side : 128 * side + 128]
        start, turn = ((0, 0), (cols - 128, 4))[side]
        for g in range(LZ // 8):
            total = None
            for x in range(rows):
                value = mask_f_ref[start // 128, pl.ds(x + g * 8 * rows, 8, stride=rows), :]
                value = pltpu.roll(value, (4 * x + turn) % 128, 1)
                total = value if total is None else jnp.where((lane >> 2) == x, value, total)
            out[NF + 8 * g : NF + 8 * g + 8] = total


def edge_kernel(
    gz_ref, table_ref, index_ref, weight_ref, mask_ref, far_mask_ref,
    edge_ref, middle_ref, low_x_ref, high_x_ref, mask_f_ref, *, capacity
):
    _, rows, cols = index_ref.shape
    chosen = [0, 1, 2, 3] + [rows - 4 + j for j in range(4)]
    pick_rows(table_ref, index_ref, weight_ref, chosen, edge_ref, capacity)
    fill_mask(gz_ref[0] == 0, mask_ref, far_mask_ref, mask_f_ref)
    for d in range(4):
        for out, x, kept in ((low_x_ref, d, d), (high_x_ref, rows - 1 - d, 7 - d)):
            for h in range(cols // 128):
                at = slice(128 * h, 128 * h + 128)
                if d < 3:
                    out[NS * d : NS * d + NF, at] = edge_ref[h, kept]
                    for g in range(LZ // 8):
                        first = NS * d + NF + 8 * g
                        out[first : first + 8, at] = mask_f_ref[
                            h, pl.ds(x + g * 8 * rows, 8, stride=rows), :
                        ]
                else:
                    out[NS * 3 : NS * 3 + 16, at] = edge_ref[h, kept, 0:16]
                    out[NS * 3 + 16 : NS * 3 + 24, at] = edge_ref[h, kept, 32:40]
    pick_rows(table_ref, index_ref, weight_ref, list(range(4, SPLIT)), middle_ref, capacity)


def middle_kernel(table_ref, index_ref, weight_ref, middle_ref, *, first, capacity):
    chosen = list(range(first, first + middle_ref.shape[1]))
    pick_rows(table_ref, index_ref, weight_ref, chosen, middle_ref, capacity)


def holder(x, rows, edge_ref, middle_refs):
    if x < 4:
        return edge_ref, x
    if x >= rows - 4:
        return edge_ref, x - rows + 8
    return (middle_refs[0], x - 4) if x < SPLIT else (middle_refs[1], x - SPLIT)


def ring_smooth(plane):
    plane = plane + 0.5 * (pltpu.roll(plane, 1, 0) + pltpu.roll(plane, XR - 1, 0))
    return plane + 0.5 * (pltpu.roll(plane, 1, 1) + pltpu.roll(plane, YR - 1, 1))


def basis_kernel(
    gx_ref, gy_ref, gz_ref, edge_ref, middle_0_ref, middle_1_ref, mask_ref, far_mask_ref,
    right_ref, left_ref, above_ref, below_ref,
    basis_ref, moments_ref,
    ext_ref, source_ref, air_ref, last_ref, *, last_gx, last_gy
):
    gx, gy = gx_ref[0], gy_ref[0]
    lower = gz_ref[0] == 0
    halves, rows = edge_ref.shape[0], mask_ref.shape[0] // LZ
    cols = 128 * halves
    lane = lax.broadcasted_iota(jnp.int32, (8, 128), 1)

    for x in range(rows):
        held_ref, j = holder(x, rows, edge_ref, (middle_0_ref, middle_1_ref))
        for h in range(halves):
            ext_ref[h, NS * x : NS * x + NF] = held_ref[h, j]
        for g in range(NS // 8):
            at = slice(8 * g, 8 * g + 8)
            right = pltpu.roll(right_ref[at], (128 - 4 * x) % 128, 1)
            left = pltpu.roll(left_ref[at], (124 - 4 * x) % 128, 1)
            side = jnp.where(lane < 4, right, jnp.where(lane >= 124, left, 0.0))
            ext_ref[halves, NS * x + 8 * g : NS * x + 8 * g + 8] = side

    for d in range(4):
        for near_ref, ring, origin in (
            (above_ref, rows + d, d),
            (below_ref, XR - 1 - d, rows - 1 - d),
        ):
            base = ring * NS
            for h in range(halves):
                at = slice(128 * h, 128 * h + 128)
                if d < 3:
                    ext_ref[h, base : base + NS] = near_ref[NS * d : NS * d + NS, at]
                else:
                    ext_ref[h, base : base + 16] = near_ref[NS * 3 : NS * 3 + 16, at]
                    ext_ref[h, base + 16 : base + 32] = jnp.zeros((16, 128), F32)
                    ext_ref[h, base + 32 : base + 40] = near_ref[NS * 3 + 16 : NS * 3 + 24, at]
                    ext_ref[h, base + 40 : base + NS] = jnp.zeros((LZ, 128), F32)
            for g in range(NS // 8):
                at = slice(STRIP + 8 * g, STRIP + 8 * g + 8)
                right = pltpu.roll(near_ref[at, 0:128], (128 - 4 * origin) % 128, 1)
                left = pltpu.roll(near_ref[at, 128:256], (124 - 4 * origin) % 128, 1)
                side = jnp.where(lane < 4, right, jnp.where(lane >= 124, left, 0.0))
                ext_ref[halves, base + 8 * g : base + 8 * g + 8] = side

    def source_row(x):
        here, after, prior = x * NS, (x + 1) % XR * NS, (x - 1) % XR * NS

        def row_of(start, f):
            return jnp.concatenate(
                [ext_ref[h, start + f : start + f + 8, :] for h in range(halves + 1)], axis=1
            )

        def east(f):
            return row_of(after, f) - row_of(prior, f)

        def north(f):
            value = row_of(here, f)
            return pltpu.roll(value, YR - 1, 1) - pltpu.roll(value, 1, 1)

        out = x * 24
        values = (
            0.5 * east(0) + 0.5 * north(16),
            0.5 * east(8) + 0.5 * north(24),
            0.5 * east(32) + 0.5 * pltpu.roll(north(32), 5, 0),
        )
        for g, value in enumerate(values):
            for h in range(halves + 1):
                source_ref[h, out + 8 * g : out + 8 * g + 8, :] = value[
                    :, 128 * h : 128 * h + 128
                ]

    for x in range(XR):
        source_row(x)

    row_id = lax.broadcasted_iota(jnp.int32, (XR, YR), 0)
    col_id = lax.broadcasted_iota(jnp.int32, (XR, YR), 1)
    row_in = (row_id < 32) | ((row_id < 36) & (gx < last_gx)) | ((row_id >= 36) & (gx > 0))
    col_in = (
        (col_id < 256) | ((col_id < 260) & (gy < last_gy)) | ((col_id >= 380) & (gy > 0))
    )
    inside = jnp.where(row_in & col_in, 1.0, 0.0)
    for layer in range(LZ + DEEP):
        picked = layer if layer < LZ else 23 - layer
        for group in range(XR // 8):
            for h in range(YR // 128):
                at = slice(128 * h, 128 * h + 128)
                x = slice(8 * group, 8 * group + 8)
                if group < 4 and h < 2:
                    if layer < LZ:
                        known = mask_ref[rows * picked + 8 * group : rows * picked + 8 * group + 8, at]
                    else:
                        first = rows * (picked - 5) + 8 * group
                        known = far_mask_ref[first : first + 8, at]
                    known = known.astype(F32)
                else:
                    known = ext_ref[h, pl.ds(8 * group * NS + NF + picked, 8, stride=NS), :]
                full = inside[x, at]
                air = jnp.where(lower, known, full) if layer < LZ else jnp.where(lower, full, known)
                air_ref[layer, x, at] = air
                source = air * source_ref[h, pl.ds(8 * group * 24 + layer, 8, stride=24), :]
                value = source / (14.0 * air + (1.0 - air))
                if layer < LZ + 1:
                    basis_ref[0, layer, x, at] = value
                else:
                    last_ref[0, layer - LZ - 1, x, at] = value

    def read(k, layer):
        if layer < LZ + 1:
            return basis_ref[k, layer]
        return last_ref[k, layer - LZ - 1]

    def advance(k, layer):
        here = read(k, layer)
        beside = read(k, layer + 1)
        if layer > 0:
            beside = beside + read(k, layer - 1)
        return air_ref[layer] * (ring_smooth(here + 0.5 * beside) - here) * (1.0 / 7.0)

    sums = [None] * 6

    def add(at, value):
        value = value[:, 0:128] + value[:, 128:256]
        sums[at] = value if sums[at] is None else sums[at] + value

    for layer in range(LZ + 2):
        value = advance(0, layer)
        if layer < LZ + 1:
            basis_ref[1, layer] = value
        else:
            last_ref[1, layer - LZ - 1] = value
    for layer in range(LZ + 1):
        basis_ref[2, layer] = advance(1, layer)
    for layer in range(LZ):
        third = advance(2, layer)[0:rows, 0:cols]
        first, second, zero = (basis_ref[k, layer, 0:rows, 0:cols] for k in (1, 2, 0))
        air = air_ref[layer, 0:rows, 0:cols]
        scaling = 14.0 * air + (1.0 - air)
        zero_s, first_s, second_s = zero * scaling, first * scaling, second * scaling
        add(0, zero_s * zero)
        add(1, zero_s * first)
        add(2, first_s * first)
        add(3, first_s * second)
        add(4, second_s * second)
        add(5, second_s * third)
    lane_id = lax.broadcasted_iota(jnp.int32, (1, 128), 1)
    packed = jnp.zeros((1, 128), F32)
    for k, value in enumerate(sums):
        value = jnp.sum(jnp.sum(value, axis=0, keepdims=True), axis=1, keepdims=True)
        packed = jnp.where(lane_id == k, value, packed)
    moments_ref[...] = jnp.broadcast_to(packed, moments_ref.shape)


def iterate(nu):
    def inner(a, b):
        total = None
        for i, left in enumerate(a):
            for j, right in enumerate(b):
                term = left * right * nu[i + j]
                total = term if total is None else total + term
        return total

    one = jnp.ones_like(nu[0])
    precond = [one]
    direction = [one]
    potential = []
    current = nu[0]
    for step in range(3):
        applied = (
            [direction[0]]
            + [direction[i] - direction[i - 1] for i in range(1, len(direction))]
            + [-direction[-1]]
        )
        alpha = current / inner(direction, applied)
        potential = [
            (potential[i] + alpha * d) if i < len(potential) else alpha * d
            for i, d in enumerate(direction)
        ]
        if step < 2:
            precond = [
                (precond[i] - alpha * a) if i < len(precond) else -(alpha * a)
                for i, a in enumerate(applied)
            ]
            updated = inner(precond, precond)
            ratio = updated / current
            direction = [
                (p + ratio * direction[i]) if i < len(direction) else p
                for i, p in enumerate(precond)
            ]
            current = updated
    return potential


def wind_kernel(
    gz_ref, moments_ref, basis_ref, edge_ref, middle_0_ref, middle_1_ref, mask_ref,
    potential_ref, wind_ref, speed_ref, balance_ref, p_ref, grid_ref
):
    gz = gz_ref[0]
    rows, cols = speed_ref.shape
    near = 4 * NF
    for h in range(cols // 128):
        grid_ref[h, 0:near] = edge_ref[h, 0:near]
        grid_ref[h, near : SPLIT * NF] = middle_0_ref[h]
        grid_ref[h, SPLIT * NF : (rows - 4) * NF] = middle_1_ref[h]
        grid_ref[h, (rows - 4) * NF :] = edge_ref[h, near:]
    totals = jnp.sum(moments_ref[...], axis=0, keepdims=True)
    factors = iterate([totals[:, k : k + 1] for k in range(6)])
    factors = [jnp.broadcast_to(c, (8, 128)) for c in factors]
    factors = [jnp.tile(c, (XR // 8, YR // 128)) for c in factors]

    def combine(layer):
        return (
            factors[0] * basis_ref[0, layer]
            + factors[1] * basis_ref[1, layer]
            + factors[2] * basis_ref[2, layer]
        )

    for layer in range(LZ + 1):
        p_ref[layer] = combine(layer)
    upward = jnp.where(gz == 0, 0.5, -0.5)

    def wind_of(layer, below):
        here = p_ref[layer]
        slope_up = p_ref[layer + 1][0:rows, 0:cols]
        if below:
            slope_up = slope_up - p_ref[layer - 1][0:rows, 0:cols]
        slope_up = upward * slope_up
        slope_east = 0.5 * (pltpu.roll(here, XR - 1, 0) - pltpu.roll(here, 1, 0))[0:rows, 0:cols]
        slope_north = 0.5 * (pltpu.roll(here, YR - 1, 1) - pltpu.roll(here, 1, 1))[0:rows, 0:cols]
        out = jnp.where(gz == 0, layer, LZ - 1 - layer)
        potential_ref[out] = here[0:rows, 0:cols]
        for group in range(rows // 8):
            x = slice(8 * group, 8 * group + 8)
            for h in range(cols // 128):
                at = slice(128 * h, 128 * h + 128)
                east = grid_ref[h, pl.ds(8 * group * NF + layer, 8, stride=NF), :]
                north = grid_ref[h, pl.ds(8 * group * NF + LZ + layer, 8, stride=NF), :]
                air = mask_ref[out, x, at].astype(F32)
                a = air * (east + slope_east[x, at])
                b = air * (north + slope_north[x, at])
                c = air * slope_up[x, at]
                wind_ref[0, out, x, at] = a
                wind_ref[1, out, x, at] = b
                wind_ref[2, out, x, at] = c
                speed = jnp.sqrt(a * a + b * b + c * c)
                if below:
                    speed = speed_ref[x, at] + speed
                speed_ref[x, at] = speed

    for layer in range(LZ):
        wind_of(layer, layer > 0)
    for group in range(rows // 8):
        x = slice(8 * group, 8 * group + 8)
        for h in range(cols // 128):
            at = slice(128 * h, 128 * h + 128)
            temp = grid_ref[h, pl.ds(8 * group * NF + NF - 2, 8, stride=NF), :] / 32.0
            humid = grid_ref[h, pl.ds(8 * group * NF + NF - 1, 8, stride=NF), :] / 32.0
            balance_ref[x, at] = 1.2 + 0.5 * jnp.tanh(humid) - 0.3 * jnp.tanh(temp)


def fuel_kernel(speed_ref, other_ref, balance_ref, start_ref, out_ref):
    speed_mean = (speed_ref[...] + other_ref[...]) / 32.0
    balance = balance_ref[...]
    for kind, lag in enumerate(LAGS):
        decay_rate = jnp.exp(-(1.0 + 0.5 * speed_mean) / lag)
        moisture = start_ref[kind]
        for hour in range(PASSES):
            goal = balance + 0.3 * math.cos(2.0 * math.pi * hour / 24.0)
            moisture = goal + (moisture - goal) * decay_rate
        out_ref[kind] = moisture


def shifted(block, axis, by):
    count = lax.axis_size(axis)
    pairs = [(i, i + by) for i in range(count) if 0 <= i + by < count]
    return lax.ppermute(block, axis, pairs)


def swapped(block, axis, bit):
    count = lax.axis_size(axis)
    return lax.ppermute(block, axis, [(i, i ^ bit) for i in range(count)])


def shards(
    era5_columns,
    column_owner,
    live_counts,
    vertical_weights,
    stencil_index,
    stencil_weight,
    terrain_mask,
    fuel_start,
):
    gx, gy, gz = (lax.axis_index(a).astype(jnp.int32) for a in ("gx", GY, "gz"))
    gx, gy, gz = gx.reshape(1), gy.reshape(1), gz.reshape(1)
    tiles = lax.axis_size(("gx", *GY))
    rows_in = column_owner.shape[1]
    capacity = rows_in // tiles
    slots = tiles * capacity
    layers, rows, cols = terrain_mask.shape
    halves = cols // 128
    vmem = pl.BlockSpec(memory_space=pltpu.VMEM)
    smem = pl.BlockSpec(memory_space=pltpu.SMEM)

    def kernel(
        body, name, outs, operands, scratch=(), in_smem=0, anywhere=(), tail=None, vmem_mib=28, cost=None
    ):
        inputs = len(operands)
        own_refs = inputs + len(outs) + len(scratch)

        def whole(*refs):
            refs, extra = list(refs[:own_refs]), refs[own_refs:]
            copies = []
            for i, at in enumerate(anywhere):
                from_ref = refs[at]
                if at == tail:
                    from_ref = from_ref.at[pl.ds(from_ref.shape[0] - far_rows, far_rows)]
                copies.append(pltpu.make_async_copy(from_ref, extra[2 * i], extra[2 * i + 1]))
                refs[at] = extra[2 * i]
            for copy in copies:
                copy.start()
            for copy in copies:
                copy.wait()
            body(*refs)

        specs = [smem if at < in_smem else vmem for at in range(inputs)]
        more = []
        for at in anywhere:
            specs[at] = pl.BlockSpec(memory_space=pl.ANY)
            shape = (far_rows, cols) if at == tail else operands[at].shape
            more.append(pltpu.VMEM(shape, operands[at].dtype))
            more.append(pltpu.SemaphoreType.DMA)
        return pl.pallas_call(
            whole,
            out_shape=tuple(jax.ShapeDtypeStruct(shape, dtype) for shape, dtype in outs),
            in_specs=specs,
            out_specs=(vmem,) * len(outs),
            scratch_shapes=[pltpu.VMEM(shape, dtype) for shape, dtype in scratch] + more,
            compiler_params=pltpu.CompilerParams(vmem_limit_bytes=vmem_mib * 1024 * 1024),
            cost_estimate=cost,
            name=name,
        )(*operands)

    near_mask = terrain_mask.reshape(layers * rows, cols)
    far_mask = swapped(terrain_mask, "gz", 1).reshape(layers * rows, cols)
    far_rows = DEEP * rows
    own, leaving = kernel(
        profile_kernel,
        "profile",
        [((NF, rows_in), F32), ((8, rows_in), F32)],
        [gz, vertical_weights, era5_columns[0]],
        in_smem=1,
        vmem_mib=PROFILE,
    )
    other = swapped(leaving, "gz", 1)
    (target,) = kernel(
        functools.partial(rank_kernel, tiles=tiles, capacity=capacity),
        "rank",
        [((1, rows_in), jnp.int32)],
        [live_counts, column_owner],
        in_smem=1,
        cost=pl.CostEstimate(flops=300_000_000, bytes_accessed=3_000_000, transcendentals=0),
    )
    target, other = lax.optimization_barrier((target, other))
    (outgoing,) = kernel(
        place_kernel,
        "place",
        [((slots // 2, 128), F32)],
        [target, own, other],
    )
    outgoing, far_mask, gx, gy, gz = lax.optimization_barrier((outgoing, far_mask, gx, gy, gz))
    received = lax.all_to_all(
        outgoing.reshape(tiles, capacity // 2, 128),
        ("gx", *GY),
        split_axis=0,
        concat_axis=0,
        tiled=True,
    ).reshape(slots // 2, 128)
    table, low_y, high_y = kernel(
        functools.partial(table_kernel, capacity=capacity),
        "table",
        [((slots // 256 * NF, 512), BF16), ((NS, 128), F32), ((NS, 128), F32)],
        [gz, received, stencil_index, stencil_weight, near_mask, far_mask],
        scratch=[((halves, layers * rows, 128), F32)],
        in_smem=1,
        anywhere=(5,),
        tail=5,
    )
    right = shifted(low_y, GY, -1)
    left = shifted(high_y, GY, 1)
    edge, middle_0, low_x, high_x = kernel(
        functools.partial(edge_kernel, capacity=capacity),
        "edge",
        [
            ((halves, 8, NF, 128), F32),
            ((halves, SPLIT - 4, NF, 128), F32),
            ((STRIP + NS, cols), F32),
            ((STRIP + NS, cols), F32),
        ],
        [gz, table, stencil_index, stencil_weight, near_mask, far_mask],
        scratch=[((halves, layers * rows, 128), F32)],
        in_smem=1,
        anywhere=(5,),
        tail=5,
        cost=pl.CostEstimate(flops=3_000_000_000, bytes_accessed=2_500_000, transcendentals=0),
    )
    corners = jnp.concatenate([right, left], axis=1)
    low_x, high_x = low_x.at[STRIP:].set(corners), high_x.at[STRIP:].set(corners)
    table, low_x, high_x = lax.optimization_barrier((table, low_x, high_x))
    above = shifted(low_x, "gx", -1)
    below = shifted(high_x, "gx", 1)
    (middle_1,) = kernel(
        functools.partial(middle_kernel, first=SPLIT, capacity=capacity),
        "middle",
        [((halves, rows - 4 - SPLIT, NF, 128), F32)],
        [table, stencil_index, stencil_weight],
        cost=pl.CostEstimate(flops=3_000_000_000, bytes_accessed=1_600_000, transcendentals=0),
    )
    middles = (middle_0, middle_1)

    devices = tiles * lax.axis_size("gz")
    basis, moments = kernel(
        functools.partial(
            basis_kernel, last_gx=lax.axis_size("gx") - 1, last_gy=lax.axis_size(GY) - 1
        ),
        "basis",
        [((3, LZ + 1, XR, YR), F32), ((devices, 128), F32)],
        [gx, gy, gz, edge, *middles, near_mask, far_mask, right, left, above, below],
        scratch=[
            ((YR // 128, XR * NS, 128), F32),
            ((YR // 128, XR * 24, 128), F32),
            ((LZ + DEEP, XR, YR), F32),
            ((2, DEEP - 1, XR, YR), F32),
        ],
        in_smem=3,
        anywhere=(7, 8, 9, 10, 11),
        tail=7,
    )
    moments = lax.all_to_all(
        moments, ("gx", *GY, "gz"), split_axis=0, concat_axis=0, tiled=True
    )
    potential, wind_field, speed, balance = kernel(
        wind_kernel,
        "wind",
        [
            ((layers, rows, cols), F32),
            ((3, layers, rows, cols), F32),
            ((rows, cols), F32),
            ((rows, cols), F32),
        ],
        [
            gz,
            moments,
            basis,
            *(piece.reshape(halves, -1, 128) for piece in (edge, *middles)),
            terrain_mask,
        ],
        scratch=[((LZ + 1, XR, YR), F32), ((halves, rows * NF, 128), F32)],
        in_smem=1,
    )
    (fuel_moisture,) = kernel(
        fuel_kernel,
        "fuel",
        [((len(LAGS), rows, cols), F32)],
        [speed, swapped(speed, "gz", 1), balance, fuel_start],
        anywhere=(1,),
    )
    return (potential, wind_field, fuel_moisture)


def solution(mesh):
    placed = (
        P(("gx", *GY), None, "gz"),
        P(("gx", *GY), None),
        P(("gx", *GY)),
        P("gz", None),
        P(None, "gx", GY),
        P(None, "gx", GY),
        P("gz", "gx", GY),
        P(None, "gx", GY),
    )
    return jax.shard_map(
        shards,
        mesh=mesh,
        in_specs=placed,
        out_specs=(P("gz", "gx", GY), P(None, "gz", "gx", GY), P(None, "gx", GY)),
        check_vma=False,
    )
```

```python
import functools
import math

import jax
import jax.numpy as jnp
from jax import lax
from jax.experimental import pallas as pl
from jax.experimental.pallas import tpu as pltpu
from jax.sharding import PartitionSpec as P

F32 = jnp.float32
BF16 = jnp.bfloat16
PASSES = 4
LAGS = (1.0, 10.0, 100.0)

LZ = 16
DEEP = 3
NF = 40
NS = NF + LZ
STRIP = NS * 3 + 24
XR = 40
YR = 384


SPLIT = 8
LOADING = 60
GY = ("gy",)


def split(value):
    high = value.astype(BF16)
    return high, (value - high.astype(F32)).astype(BF16)


def dot_nt(a, b):
    return lax.dot_general(a, b, (((1,), (1,)), ((), ())), preferred_element_type=F32)


def profile_kernel(gz_ref, weights_ref, columns_ref, own_ref, leaving_ref):
    plain = weights_ref[...]
    turned = jnp.concatenate([plain[LZ - 1 - i : LZ - i] for i in range(LZ)], axis=0)
    weights = jnp.where(gz_ref[0] == 0, plain, turned)
    total = jnp.sum(plain, axis=0, keepdims=True)
    edge = jnp.concatenate([weights[LZ - 1 - i : LZ - i] for i in range(DEEP)], axis=0)

    def at_field(value, field):
        blank = jnp.zeros_like(value)
        return jnp.concatenate([value if f == field else blank for f in range(4)], axis=1)

    sums = [at_field(total, 2), at_field(total, 3)]
    stack = jnp.concatenate(
        [at_field(weights, 0), at_field(weights, 1), jnp.zeros((2 * DEEP, columns_ref.shape[1]), F32)]
        + sums
        + [at_field(edge, 0), at_field(edge, 1)]
        + sums,
        axis=0,
    )
    w_high, w_low = split(stack)
    c_high, c_low = split(columns_ref[...])
    profile = dot_nt(w_high, c_high) + dot_nt(w_high, c_low) + dot_nt(w_low, c_high)
    own_ref[...] = profile[:NF]
    leaving_ref[...] = profile[NF:]


def rank_kernel(live_ref, owner_ref, target_ref, *, tiles, capacity):
    rows = owner_ref.shape[1]
    slots = tiles * capacity
    half = capacity // 2
    position = lax.broadcasted_iota(jnp.int32, (1, rows), 1)
    owner = jnp.where(position < live_ref[0], owner_ref[...], -1)
    matches = lax.broadcasted_iota(jnp.int32, (tiles, rows), 0) == owner
    hits = jnp.where(matches, 1.0, 0.0)
    earlier = lax.broadcasted_iota(jnp.int32, (rows, rows), 0) < lax.broadcasted_iota(
        jnp.int32, (rows, rows), 1
    )
    before = jnp.dot(
        hits.astype(BF16), jnp.where(earlier, 1.0, 0.0).astype(BF16), preferred_element_type=F32
    )
    rank = jnp.sum(hits * before, axis=0, keepdims=True).astype(jnp.int32)
    upper = jnp.where(rank >= half, 1, 0)
    target_ref[...] = jnp.where(
        owner >= 0, owner * half + rank + upper * (slots // 2 - half), -1
    )


def place_kernel(target_ref, own_ref, other_ref, out_ref):
    slots = 2 * out_ref.shape[0]
    rows = target_ref.shape[1]
    profile = jnp.concatenate([own_ref[: NF - 8], own_ref[NF - 8 :] + other_ref[...]], axis=0)
    target = target_ref[...]
    place = lax.broadcasted_iota(jnp.int32, (slots, rows), 0) == target
    high, low = split(profile)
    pad = jnp.zeros((64 - NF, rows), BF16)
    both = jnp.concatenate([high, pad, low, pad], axis=0)
    placed = dot_nt(jnp.where(place, 1.0, 0.0).astype(BF16), both)
    placed = placed + pltpu.roll(placed, 64, 1)
    lane = lax.broadcasted_iota(jnp.int32, (slots // 2, 128), 1)
    out_ref[...] = jnp.where(lane < 64, placed[: slots // 2], placed[slots // 2 :])


def fill_table(received_ref, table_ref):
    blocks = received_ref.shape[0] // 256
    turned = [jnp.transpose(received_ref[256 * p : 256 * p + 256, :]) for p in range(blocks)]
    parts = 2 * blocks
    for g in range(NF // 8):
        value = jnp.concatenate(
            [
                turned[p][64 * side + 8 * g : 64 * side + 8 * g + 8]
                for side in range(2)
                for p in range(blocks)
            ],
            axis=0,
        )
        rows = slice(8 * parts * g, 8 * parts * (g + 1))
        table_ref[rows, 0:256], table_ref[rows, 256:512] = split(value)


def place_of(slot, capacity):
    half = capacity // 2
    bits = half.bit_length() - 1
    row = ((slot >> (bits + 1)) << bits) | (slot & (half - 1))
    return row, (slot >> bits) & 1


def pick_columns(table_ref, index, weight, capacity):
    parts = table_ref.shape[0] // NF
    total = weight[0] + weight[1] + weight[2] + weight[3]
    slot = lax.broadcasted_iota(jnp.int32, (256, 256), 0).astype(F32).astype(BF16)
    acc = [None] * (NF // 8)
    for point in range(len(index)):
        row, side = place_of(index[point], capacity)
        low = jnp.broadcast_to((row & 255).astype(F32), (16, 256)).astype(BF16)
        low = jnp.concatenate([low] * 16, axis=0)
        chosen = jnp.where(slot == low, jnp.ones((256, 256), BF16), jnp.zeros((256, 256), BF16))
        chosen = jnp.concatenate([chosen, chosen], axis=0)
        found = jnp.dot(table_ref[...], chosen, preferred_element_type=F32)
        part = jnp.broadcast_to((row >> 8) + side * (parts // 2), (8, 256))
        share = jnp.broadcast_to(weight[point] / total, (8, 256))
        for g in range(NF // 8):
            values = [
                found[8 * (parts * g + p) : 8 * (parts * g + p) + 8] for p in range(parts)
            ]
            bit = 1
            while len(values) > 1:
                odd = (part & bit) != 0
                values = [
                    jnp.where(odd, values[i + 1], values[i]) for i in range(0, len(values), 2)
                ]
                bit *= 2
            term = values[0] * share
            acc[g] = term if acc[g] is None else acc[g] + term
    return acc


def pick_rows(table_ref, index_ref, weight_ref, chosen, out_ref, capacity):
    points, _, cols = index_ref.shape
    for at, x in enumerate(chosen):
        got = pick_columns(
            table_ref,
            [index_ref[k, x : x + 1, :] for k in range(points)],
            [weight_ref[k, x : x + 1, :] for k in range(points)],
            capacity,
        )
        for g in range(NF // 8):
            for h in range(cols // 128):
                out_ref[h, at, 8 * g : 8 * g + 8, :] = got[g][:, 128 * h : 128 * h + 128]


def fill_mask(lower, mask_ref, far_mask_ref, mask_f_ref):
    first = mask_ref.shape[0] // 2 - far_mask_ref.shape[0]
    last = first + far_mask_ref.shape[0]
    for h in range(mask_f_ref.shape[0]):
        at = slice(128 * h, 128 * h + 128)
        mask_f_ref[h, 0:first] = mask_ref[0:first, at].astype(F32)
        mask_f_ref[h, first:last] = jnp.where(
            lower, mask_ref[first:last, at], far_mask_ref[:, at]
        ).astype(F32)
        mask_f_ref[h, last:] = mask_ref[last:, at].astype(F32)


def table_kernel(
    gz_ref, received_ref, index_ref, weight_ref, mask_ref, far_mask_ref,
    table_ref, low_y_ref, high_y_ref, mask_f_ref, *, capacity
):
    points, rows, cols = index_ref.shape
    fill_table(received_ref, table_ref)
    fill_mask(gz_ref[0] == 0, mask_ref, far_mask_ref, mask_f_ref)
    lane = lax.broadcasted_iota(jnp.int32, (8, 128), 1)
    row = lax.broadcasted_iota(jnp.int32, (8, 128), 0)

    def packed(value_ref, k):
        sides = []
        for start, turn in ((0, 0), (cols - 128, 4)):
            total = None
            for group in range(rows // 8):
                value = value_ref[k, 8 * group : 8 * group + 8, start : start + 128]
                value = pltpu.roll(value, 32 * group + turn, 1, stride=4, stride_axis=0)
                value = jnp.where((lane >> 2) == row + 8 * group, value, jnp.zeros_like(value))
                total = value if total is None else total + value
            sides.append(jnp.sum(total, axis=0, keepdims=True))
        return jnp.concatenate(sides, axis=1)

    got = pick_columns(
        table_ref,
        [packed(index_ref, k) for k in range(points)],
        [packed(weight_ref, k) for k in range(points)],
        capacity,
    )
    for side, out in ((0, low_y_ref), (1, high_y_ref)):
        for g in range(NF // 8):
            out[8 * g : 8 * g + 8] = got[g][:, 128 * side : 128 * side + 128]
        start, turn = ((0, 0), (cols - 128, 4))[side]
        for g in range(LZ // 8):
            total = None
            for x in range(rows):
                value = mask_f_ref[start // 128, pl.ds(x + g * 8 * rows, 8, stride=rows), :]
                value = pltpu.roll(value, (4 * x + turn) % 128, 1)
                total = value if total is None else jnp.where((lane >> 2) == x, value, total)
            out[NF + 8 * g : NF + 8 * g + 8] = total


def edge_kernel(
    gz_ref, table_ref, index_ref, weight_ref, mask_ref, far_mask_ref,
    edge_ref, middle_ref, low_x_ref, high_x_ref, mask_f_ref, *, capacity
):
    _, rows, cols = index_ref.shape
    chosen = [0, 1, 2, 3] + [rows - 4 + j for j in range(4)]
    pick_rows(table_ref, index_ref, weight_ref, chosen, edge_ref, capacity)
    fill_mask(gz_ref[0] == 0, mask_ref, far_mask_ref, mask_f_ref)
    for d in range(4):
        for out, x, kept in ((low_x_ref, d, d), (high_x_ref, rows - 1 - d, 7 - d)):
            for h in range(cols // 128):
                at = slice(128 * h, 128 * h + 128)
                if d < 3:
                    out[NS * d : NS * d + NF, at] = edge_ref[h, kept]
                    for g in range(LZ // 8):
                        first = NS * d + NF + 8 * g
                        out[first : first + 8, at] = mask_f_ref[
                            h, pl.ds(x + g * 8 * rows, 8, stride=rows), :
                        ]
                else:
                    out[NS * 3 : NS * 3 + 16, at] = edge_ref[h, kept, 0:16]
                    out[NS * 3 + 16 : NS * 3 + 24, at] = edge_ref[h, kept, 32:40]
    pick_rows(table_ref, index_ref, weight_ref, list(range(4, SPLIT)), middle_ref, capacity)


def middle_kernel(table_ref, index_ref, weight_ref, middle_ref, *, first, capacity):
    chosen = list(range(first, first + middle_ref.shape[1]))
    pick_rows(table_ref, index_ref, weight_ref, chosen, middle_ref, capacity)


def holder(x, rows, edge_ref, middle_refs):
    if x < 4:
        return edge_ref, x
    if x >= rows - 4:
        return edge_ref, x - rows + 8
    return (middle_refs[0], x - 4) if x < SPLIT else (middle_refs[1], x - SPLIT)


def ring_smooth(plane):
    plane = plane + 0.5 * (pltpu.roll(plane, 1, 0) + pltpu.roll(plane, XR - 1, 0))
    return plane + 0.5 * (pltpu.roll(plane, 1, 1) + pltpu.roll(plane, YR - 1, 1))


def basis_kernel(
    gx_ref, gy_ref, gz_ref, edge_ref, middle_0_ref, middle_1_ref, mask_ref, far_mask_ref,
    right_ref, left_ref, above_ref, below_ref,
    basis_ref, moments_ref,
    ext_ref, source_ref, air_ref, last_ref, *, last_gx, last_gy
):
    gx, gy = gx_ref[0], gy_ref[0]
    lower = gz_ref[0] == 0
    halves, rows = edge_ref.shape[0], mask_ref.shape[0] // LZ
    cols = 128 * halves
    lane = lax.broadcasted_iota(jnp.int32, (8, 128), 1)

    for x in range(rows):
        held_ref, j = holder(x, rows, edge_ref, (middle_0_ref, middle_1_ref))
        for h in range(halves):
            ext_ref[h, NS * x : NS * x + NF] = held_ref[h, j]
        for g in range(NS // 8):
            at = slice(8 * g, 8 * g + 8)
            right = pltpu.roll(right_ref[at], (128 - 4 * x) % 128, 1)
            left = pltpu.roll(left_ref[at], (124 - 4 * x) % 128, 1)
            side = jnp.where(lane < 4, right, jnp.where(lane >= 124, left, 0.0))
            ext_ref[halves, NS * x + 8 * g : NS * x + 8 * g + 8] = side

    for d in range(4):
        for near_ref, ring, origin in (
            (above_ref, rows + d, d),
            (below_ref, XR - 1 - d, rows - 1 - d),
        ):
            base = ring * NS
            for h in range(halves):
                at = slice(128 * h, 128 * h + 128)
                if d < 3:
                    ext_ref[h, base : base + NS] = near_ref[NS * d : NS * d + NS, at]
                else:
                    ext_ref[h, base : base + 16] = near_ref[NS * 3 : NS * 3 + 16, at]
                    ext_ref[h, base + 16 : base + 32] = jnp.zeros((16, 128), F32)
                    ext_ref[h, base + 32 : base + 40] = near_ref[NS * 3 + 16 : NS * 3 + 24, at]
                    ext_ref[h, base + 40 : base + NS] = jnp.zeros((LZ, 128), F32)
            for g in range(NS // 8):
                at = slice(STRIP + 8 * g, STRIP + 8 * g + 8)
                right = pltpu.roll(near_ref[at, 0:128], (128 - 4 * origin) % 128, 1)
                left = pltpu.roll(near_ref[at, 128:256], (124 - 4 * origin) % 128, 1)
                side = jnp.where(lane < 4, right, jnp.where(lane >= 124, left, 0.0))
                ext_ref[halves, base + 8 * g : base + 8 * g + 8] = side

    def source_row(x):
        here, after, prior = x * NS, (x + 1) % XR * NS, (x - 1) % XR * NS

        def row_of(start, f):
            return jnp.concatenate(
                [ext_ref[h, start + f : start + f + 8, :] for h in range(halves + 1)], axis=1
            )

        def east(f):
            return row_of(after, f) - row_of(prior, f)

        def north(f):
            value = row_of(here, f)
            return pltpu.roll(value, YR - 1, 1) - pltpu.roll(value, 1, 1)

        out = x * 24
        values = (
            0.5 * east(0) + 0.5 * north(16),
            0.5 * east(8) + 0.5 * north(24),
            0.5 * east(32) + 0.5 * pltpu.roll(north(32), 5, 0),
        )
        for g, value in enumerate(values):
            for h in range(halves + 1):
                source_ref[h, out + 8 * g : out + 8 * g + 8, :] = value[
                    :, 128 * h : 128 * h + 128
                ]

    for x in range(XR):
        source_row(x)

    row_id = lax.broadcasted_iota(jnp.int32, (XR, YR), 0)
    col_id = lax.broadcasted_iota(jnp.int32, (XR, YR), 1)
    row_in = (row_id < 32) | ((row_id < 36) & (gx < last_gx)) | ((row_id >= 36) & (gx > 0))
    col_in = (
        (col_id < 256) | ((col_id < 260) & (gy < last_gy)) | ((col_id >= 380) & (gy > 0))
    )
    inside = jnp.where(row_in & col_in, 1.0, 0.0)
    for layer in range(LZ + DEEP):
        picked = layer if layer < LZ else 23 - layer
        for group in range(XR // 8):
            for h in range(YR // 128):
                at = slice(128 * h, 128 * h + 128)
                x = slice(8 * group, 8 * group + 8)
                if group < 4 and h < 2:
                    if layer < LZ:
                        known = mask_ref[rows * picked + 8 * group : rows * picked + 8 * group + 8, at]
                    else:
                        first = rows * (picked - 5) + 8 * group
                        known = far_mask_ref[first : first + 8, at]
                    known = known.astype(F32)
                else:
                    known = ext_ref[h, pl.ds(8 * group * NS + NF + picked, 8, stride=NS), :]
                full = inside[x, at]
                air = jnp.where(lower, known, full) if layer < LZ else jnp.where(lower, full, known)
                air_ref[layer, x, at] = air
                source = air * source_ref[h, pl.ds(8 * group * 24 + layer, 8, stride=24), :]
                value = source / (14.0 * air + (1.0 - air))
                if layer < LZ + 1:
                    basis_ref[0, layer, x, at] = value
                else:
                    last_ref[0, layer - LZ - 1, x, at] = value

    def read(k, layer):
        if layer < LZ + 1:
            return basis_ref[k, layer]
        return last_ref[k, layer - LZ - 1]

    def advance(k, layer):
        here = read(k, layer)
        beside = read(k, layer + 1)
        if layer > 0:
            beside = beside + read(k, layer - 1)
        return air_ref[layer] * (ring_smooth(here + 0.5 * beside) - here) * (1.0 / 7.0)

    sums = [None] * 6

    def add(at, value):
        value = value[:, 0:128] + value[:, 128:256]
        sums[at] = value if sums[at] is None else sums[at] + value

    for layer in range(LZ + 2):
        value = advance(0, layer)
        if layer < LZ + 1:
            basis_ref[1, layer] = value
        else:
            last_ref[1, layer - LZ - 1] = value
    for layer in range(LZ + 1):
        basis_ref[2, layer] = advance(1, layer)
    for layer in range(LZ):
        third = advance(2, layer)[0:rows, 0:cols]
        first, second, zero = (basis_ref[k, layer, 0:rows, 0:cols] for k in (1, 2, 0))
        air = air_ref[layer, 0:rows, 0:cols]
        scaling = 14.0 * air + (1.0 - air)
        zero_s, first_s, second_s = zero * scaling, first * scaling, second * scaling
        add(0, zero_s * zero)
        add(1, zero_s * first)
        add(2, first_s * first)
        add(3, first_s * second)
        add(4, second_s * second)
        add(5, second_s * third)
    lane_id = lax.broadcasted_iota(jnp.int32, (1, 128), 1)
    packed = jnp.zeros((1, 128), F32)
    for k, value in enumerate(sums):
        value = jnp.sum(jnp.sum(value, axis=0, keepdims=True), axis=1, keepdims=True)
        packed = jnp.where(lane_id == k, value, packed)
    moments_ref[...] = jnp.broadcast_to(packed, moments_ref.shape)


def iterate(nu):
    def inner(a, b):
        total = None
        for i, left in enumerate(a):
            for j, right in enumerate(b):
                term = left * right * nu[i + j]
                total = term if total is None else total + term
        return total

    one = jnp.ones_like(nu[0])
    precond = [one]
    direction = [one]
    potential = []
    current = nu[0]
    for step in range(3):
        applied = (
            [direction[0]]
            + [direction[i] - direction[i - 1] for i in range(1, len(direction))]
            + [-direction[-1]]
        )
        alpha = current / inner(direction, applied)
        potential = [
            (potential[i] + alpha * d) if i < len(potential) else alpha * d
            for i, d in enumerate(direction)
        ]
        if step < 2:
            precond = [
                (precond[i] - alpha * a) if i < len(precond) else -(alpha * a)
                for i, a in enumerate(applied)
            ]
            updated = inner(precond, precond)
            ratio = updated / current
            direction = [
                (p + ratio * direction[i]) if i < len(direction) else p
                for i, p in enumerate(precond)
            ]
            current = updated
    return potential


def wind_kernel(
    gz_ref, moments_ref, basis_ref, edge_ref, middle_0_ref, middle_1_ref, mask_ref,
    potential_ref, wind_ref, speed_ref, balance_ref, p_ref, grid_ref
):
    gz = gz_ref[0]
    rows, cols = speed_ref.shape
    near = 4 * NF
    for h in range(cols // 128):
        grid_ref[h, 0:near] = edge_ref[h, 0:near]
        grid_ref[h, near : SPLIT * NF] = middle_0_ref[h]
        grid_ref[h, SPLIT * NF : (rows - 4) * NF] = middle_1_ref[h]
        grid_ref[h, (rows - 4) * NF :] = edge_ref[h, near:]
    totals = jnp.sum(moments_ref[...], axis=0, keepdims=True)
    factors = iterate([totals[:, k : k + 1] for k in range(6)])
    factors = [jnp.broadcast_to(c, (8, 128)) for c in factors]
    factors = [jnp.tile(c, (XR // 8, YR // 128)) for c in factors]

    def combine(layer):
        return (
            factors[0] * basis_ref[0, layer]
            + factors[1] * basis_ref[1, layer]
            + factors[2] * basis_ref[2, layer]
        )

    for layer in range(LZ + 1):
        p_ref[layer] = combine(layer)
    upward = jnp.where(gz == 0, 0.5, -0.5)

    def wind_of(layer, below):
        here = p_ref[layer]
        slope_up = p_ref[layer + 1][0:rows, 0:cols]
        if below:
            slope_up = slope_up - p_ref[layer - 1][0:rows, 0:cols]
        slope_up = upward * slope_up
        slope_east = 0.5 * (pltpu.roll(here, XR - 1, 0) - pltpu.roll(here, 1, 0))[0:rows, 0:cols]
        slope_north = 0.5 * (pltpu.roll(here, YR - 1, 1) - pltpu.roll(here, 1, 1))[0:rows, 0:cols]
        out = jnp.where(gz == 0, layer, LZ - 1 - layer)
        potential_ref[out] = here[0:rows, 0:cols]
        for group in range(rows // 8):
            x = slice(8 * group, 8 * group + 8)
            for h in range(cols // 128):
                at = slice(128 * h, 128 * h + 128)
                east = grid_ref[h, pl.ds(8 * group * NF + layer, 8, stride=NF), :]
                north = grid_ref[h, pl.ds(8 * group * NF + LZ + layer, 8, stride=NF), :]
                air = mask_ref[out, x, at].astype(F32)
                a = air * (east + slope_east[x, at])
                b = air * (north + slope_north[x, at])
                c = air * slope_up[x, at]
                wind_ref[0, out, x, at] = a
                wind_ref[1, out, x, at] = b
                wind_ref[2, out, x, at] = c
                speed = jnp.sqrt(a * a + b * b + c * c)
                if below:
                    speed = speed_ref[x, at] + speed
                speed_ref[x, at] = speed

    for layer in range(LZ):
        wind_of(layer, layer > 0)
    for group in range(rows // 8):
        x = slice(8 * group, 8 * group + 8)
        for h in range(cols // 128):
            at = slice(128 * h, 128 * h + 128)
            temp = grid_ref[h, pl.ds(8 * group * NF + NF - 2, 8, stride=NF), :] / 32.0
            humid = grid_ref[h, pl.ds(8 * group * NF + NF - 1, 8, stride=NF), :] / 32.0
            balance_ref[x, at] = 1.2 + 0.5 * jnp.tanh(humid) - 0.3 * jnp.tanh(temp)


def fuel_kernel(speed_ref, other_ref, balance_ref, start_ref, out_ref):
    speed_mean = (speed_ref[...] + other_ref[...]) / 32.0
    balance = balance_ref[...]
    for kind, lag in enumerate(LAGS):
        decay_rate = jnp.exp(-(1.0 + 0.5 * speed_mean) / lag)
        moisture = start_ref[kind]
        for hour in range(PASSES):
            goal = balance + 0.3 * math.cos(2.0 * math.pi * hour / 24.0)
            moisture = goal + (moisture - goal) * decay_rate
        out_ref[kind] = moisture


def shifted(block, axis, by):
    count = lax.axis_size(axis)
    pairs = [(i, i + by) for i in range(count) if 0 <= i + by < count]
    return lax.ppermute(block, axis, pairs)


def swapped(block, axis, bit):
    count = lax.axis_size(axis)
    return lax.ppermute(block, axis, [(i, i ^ bit) for i in range(count)])


def shards(
    era5_columns,
    column_owner,
    live_counts,
    vertical_weights,
    stencil_index,
    stencil_weight,
    terrain_mask,
    fuel_start,
):
    gx, gy, gz = (lax.axis_index(a).astype(jnp.int32) for a in ("gx", GY, "gz"))
    gx, gy, gz = gx.reshape(1), gy.reshape(1), gz.reshape(1)
    tiles = lax.axis_size(("gx", *GY))
    rows_in = column_owner.shape[1]
    capacity = rows_in // tiles
    slots = tiles * capacity
    layers, rows, cols = terrain_mask.shape
    halves = cols // 128
    vmem = pl.BlockSpec(memory_space=pltpu.VMEM)
    smem = pl.BlockSpec(memory_space=pltpu.SMEM)

    def kernel(
        body, name, outs, operands, scratch=(), in_smem=0, anywhere=(), tail=None, vmem_mib=28, cost=None
    ):
        inputs = len(operands)
        own_refs = inputs + len(outs) + len(scratch)

        def whole(*refs):
            refs, extra = list(refs[:own_refs]), refs[own_refs:]
            copies = []
            for i, at in enumerate(anywhere):
                from_ref = refs[at]
                if at == tail:
                    from_ref = from_ref.at[pl.ds(from_ref.shape[0] - far_rows, far_rows)]
                copies.append(pltpu.make_async_copy(from_ref, extra[2 * i], extra[2 * i + 1]))
                refs[at] = extra[2 * i]
            for copy in copies:
                copy.start()
            for copy in copies:
                copy.wait()
            body(*refs)

        specs = [smem if at < in_smem else vmem for at in range(inputs)]
        more = []
        for at in anywhere:
            specs[at] = pl.BlockSpec(memory_space=pl.ANY)
            shape = (far_rows, cols) if at == tail else operands[at].shape
            more.append(pltpu.VMEM(shape, operands[at].dtype))
            more.append(pltpu.SemaphoreType.DMA)
        return pl.pallas_call(
            whole,
            out_shape=tuple(jax.ShapeDtypeStruct(shape, dtype) for shape, dtype in outs),
            in_specs=specs,
            out_specs=(vmem,) * len(outs),
            scratch_shapes=[pltpu.VMEM(shape, dtype) for shape, dtype in scratch] + more,
            compiler_params=pltpu.CompilerParams(vmem_limit_bytes=vmem_mib * 1024 * 1024),
            cost_estimate=cost,
            name=name,
        )(*operands)

    near_mask = terrain_mask.reshape(layers * rows, cols)
    far_mask = swapped(terrain_mask, "gz", 1).reshape(layers * rows, cols)
    far_rows = DEEP * rows
    own, leaving = kernel(
        profile_kernel,
        "profile",
        [((NF, rows_in), F32), ((8, rows_in), F32)],
        [gz, vertical_weights, era5_columns[0]],
        in_smem=1,
        vmem_mib=LOADING,
    )
    other = swapped(leaving, "gz", 1)
    (target,) = kernel(
        functools.partial(rank_kernel, tiles=tiles, capacity=capacity),
        "rank",
        [((1, rows_in), jnp.int32)],
        [live_counts, column_owner],
        in_smem=1,
        cost=pl.CostEstimate(flops=300_000_000, bytes_accessed=3_000_000, transcendentals=0),
    )
    target, other = lax.optimization_barrier((target, other))
    (outgoing,) = kernel(
        place_kernel,
        "place",
        [((slots // 2, 128), F32)],
        [target, own, other],
    )
    outgoing, far_mask, gx, gy, gz = lax.optimization_barrier((outgoing, far_mask, gx, gy, gz))
    received = lax.all_to_all(
        outgoing.reshape(tiles, capacity // 2, 128),
        ("gx", *GY),
        split_axis=0,
        concat_axis=0,
        tiled=True,
    ).reshape(slots // 2, 128)
    table, low_y, high_y = kernel(
        functools.partial(table_kernel, capacity=capacity),
        "table",
        [((slots // 256 * NF, 512), BF16), ((NS, 128), F32), ((NS, 128), F32)],
        [gz, received, stencil_index, stencil_weight, near_mask, far_mask],
        scratch=[((halves, layers * rows, 128), F32)],
        in_smem=1,
        anywhere=(5,),
        tail=5,
        vmem_mib=LOADING,
    )
    right = shifted(low_y, GY, -1)
    left = shifted(high_y, GY, 1)
    edge, middle_0, low_x, high_x = kernel(
        functools.partial(edge_kernel, capacity=capacity),
        "edge",
        [
            ((halves, 8, NF, 128), F32),
            ((halves, SPLIT - 4, NF, 128), F32),
            ((STRIP + NS, cols), F32),
            ((STRIP + NS, cols), F32),
        ],
        [gz, table, stencil_index, stencil_weight, near_mask, far_mask],
        scratch=[((halves, layers * rows, 128), F32)],
        in_smem=1,
        anywhere=(5,),
        tail=5,
        cost=pl.CostEstimate(flops=3_000_000_000, bytes_accessed=2_500_000, transcendentals=0),
    )
    corners = jnp.concatenate([right, left], axis=1)
    low_x, high_x = low_x.at[STRIP:].set(corners), high_x.at[STRIP:].set(corners)
    table, low_x, high_x = lax.optimization_barrier((table, low_x, high_x))
    above = shifted(low_x, "gx", -1)
    below = shifted(high_x, "gx", 1)
    (middle_1,) = kernel(
        functools.partial(middle_kernel, first=SPLIT, capacity=capacity),
        "middle",
        [((halves, rows - 4 - SPLIT, NF, 128), F32)],
        [table, stencil_index, stencil_weight],
        cost=pl.CostEstimate(flops=3_000_000_000, bytes_accessed=1_600_000, transcendentals=0),
    )
    middles = (middle_0, middle_1)

    devices = tiles * lax.axis_size("gz")
    basis, moments = kernel(
        functools.partial(
            basis_kernel, last_gx=lax.axis_size("gx") - 1, last_gy=lax.axis_size(GY) - 1
        ),
        "basis",
        [((3, LZ + 1, XR, YR), F32), ((devices, 128), F32)],
        [gx, gy, gz, edge, *middles, near_mask, far_mask, right, left, above, below],
        scratch=[
            ((YR // 128, XR * NS, 128), F32),
            ((YR // 128, XR * 24, 128), F32),
            ((LZ + DEEP, XR, YR), F32),
            ((2, DEEP - 1, XR, YR), F32),
        ],
        in_smem=3,
        anywhere=(7, 8, 9, 10, 11),
        tail=7,
    )
    moments = lax.all_to_all(
        moments, ("gx", *GY, "gz"), split_axis=0, concat_axis=0, tiled=True
    )
    potential, wind_field, speed, balance = kernel(
        wind_kernel,
        "wind",
        [
            ((layers, rows, cols), F32),
            ((3, layers, rows, cols), F32),
            ((rows, cols), F32),
            ((rows, cols), F32),
        ],
        [
            gz,
            moments,
            basis,
            *(piece.reshape(halves, -1, 128) for piece in (edge, *middles)),
            terrain_mask,
        ],
        scratch=[((LZ + 1, XR, YR), F32), ((halves, rows * NF, 128), F32)],
        in_smem=1,
    )
    (fuel_moisture,) = kernel(
        fuel_kernel,
        "fuel",
        [((len(LAGS), rows, cols), F32)],
        [speed, swapped(speed, "gz", 1), balance, fuel_start],
        anywhere=(1,),
    )
    return (potential, wind_field, fuel_moisture)


def solution(mesh):
    placed = (
        P(("gx", *GY), None, "gz"),
        P(("gx", *GY), None),
        P(("gx", *GY)),
        P("gz", None),
        P(None, "gx", GY),
        P(None, "gx", GY),
        P("gz", "gx", GY),
        P(None, "gx", GY),
    )
    return jax.shard_map(
        shards,
        mesh=mesh,
        in_specs=placed,
        out_specs=(P("gz", "gx", GY), P(None, "gz", "gx", GY), P(None, "gx", GY)),
        check_vma=False,
    )
```

```python
import functools
import math

import jax
import jax.numpy as jnp
from jax import lax
from jax.experimental import pallas as pl
from jax.experimental.pallas import tpu as pltpu
from jax.sharding import PartitionSpec as P

F32 = jnp.float32
BF16 = jnp.bfloat16
PASSES = 4
LAGS = (1.0, 10.0, 100.0)

LZ = 16
DEEP = 3
NF = 40
NS = NF + LZ
STRIP = NS * 3 + 24
XR = 40
YR = 384


SPLIT = 8
GY = ("gy",)


def split(value):
    high = value.astype(BF16)
    return high, (value - high.astype(F32)).astype(BF16)


def dot_nt(a, b):
    return lax.dot_general(a, b, (((1,), (1,)), ((), ())), preferred_element_type=F32)


def route_kernel(
    gz_ref, live_ref, weights_ref, columns_ref, owner_ref, out_ref, *, tiles, capacity
):
    plain = weights_ref[...]
    turned = jnp.concatenate([plain[LZ - 1 - i : LZ - i] for i in range(LZ)], axis=0)
    weights = jnp.where(gz_ref[0] == 0, plain, turned)
    total = jnp.sum(plain, axis=0, keepdims=True)
    edge = jnp.concatenate([weights[LZ - 1 - i : LZ - i] for i in range(DEEP)], axis=0)

    def at_field(value, field):
        blank = jnp.zeros_like(value)
        return jnp.concatenate([value if f == field else blank for f in range(4)], axis=1)

    sums = [at_field(total, 2), at_field(total, 3)]
    stack = jnp.concatenate(
        [at_field(weights, 0), at_field(weights, 1), jnp.zeros((2 * DEEP, columns_ref.shape[1]), F32)]
        + sums
        + [at_field(edge, 0), at_field(edge, 1)]
        + sums,
        axis=0,
    )
    w_high, w_low = split(stack)
    c_high, c_low = split(columns_ref[...])
    profile = dot_nt(w_high, c_high) + dot_nt(w_high, c_low) + dot_nt(w_low, c_high)

    rows = owner_ref.shape[1]
    slots = tiles * capacity
    half = capacity // 2
    position = lax.broadcasted_iota(jnp.int32, (1, rows), 1)
    owner = jnp.where(position < live_ref[0], owner_ref[...], -1)
    matches = lax.broadcasted_iota(jnp.int32, (tiles, rows), 0) == owner
    hits = jnp.where(matches, 1.0, 0.0)
    earlier = lax.broadcasted_iota(jnp.int32, (rows, rows), 0) < lax.broadcasted_iota(
        jnp.int32, (rows, rows), 1
    )
    before = jnp.dot(
        hits.astype(BF16), jnp.where(earlier, 1.0, 0.0).astype(BF16), preferred_element_type=F32
    )
    rank = jnp.sum(hits * before, axis=0, keepdims=True).astype(jnp.int32)
    upper = jnp.where(rank >= half, 1, 0)
    target = jnp.where(owner >= 0, owner * half + rank + upper * (slots // 2 - half), -1)
    place = lax.broadcasted_iota(jnp.int32, (slots, rows), 0) == target
    high, low = split(profile)
    pad = jnp.zeros((64 - NF - 8, rows), BF16)
    both = jnp.concatenate([high, pad, low, pad], axis=0)
    placed = dot_nt(jnp.where(place, 1.0, 0.0).astype(BF16), both)
    placed = placed + pltpu.roll(placed, 64, 1)
    lane = lax.broadcasted_iota(jnp.int32, (slots // 2, 128), 1)
    out_ref[...] = jnp.where(lane < 64, placed[: slots // 2], placed[slots // 2 :])


def fill_table(received_ref, other_ref, table_ref):
    blocks = received_ref.shape[0] // 256
    turned = [jnp.transpose(received_ref[256 * p : 256 * p + 256, :]) for p in range(blocks)]
    beyond = [jnp.transpose(other_ref[256 * p : 256 * p + 256, :]) for p in range(blocks)]
    parts = 2 * blocks
    for g in range(NF // 8):
        value = jnp.concatenate(
            [
                turned[p][64 * side + 8 * g : 64 * side + 8 * g + 8]
                for side in range(2)
                for p in range(blocks)
            ],
            axis=0,
        )
        if g == NF // 8 - 1:
            value = value + jnp.concatenate(
                [
                    beyond[p][64 * side + NF : 64 * side + NF + 8]
                    for side in range(2)
                    for p in range(blocks)
                ],
                axis=0,
            )
        rows = slice(8 * parts * g, 8 * parts * (g + 1))
        table_ref[rows, 0:256], table_ref[rows, 256:512] = split(value)


def place_of(slot, capacity):
    half = capacity // 2
    bits = half.bit_length() - 1
    row = ((slot >> (bits + 1)) << bits) | (slot & (half - 1))
    return row, (slot >> bits) & 1


def pick_columns(table_ref, index, weight, capacity):
    parts = table_ref.shape[0] // NF
    total = weight[0] + weight[1] + weight[2] + weight[3]
    slot = lax.broadcasted_iota(jnp.int32, (256, 256), 0).astype(F32).astype(BF16)
    acc = [None] * (NF // 8)
    for point in range(len(index)):
        row, side = place_of(index[point], capacity)
        low = jnp.broadcast_to((row & 255).astype(F32), (16, 256)).astype(BF16)
        low = jnp.concatenate([low] * 16, axis=0)
        chosen = jnp.where(slot == low, jnp.ones((256, 256), BF16), jnp.zeros((256, 256), BF16))
        chosen = jnp.concatenate([chosen, chosen], axis=0)
        found = jnp.dot(table_ref[...], chosen, preferred_element_type=F32)
        part = jnp.broadcast_to((row >> 8) + side * (parts // 2), (8, 256))
        share = jnp.broadcast_to(weight[point] / total, (8, 256))
        for g in range(NF // 8):
            values = [
                found[8 * (parts * g + p) : 8 * (parts * g + p) + 8] for p in range(parts)
            ]
            bit = 1
            while len(values) > 1:
                odd = (part & bit) != 0
                values = [
                    jnp.where(odd, values[i + 1], values[i]) for i in range(0, len(values), 2)
                ]
                bit *= 2
            term = values[0] * share
            acc[g] = term if acc[g] is None else acc[g] + term
    return acc


def pick_rows(table_ref, index_ref, weight_ref, chosen, out_ref, capacity):
    points, _, cols = index_ref.shape
    for at, x in enumerate(chosen):
        got = pick_columns(
            table_ref,
            [index_ref[k, x : x + 1, :] for k in range(points)],
            [weight_ref[k, x : x + 1, :] for k in range(points)],
            capacity,
        )
        for g in range(NF // 8):
            for h in range(cols // 128):
                out_ref[h, at, 8 * g : 8 * g + 8, :] = got[g][:, 128 * h : 128 * h + 128]


def fill_mask(lower, mask_ref, far_mask_ref, mask_f_ref):
    first = mask_ref.shape[0] // 2 - far_mask_ref.shape[0]
    last = first + far_mask_ref.shape[0]
    for h in range(mask_f_ref.shape[0]):
        at = slice(128 * h, 128 * h + 128)
        mask_f_ref[h, 0:first] = mask_ref[0:first, at].astype(F32)
        mask_f_ref[h, first:last] = jnp.where(
            lower, mask_ref[first:last, at], far_mask_ref[:, at]
        ).astype(F32)
        mask_f_ref[h, last:] = mask_ref[last:, at].astype(F32)


def table_kernel(
    gz_ref, received_ref, other_ref, index_ref, weight_ref, mask_ref, far_mask_ref,
    table_ref, low_y_ref, high_y_ref, mask_f_ref, *, capacity
):
    points, rows, cols = index_ref.shape
    fill_table(received_ref, other_ref, table_ref)
    fill_mask(gz_ref[0] == 0, mask_ref, far_mask_ref, mask_f_ref)
    lane = lax.broadcasted_iota(jnp.int32, (8, 128), 1)
    row = lax.broadcasted_iota(jnp.int32, (8, 128), 0)

    def packed(value_ref, k):
        sides = []
        for start, turn in ((0, 0), (cols - 128, 4)):
            total = None
            for group in range(rows // 8):
                value = value_ref[k, 8 * group : 8 * group + 8, start : start + 128]
                value = pltpu.roll(value, 32 * group + turn, 1, stride=4, stride_axis=0)
                value = jnp.where((lane >> 2) == row + 8 * group, value, jnp.zeros_like(value))
                total = value if total is None else total + value
            sides.append(jnp.sum(total, axis=0, keepdims=True))
        return jnp.concatenate(sides, axis=1)

    got = pick_columns(
        table_ref,
        [packed(index_ref, k) for k in range(points)],
        [packed(weight_ref, k) for k in range(points)],
        capacity,
    )
    for side, out in ((0, low_y_ref), (1, high_y_ref)):
        for g in range(NF // 8):
            out[8 * g : 8 * g + 8] = got[g][:, 128 * side : 128 * side + 128]
        start, turn = ((0, 0), (cols - 128, 4))[side]
        for g in range(LZ // 8):
            total = None
            for x in range(rows):
                value = mask_f_ref[start // 128, pl.ds(x + g * 8 * rows, 8, stride=rows), :]
                value = pltpu.roll(value, (4 * x + turn) % 128, 1)
                total = value if total is None else jnp.where((lane >> 2) == x, value, total)
            out[NF + 8 * g : NF + 8 * g + 8] = total


def edge_kernel(
    gz_ref, table_ref, index_ref, weight_ref, mask_ref, far_mask_ref,
    edge_ref, middle_ref, low_x_ref, high_x_ref, mask_f_ref, *, capacity
):
    _, rows, cols = index_ref.shape
    chosen = [0, 1, 2, 3] + [rows - 4 + j for j in range(4)]
    pick_rows(table_ref, index_ref, weight_ref, chosen, edge_ref, capacity)
    fill_mask(gz_ref[0] == 0, mask_ref, far_mask_ref, mask_f_ref)
    for d in range(4):
        for out, x, kept in ((low_x_ref, d, d), (high_x_ref, rows - 1 - d, 7 - d)):
            for h in range(cols // 128):
                at = slice(128 * h, 128 * h + 128)
                if d < 3:
                    out[NS * d : NS * d + NF, at] = edge_ref[h, kept]
                    for g in range(LZ // 8):
                        first = NS * d + NF + 8 * g
                        out[first : first + 8, at] = mask_f_ref[
                            h, pl.ds(x + g * 8 * rows, 8, stride=rows), :
                        ]
                else:
                    out[NS * 3 : NS * 3 + 16, at] = edge_ref[h, kept, 0:16]
                    out[NS * 3 + 16 : NS * 3 + 24, at] = edge_ref[h, kept, 32:40]
    pick_rows(table_ref, index_ref, weight_ref, list(range(4, SPLIT)), middle_ref, capacity)


def middle_kernel(table_ref, index_ref, weight_ref, middle_ref, *, first, capacity):
    chosen = list(range(first, first + middle_ref.shape[1]))
    pick_rows(table_ref, index_ref, weight_ref, chosen, middle_ref, capacity)


def holder(x, rows, edge_ref, middle_refs):
    if x < 4:
        return edge_ref, x
    if x >= rows - 4:
        return edge_ref, x - rows + 8
    return (middle_refs[0], x - 4) if x < SPLIT else (middle_refs[1], x - SPLIT)


def ring_smooth(plane):
    plane = plane + 0.5 * (pltpu.roll(plane, 1, 0) + pltpu.roll(plane, XR - 1, 0))
    return plane + 0.5 * (pltpu.roll(plane, 1, 1) + pltpu.roll(plane, YR - 1, 1))


def basis_kernel(
    gx_ref, gy_ref, gz_ref, edge_ref, middle_0_ref, middle_1_ref, mask_ref, far_mask_ref,
    right_ref, left_ref, above_ref, below_ref,
    basis_ref, moments_ref,
    ext_ref, source_ref, air_ref, last_ref, *, last_gx, last_gy
):
    gx, gy = gx_ref[0], gy_ref[0]
    lower = gz_ref[0] == 0
    halves, rows = edge_ref.shape[0], mask_ref.shape[0] // LZ
    cols = 128 * halves
    lane = lax.broadcasted_iota(jnp.int32, (8, 128), 1)

    for x in range(rows):
        held_ref, j = holder(x, rows, edge_ref, (middle_0_ref, middle_1_ref))
        for h in range(halves):
            ext_ref[h, NS * x : NS * x + NF] = held_ref[h, j]
        for g in range(NS // 8):
            at = slice(8 * g, 8 * g + 8)
            right = pltpu.roll(right_ref[at], (128 - 4 * x) % 128, 1)
            left = pltpu.roll(left_ref[at], (124 - 4 * x) % 128, 1)
            side = jnp.where(lane < 4, right, jnp.where(lane >= 124, left, 0.0))
            ext_ref[halves, NS * x + 8 * g : NS * x + 8 * g + 8] = side

    for d in range(4):
        for near_ref, ring, origin in (
            (above_ref, rows + d, d),
            (below_ref, XR - 1 - d, rows - 1 - d),
        ):
            base = ring * NS
            for h in range(halves):
                at = slice(128 * h, 128 * h + 128)
                if d < 3:
                    ext_ref[h, base : base + NS] = near_ref[NS * d : NS * d + NS, at]
                else:
                    ext_ref[h, base : base + 16] = near_ref[NS * 3 : NS * 3 + 16, at]
                    ext_ref[h, base + 16 : base + 32] = jnp.zeros((16, 128), F32)
                    ext_ref[h, base + 32 : base + 40] = near_ref[NS * 3 + 16 : NS * 3 + 24, at]
                    ext_ref[h, base + 40 : base + NS] = jnp.zeros((LZ, 128), F32)
            for g in range(NS // 8):
                at = slice(STRIP + 8 * g, STRIP + 8 * g + 8)
                right = pltpu.roll(near_ref[at, 0:128], (128 - 4 * origin) % 128, 1)
                left = pltpu.roll(near_ref[at, 128:256], (124 - 4 * origin) % 128, 1)
                side = jnp.where(lane < 4, right, jnp.where(lane >= 124, left, 0.0))
                ext_ref[halves, base + 8 * g : base + 8 * g + 8] = side

    def source_row(x):
        here, after, prior = x * NS, (x + 1) % XR * NS, (x - 1) % XR * NS

        def row_of(start, f):
            return jnp.concatenate(
                [ext_ref[h, start + f : start + f + 8, :] for h in range(halves + 1)], axis=1
            )

        def east(f):
            return row_of(after, f) - row_of(prior, f)

        def north(f):
            value = row_of(here, f)
            return pltpu.roll(value, YR - 1, 1) - pltpu.roll(value, 1, 1)

        out = x * 24
        values = (
            0.5 * east(0) + 0.5 * north(16),
            0.5 * east(8) + 0.5 * north(24),
            0.5 * east(32) + 0.5 * pltpu.roll(north(32), 5, 0),
        )
        for g, value in enumerate(values):
            for h in range(halves + 1):
                source_ref[h, out + 8 * g : out + 8 * g + 8, :] = value[
                    :, 128 * h : 128 * h + 128
                ]

    for x in range(XR):
        source_row(x)

    row_id = lax.broadcasted_iota(jnp.int32, (XR, YR), 0)
    col_id = lax.broadcasted_iota(jnp.int32, (XR, YR), 1)
    row_in = (row_id < 32) | ((row_id < 36) & (gx < last_gx)) | ((row_id >= 36) & (gx > 0))
    col_in = (
        (col_id < 256) | ((col_id < 260) & (gy < last_gy)) | ((col_id >= 380) & (gy > 0))
    )
    inside = jnp.where(row_in & col_in, 1.0, 0.0)
    for layer in range(LZ + DEEP):
        picked = layer if layer < LZ else 23 - layer
        for group in range(XR // 8):
            for h in range(YR // 128):
                at = slice(128 * h, 128 * h + 128)
                x = slice(8 * group, 8 * group + 8)
                if group < 4 and h < 2:
                    if layer < LZ:
                        known = mask_ref[rows * picked + 8 * group : rows * picked + 8 * group + 8, at]
                    else:
                        first = rows * (picked - 5) + 8 * group
                        known = far_mask_ref[first : first + 8, at]
                    known = known.astype(F32)
                else:
                    known = ext_ref[h, pl.ds(8 * group * NS + NF + picked, 8, stride=NS), :]
                full = inside[x, at]
                air = jnp.where(lower, known, full) if layer < LZ else jnp.where(lower, full, known)
                air_ref[layer, x, at] = air
                source = air * source_ref[h, pl.ds(8 * group * 24 + layer, 8, stride=24), :]
                value = source / (14.0 * air + (1.0 - air))
                if layer < LZ + 1:
                    basis_ref[0, layer, x, at] = value
                else:
                    last_ref[0, layer - LZ - 1, x, at] = value

    def read(k, layer):
        if layer < LZ + 1:
            return basis_ref[k, layer]
        return last_ref[k, layer - LZ - 1]

    def advance(k, layer):
        here = read(k, layer)
        beside = read(k, layer + 1)
        if layer > 0:
            beside = beside + read(k, layer - 1)
        return air_ref[layer] * (ring_smooth(here + 0.5 * beside) - here) * (1.0 / 7.0)

    sums = [None] * 6

    def add(at, value):
        value = value[:, 0:128] + value[:, 128:256]
        sums[at] = value if sums[at] is None else sums[at] + value

    for layer in range(LZ + 2):
        value = advance(0, layer)
        if layer < LZ + 1:
            basis_ref[1, layer] = value
        else:
            last_ref[1, layer - LZ - 1] = value
    for layer in range(LZ + 1):
        basis_ref[2, layer] = advance(1, layer)
    for layer in range(LZ):
        third = advance(2, layer)[0:rows, 0:cols]
        first, second, zero = (basis_ref[k, layer, 0:rows, 0:cols] for k in (1, 2, 0))
        air = air_ref[layer, 0:rows, 0:cols]
        scaling = 14.0 * air + (1.0 - air)
        zero_s, first_s, second_s = zero * scaling, first * scaling, second * scaling
        add(0, zero_s * zero)
        add(1, zero_s * first)
        add(2, first_s * first)
        add(3, first_s * second)
        add(4, second_s * second)
        add(5, second_s * third)
    lane_id = lax.broadcasted_iota(jnp.int32, (1, 128), 1)
    packed = jnp.zeros((1, 128), F32)
    for k, value in enumerate(sums):
        value = jnp.sum(jnp.sum(value, axis=0, keepdims=True), axis=1, keepdims=True)
        packed = jnp.where(lane_id == k, value, packed)
    moments_ref[...] = jnp.broadcast_to(packed, moments_ref.shape)


def iterate(nu):
    def inner(a, b):
        total = None
        for i, left in enumerate(a):
            for j, right in enumerate(b):
                term = left * right * nu[i + j]
                total = term if total is None else total + term
        return total

    one = jnp.ones_like(nu[0])
    precond = [one]
    direction = [one]
    potential = []
    current = nu[0]
    for step in range(3):
        applied = (
            [direction[0]]
            + [direction[i] - direction[i - 1] for i in range(1, len(direction))]
            + [-direction[-1]]
        )
        alpha = current / inner(direction, applied)
        potential = [
            (potential[i] + alpha * d) if i < len(potential) else alpha * d
            for i, d in enumerate(direction)
        ]
        if step < 2:
            precond = [
                (precond[i] - alpha * a) if i < len(precond) else -(alpha * a)
                for i, a in enumerate(applied)
            ]
            updated = inner(precond, precond)
            ratio = updated / current
            direction = [
                (p + ratio * direction[i]) if i < len(direction) else p
                for i, p in enumerate(precond)
            ]
            current = updated
    return potential


def wind_kernel(
    gz_ref, moments_ref, basis_ref, edge_ref, middle_0_ref, middle_1_ref, mask_ref,
    potential_ref, wind_ref, speed_ref, balance_ref, p_ref, grid_ref
):
    gz = gz_ref[0]
    rows, cols = speed_ref.shape
    near = 4 * NF
    for h in range(cols // 128):
        grid_ref[h, 0:near] = edge_ref[h, 0:near]
        grid_ref[h, near : SPLIT * NF] = middle_0_ref[h]
        grid_ref[h, SPLIT * NF : (rows - 4) * NF] = middle_1_ref[h]
        grid_ref[h, (rows - 4) * NF :] = edge_ref[h, near:]
    totals = jnp.sum(moments_ref[...], axis=0, keepdims=True)
    factors = iterate([totals[:, k : k + 1] for k in range(6)])
    factors = [jnp.broadcast_to(c, (8, 128)) for c in factors]
    factors = [jnp.tile(c, (XR // 8, YR // 128)) for c in factors]

    def combine(layer):
        return (
            factors[0] * basis_ref[0, layer]
            + factors[1] * basis_ref[1, layer]
            + factors[2] * basis_ref[2, layer]
        )

    for layer in range(LZ + 1):
        p_ref[layer] = combine(layer)
    upward = jnp.where(gz == 0, 0.5, -0.5)

    def wind_of(layer, below):
        here = p_ref[layer]
        slope_up = p_ref[layer + 1][0:rows, 0:cols]
        if below:
            slope_up = slope_up - p_ref[layer - 1][0:rows, 0:cols]
        slope_up = upward * slope_up
        slope_east = 0.5 * (pltpu.roll(here, XR - 1, 0) - pltpu.roll(here, 1, 0))[0:rows, 0:cols]
        slope_north = 0.5 * (pltpu.roll(here, YR - 1, 1) - pltpu.roll(here, 1, 1))[0:rows, 0:cols]
        out = jnp.where(gz == 0, layer, LZ - 1 - layer)
        potential_ref[out] = here[0:rows, 0:cols]
        for group in range(rows // 8):
            x = slice(8 * group, 8 * group + 8)
            for h in range(cols // 128):
                at = slice(128 * h, 128 * h + 128)
                east = grid_ref[h, pl.ds(8 * group * NF + layer, 8, stride=NF), :]
                north = grid_ref[h, pl.ds(8 * group * NF + LZ + layer, 8, stride=NF), :]
                air = mask_ref[out, x, at].astype(F32)
                a = air * (east + slope_east[x, at])
                b = air * (north + slope_north[x, at])
                c = air * slope_up[x, at]
                wind_ref[0, out, x, at] = a
                wind_ref[1, out, x, at] = b
                wind_ref[2, out, x, at] = c
                speed = jnp.sqrt(a * a + b * b + c * c)
                if below:
                    speed = speed_ref[x, at] + speed
                speed_ref[x, at] = speed

    for layer in range(LZ):
        wind_of(layer, layer > 0)
    for group in range(rows // 8):
        x = slice(8 * group, 8 * group + 8)
        for h in range(cols // 128):
            at = slice(128 * h, 128 * h + 128)
            temp = grid_ref[h, pl.ds(8 * group * NF + NF - 2, 8, stride=NF), :] / 32.0
            humid = grid_ref[h, pl.ds(8 * group * NF + NF - 1, 8, stride=NF), :] / 32.0
            balance_ref[x, at] = 1.2 + 0.5 * jnp.tanh(humid) - 0.3 * jnp.tanh(temp)


def fuel_kernel(speed_ref, other_ref, balance_ref, start_ref, out_ref):
    speed_mean = (speed_ref[...] + other_ref[...]) / 32.0
    balance = balance_ref[...]
    for kind, lag in enumerate(LAGS):
        decay_rate = jnp.exp(-(1.0 + 0.5 * speed_mean) / lag)
        moisture = start_ref[kind]
        for hour in range(PASSES):
            goal = balance + 0.3 * math.cos(2.0 * math.pi * hour / 24.0)
            moisture = goal + (moisture - goal) * decay_rate
        out_ref[kind] = moisture


def shifted(block, axis, by):
    count = lax.axis_size(axis)
    pairs = [(i, i + by) for i in range(count) if 0 <= i + by < count]
    return lax.ppermute(block, axis, pairs)


def swapped(block, axis, bit):
    count = lax.axis_size(axis)
    return lax.ppermute(block, axis, [(i, i ^ bit) for i in range(count)])


def shards(
    era5_columns,
    column_owner,
    live_counts,
    vertical_weights,
    stencil_index,
    stencil_weight,
    terrain_mask,
    fuel_start,
):
    gx, gy, gz = (lax.axis_index(a).astype(jnp.int32) for a in ("gx", GY, "gz"))
    gx, gy, gz = gx.reshape(1), gy.reshape(1), gz.reshape(1)
    tiles = lax.axis_size(("gx", *GY))
    rows_in = column_owner.shape[1]
    capacity = rows_in // tiles
    slots = tiles * capacity
    layers, rows, cols = terrain_mask.shape
    halves = cols // 128
    vmem = pl.BlockSpec(memory_space=pltpu.VMEM)
    smem = pl.BlockSpec(memory_space=pltpu.SMEM)

    def kernel(
        body, name, outs, operands, scratch=(), in_smem=0, anywhere=(), tail=None, vmem_mib=28, cost=None
    ):
        inputs = len(operands)
        own_refs = inputs + len(outs) + len(scratch)

        def whole(*refs):
            refs, extra = list(refs[:own_refs]), refs[own_refs:]
            copies = []
            for i, at in enumerate(anywhere):
                from_ref = refs[at]
                if at == tail:
                    from_ref = from_ref.at[pl.ds(from_ref.shape[0] - far_rows, far_rows)]
                copies.append(pltpu.make_async_copy(from_ref, extra[2 * i], extra[2 * i + 1]))
                refs[at] = extra[2 * i]
            for copy in copies:
                copy.start()
            for copy in copies:
                copy.wait()
            body(*refs)

        specs = [smem if at < in_smem else vmem for at in range(inputs)]
        more = []
        for at in anywhere:
            specs[at] = pl.BlockSpec(memory_space=pl.ANY)
            shape = (far_rows, cols) if at == tail else operands[at].shape
            more.append(pltpu.VMEM(shape, operands[at].dtype))
            more.append(pltpu.SemaphoreType.DMA)
        return pl.pallas_call(
            whole,
            out_shape=tuple(jax.ShapeDtypeStruct(shape, dtype) for shape, dtype in outs),
            in_specs=specs,
            out_specs=(vmem,) * len(outs),
            scratch_shapes=[pltpu.VMEM(shape, dtype) for shape, dtype in scratch] + more,
            compiler_params=pltpu.CompilerParams(vmem_limit_bytes=vmem_mib * 1024 * 1024),
            cost_estimate=cost,
            name=name,
        )(*operands)

    near_mask = terrain_mask.reshape(layers * rows, cols)
    far_mask = swapped(terrain_mask, "gz", 1).reshape(layers * rows, cols)
    far_rows = DEEP * rows
    (outgoing,) = kernel(
        functools.partial(route_kernel, tiles=tiles, capacity=capacity),
        "route",
        [((slots // 2, 128), F32)],
        [gz, live_counts, vertical_weights, era5_columns[0], column_owner],
        in_smem=2,
        vmem_mib=60,
        cost=pl.CostEstimate(flops=1_000_000_000, bytes_accessed=1_000_000, transcendentals=0),
    )
    outgoing, far_mask, gx, gy, gz = lax.optimization_barrier((outgoing, far_mask, gx, gy, gz))
    received = lax.all_to_all(
        outgoing.reshape(tiles, capacity // 2, 128),
        ("gx", *GY),
        split_axis=0,
        concat_axis=0,
        tiled=True,
    ).reshape(slots // 2, 128)
    other = swapped(received, "gz", 1)

    table, low_y, high_y = kernel(
        functools.partial(table_kernel, capacity=capacity),
        "table",
        [((slots // 256 * NF, 512), BF16), ((NS, 128), F32), ((NS, 128), F32)],
        [gz, received, other, stencil_index, stencil_weight, near_mask, far_mask],
        scratch=[((halves, layers * rows, 128), F32)],
        in_smem=1,
        anywhere=(2, 6),
        tail=6,
    )
    right = shifted(low_y, GY, -1)
    left = shifted(high_y, GY, 1)
    edge, middle_0, low_x, high_x = kernel(
        functools.partial(edge_kernel, capacity=capacity),
        "edge",
        [
            ((halves, 8, NF, 128), F32),
            ((halves, SPLIT - 4, NF, 128), F32),
            ((STRIP + NS, cols), F32),
            ((STRIP + NS, cols), F32),
        ],
        [gz, table, stencil_index, stencil_weight, near_mask, far_mask],
        scratch=[((halves, layers * rows, 128), F32)],
        in_smem=1,
        anywhere=(5,),
        tail=5,
        cost=pl.CostEstimate(flops=3_000_000_000, bytes_accessed=2_500_000, transcendentals=0),
    )
    corners = jnp.concatenate([right, left], axis=1)
    low_x, high_x = low_x.at[STRIP:].set(corners), high_x.at[STRIP:].set(corners)
    table, low_x, high_x = lax.optimization_barrier((table, low_x, high_x))
    above = shifted(low_x, "gx", -1)
    below = shifted(high_x, "gx", 1)
    (middle_1,) = kernel(
        functools.partial(middle_kernel, first=SPLIT, capacity=capacity),
        "middle",
        [((halves, rows - 4 - SPLIT, NF, 128), F32)],
        [table, stencil_index, stencil_weight],
        cost=pl.CostEstimate(flops=3_000_000_000, bytes_accessed=1_600_000, transcendentals=0),
    )
    middles = (middle_0, middle_1)

    devices = tiles * lax.axis_size("gz")
    basis, moments = kernel(
        functools.partial(
            basis_kernel, last_gx=lax.axis_size("gx") - 1, last_gy=lax.axis_size(GY) - 1
        ),
        "basis",
        [((3, LZ + 1, XR, YR), F32), ((devices, 128), F32)],
        [gx, gy, gz, edge, *middles, near_mask, far_mask, right, left, above, below],
        scratch=[
            ((YR // 128, XR * NS, 128), F32),
            ((YR // 128, XR * 24, 128), F32),
            ((LZ + DEEP, XR, YR), F32),
            ((2, DEEP - 1, XR, YR), F32),
        ],
        in_smem=3,
        anywhere=(7, 8, 9, 10, 11),
        tail=7,
    )
    moments = lax.all_to_all(
        moments, ("gx", *GY, "gz"), split_axis=0, concat_axis=0, tiled=True
    )
    potential, wind_field, speed, balance = kernel(
        wind_kernel,
        "wind",
        [
            ((layers, rows, cols), F32),
            ((3, layers, rows, cols), F32),
            ((rows, cols), F32),
            ((rows, cols), F32),
        ],
        [
            gz,
            moments,
            basis,
            *(piece.reshape(halves, -1, 128) for piece in (edge, *middles)),
            terrain_mask,
        ],
        scratch=[((LZ + 1, XR, YR), F32), ((halves, rows * NF, 128), F32)],
        in_smem=1,
    )
    (fuel_moisture,) = kernel(
        fuel_kernel,
        "fuel",
        [((len(LAGS), rows, cols), F32)],
        [speed, swapped(speed, "gz", 1), balance, fuel_start],
        anywhere=(1,),
    )
    return (potential, wind_field, fuel_moisture)


def solution(mesh):
    placed = (
        P(("gx", *GY), None, "gz"),
        P(("gx", *GY), None),
        P(("gx", *GY)),
        P("gz", None),
        P(None, "gx", GY),
        P(None, "gx", GY),
        P("gz", "gx", GY),
        P(None, "gx", GY),
    )
    return jax.shard_map(
        shards,
        mesh=mesh,
        in_specs=placed,
        out_specs=(P("gz", "gx", GY), P(None, "gz", "gx", GY), P(None, "gx", GY)),
        check_vma=False,
    )
```

```python
import functools
import math

import jax
import jax.numpy as jnp
from jax import lax
from jax.experimental import pallas as pl
from jax.experimental.pallas import tpu as pltpu
from jax.sharding import PartitionSpec as P

F32 = jnp.float32
BF16 = jnp.bfloat16
PASSES = 4
LAGS = (1.0, 10.0, 100.0)

LZ = 16
DEEP = 3
NF = 40
NS = NF + LZ
STRIP = NS * 3 + 24
XR = 40
YR = 384


SPLIT = 5
GY = ("gy",)


def split(value):
    high = value.astype(BF16)
    return high, (value - high.astype(F32)).astype(BF16)


def dot_nt(a, b):
    return lax.dot_general(a, b, (((1,), (1,)), ((), ())), preferred_element_type=F32)


def route_kernel(
    gz_ref, live_ref, weights_ref, columns_ref, owner_ref, out_ref, *, tiles, capacity
):
    plain = weights_ref[...]
    turned = jnp.concatenate([plain[LZ - 1 - i : LZ - i] for i in range(LZ)], axis=0)
    weights = jnp.where(gz_ref[0] == 0, plain, turned)
    total = jnp.sum(plain, axis=0, keepdims=True)
    edge = jnp.concatenate([weights[LZ - 1 - i : LZ - i] for i in range(DEEP)], axis=0)

    def at_field(value, field):
        blank = jnp.zeros_like(value)
        return jnp.concatenate([value if f == field else blank for f in range(4)], axis=1)

    sums = [at_field(total, 2), at_field(total, 3)]
    stack = jnp.concatenate(
        [at_field(weights, 0), at_field(weights, 1), jnp.zeros((2 * DEEP, columns_ref.shape[1]), F32)]
        + sums
        + [at_field(edge, 0), at_field(edge, 1)]
        + sums,
        axis=0,
    )
    w_high, w_low = split(stack)
    c_high, c_low = split(columns_ref[...])
    profile = dot_nt(w_high, c_high) + dot_nt(w_high, c_low) + dot_nt(w_low, c_high)

    rows = owner_ref.shape[1]
    slots = tiles * capacity
    half = capacity // 2
    position = lax.broadcasted_iota(jnp.int32, (1, rows), 1)
    owner = jnp.where(position < live_ref[0], owner_ref[...], -1)
    matches = lax.broadcasted_iota(jnp.int32, (tiles, rows), 0) == owner
    hits = jnp.where(matches, 1.0, 0.0)
    earlier = lax.broadcasted_iota(jnp.int32, (rows, rows), 0) < lax.broadcasted_iota(
        jnp.int32, (rows, rows), 1
    )
    before = jnp.dot(
        hits.astype(BF16), jnp.where(earlier, 1.0, 0.0).astype(BF16), preferred_element_type=F32
    )
    rank = jnp.sum(hits * before, axis=0, keepdims=True).astype(jnp.int32)
    upper = jnp.where(rank >= half, 1, 0)
    target = jnp.where(owner >= 0, owner * half + rank + upper * (slots // 2 - half), -1)
    place = lax.broadcasted_iota(jnp.int32, (slots, rows), 0) == target
    high, low = split(profile)
    pad = jnp.zeros((64 - NF - 8, rows), BF16)
    both = jnp.concatenate([high, pad, low, pad], axis=0)
    placed = dot_nt(jnp.where(place, 1.0, 0.0).astype(BF16), both)
    placed = placed + pltpu.roll(placed, 64, 1)
    lane = lax.broadcasted_iota(jnp.int32, (slots // 2, 128), 1)
    out_ref[...] = jnp.where(lane < 64, placed[: slots // 2], placed[slots // 2 :])


def fill_table(received_ref, other_ref, table_ref):
    blocks = received_ref.shape[0] // 256
    turned = [jnp.transpose(received_ref[256 * p : 256 * p + 256, :]) for p in range(blocks)]
    beyond = [jnp.transpose(other_ref[256 * p : 256 * p + 256, :]) for p in range(blocks)]
    parts = 2 * blocks
    for g in range(NF // 8):
        value = jnp.concatenate(
            [
                turned[p][64 * side + 8 * g : 64 * side + 8 * g + 8]
                for side in range(2)
                for p in range(blocks)
            ],
            axis=0,
        )
        if g == NF // 8 - 1:
            value = value + jnp.concatenate(
                [
                    beyond[p][64 * side + NF : 64 * side + NF + 8]
                    for side in range(2)
                    for p in range(blocks)
                ],
                axis=0,
            )
        rows = slice(8 * parts * g, 8 * parts * (g + 1))
        table_ref[rows, 0:256], table_ref[rows, 256:512] = split(value)


def place_of(slot, capacity):
    half = capacity // 2
    bits = half.bit_length() - 1
    row = ((slot >> (bits + 1)) << bits) | (slot & (half - 1))
    return row, (slot >> bits) & 1


def pick_columns(table_ref, index, weight, capacity):
    parts = table_ref.shape[0] // NF
    total = weight[0] + weight[1] + weight[2] + weight[3]
    slot = lax.broadcasted_iota(jnp.int32, (256, 256), 0).astype(F32).astype(BF16)
    acc = [None] * (NF // 8)
    for point in range(len(index)):
        row, side = place_of(index[point], capacity)
        low = jnp.broadcast_to((row & 255).astype(F32), (16, 256)).astype(BF16)
        low = jnp.concatenate([low] * 16, axis=0)
        chosen = jnp.where(slot == low, jnp.ones((256, 256), BF16), jnp.zeros((256, 256), BF16))
        chosen = jnp.concatenate([chosen, chosen], axis=0)
        found = jnp.dot(table_ref[...], chosen, preferred_element_type=F32)
        part = jnp.broadcast_to((row >> 8) + side * (parts // 2), (8, 256))
        share = jnp.broadcast_to(weight[point] / total, (8, 256))
        for g in range(NF // 8):
            values = [
                found[8 * (parts * g + p) : 8 * (parts * g + p) + 8] for p in range(parts)
            ]
            bit = 1
            while len(values) > 1:
                odd = (part & bit) != 0
                values = [
                    jnp.where(odd, values[i + 1], values[i]) for i in range(0, len(values), 2)
                ]
                bit *= 2
            term = values[0] * share
            acc[g] = term if acc[g] is None else acc[g] + term
    return acc


def pick_rows(table_ref, index_ref, weight_ref, chosen, out_ref, capacity):
    points, _, cols = index_ref.shape
    for at, x in enumerate(chosen):
        got = pick_columns(
            table_ref,
            [index_ref[k, x : x + 1, :] for k in range(points)],
            [weight_ref[k, x : x + 1, :] for k in range(points)],
            capacity,
        )
        for g in range(NF // 8):
            for h in range(cols // 128):
                out_ref[h, at, 8 * g : 8 * g + 8, :] = got[g][:, 128 * h : 128 * h + 128]


def fill_mask(lower, mask_ref, far_mask_ref, mask_f_ref):
    first = mask_ref.shape[0] // 2 - far_mask_ref.shape[0]
    last = first + far_mask_ref.shape[0]
    for h in range(mask_f_ref.shape[0]):
        at = slice(128 * h, 128 * h + 128)
        mask_f_ref[h, 0:first] = mask_ref[0:first, at].astype(F32)
        mask_f_ref[h, first:last] = jnp.where(
            lower, mask_ref[first:last, at], far_mask_ref[:, at]
        ).astype(F32)
        mask_f_ref[h, last:] = mask_ref[last:, at].astype(F32)


def table_kernel(
    gz_ref, received_ref, other_ref, index_ref, weight_ref, mask_ref, far_mask_ref,
    table_ref, low_y_ref, high_y_ref, mask_f_ref, *, capacity
):
    points, rows, cols = index_ref.shape
    fill_table(received_ref, other_ref, table_ref)
    fill_mask(gz_ref[0] == 0, mask_ref, far_mask_ref, mask_f_ref)
    lane = lax.broadcasted_iota(jnp.int32, (8, 128), 1)
    row = lax.broadcasted_iota(jnp.int32, (8, 128), 0)

    def packed(value_ref, k):
        sides = []
        for start, turn in ((0, 0), (cols - 128, 4)):
            total = None
            for group in range(rows // 8):
                value = value_ref[k, 8 * group : 8 * group + 8, start : start + 128]
                value = pltpu.roll(value, 32 * group + turn, 1, stride=4, stride_axis=0)
                value = jnp.where((lane >> 2) == row + 8 * group, value, jnp.zeros_like(value))
                total = value if total is None else total + value
            sides.append(jnp.sum(total, axis=0, keepdims=True))
        return jnp.concatenate(sides, axis=1)

    got = pick_columns(
        table_ref,
        [packed(index_ref, k) for k in range(points)],
        [packed(weight_ref, k) for k in range(points)],
        capacity,
    )
    for side, out in ((0, low_y_ref), (1, high_y_ref)):
        for g in range(NF // 8):
            out[8 * g : 8 * g + 8] = got[g][:, 128 * side : 128 * side + 128]
        start, turn = ((0, 0), (cols - 128, 4))[side]
        for g in range(LZ // 8):
            total = None
            for x in range(rows):
                value = mask_f_ref[start // 128, pl.ds(x + g * 8 * rows, 8, stride=rows), :]
                value = pltpu.roll(value, (4 * x + turn) % 128, 1)
                total = value if total is None else jnp.where((lane >> 2) == x, value, total)
            out[NF + 8 * g : NF + 8 * g + 8] = total


def edge_kernel(
    gz_ref, table_ref, index_ref, weight_ref, mask_ref, far_mask_ref,
    edge_ref, middle_ref, low_x_ref, high_x_ref, mask_f_ref, *, capacity
):
    _, rows, cols = index_ref.shape
    chosen = [0, 1, 2, 3] + [rows - 4 + j for j in range(4)]
    pick_rows(table_ref, index_ref, weight_ref, chosen, edge_ref, capacity)
    fill_mask(gz_ref[0] == 0, mask_ref, far_mask_ref, mask_f_ref)
    for d in range(4):
        for out, x, kept in ((low_x_ref, d, d), (high_x_ref, rows - 1 - d, 7 - d)):
            for h in range(cols // 128):
                at = slice(128 * h, 128 * h + 128)
                if d < 3:
                    out[NS * d : NS * d + NF, at] = edge_ref[h, kept]
                    for g in range(LZ // 8):
                        first = NS * d + NF + 8 * g
                        out[first : first + 8, at] = mask_f_ref[
                            h, pl.ds(x + g * 8 * rows, 8, stride=rows), :
                        ]
                else:
                    out[NS * 3 : NS * 3 + 16, at] = edge_ref[h, kept, 0:16]
                    out[NS * 3 + 16 : NS * 3 + 24, at] = edge_ref[h, kept, 32:40]
    pick_rows(table_ref, index_ref, weight_ref, list(range(4, SPLIT)), middle_ref, capacity)


def middle_kernel(table_ref, index_ref, weight_ref, middle_ref, *, first, capacity):
    chosen = list(range(first, first + middle_ref.shape[1]))
    pick_rows(table_ref, index_ref, weight_ref, chosen, middle_ref, capacity)


def holder(x, rows, edge_ref, middle_refs):
    if x < 4:
        return edge_ref, x
    if x >= rows - 4:
        return edge_ref, x - rows + 8
    return (middle_refs[0], x - 4) if x < SPLIT else (middle_refs[1], x - SPLIT)


def ring_smooth(plane):
    plane = plane + 0.5 * (pltpu.roll(plane, 1, 0) + pltpu.roll(plane, XR - 1, 0))
    return plane + 0.5 * (pltpu.roll(plane, 1, 1) + pltpu.roll(plane, YR - 1, 1))


def basis_kernel(
    gx_ref, gy_ref, gz_ref, edge_ref, middle_0_ref, middle_1_ref, mask_ref, far_mask_ref,
    right_ref, left_ref, above_ref, below_ref,
    basis_ref, moments_ref,
    ext_ref, source_ref, air_ref, last_ref, *, last_gx, last_gy
):
    gx, gy = gx_ref[0], gy_ref[0]
    lower = gz_ref[0] == 0
    halves, rows = edge_ref.shape[0], mask_ref.shape[0] // LZ
    cols = 128 * halves
    lane = lax.broadcasted_iota(jnp.int32, (8, 128), 1)

    for x in range(rows):
        held_ref, j = holder(x, rows, edge_ref, (middle_0_ref, middle_1_ref))
        for h in range(halves):
            ext_ref[h, NS * x : NS * x + NF] = held_ref[h, j]
        for g in range(NS // 8):
            at = slice(8 * g, 8 * g + 8)
            right = pltpu.roll(right_ref[at], (128 - 4 * x) % 128, 1)
            left = pltpu.roll(left_ref[at], (124 - 4 * x) % 128, 1)
            side = jnp.where(lane < 4, right, jnp.where(lane >= 124, left, 0.0))
            ext_ref[halves, NS * x + 8 * g : NS * x + 8 * g + 8] = side

    for d in range(4):
        for near_ref, ring, origin in (
            (above_ref, rows + d, d),
            (below_ref, XR - 1 - d, rows - 1 - d),
        ):
            base = ring * NS
            for h in range(halves):
                at = slice(128 * h, 128 * h + 128)
                if d < 3:
                    ext_ref[h, base : base + NS] = near_ref[NS * d : NS * d + NS, at]
                else:
                    ext_ref[h, base : base + 16] = near_ref[NS * 3 : NS * 3 + 16, at]
                    ext_ref[h, base + 16 : base + 32] = jnp.zeros((16, 128), F32)
                    ext_ref[h, base + 32 : base + 40] = near_ref[NS * 3 + 16 : NS * 3 + 24, at]
                    ext_ref[h, base + 40 : base + NS] = jnp.zeros((LZ, 128), F32)
            for g in range(NS // 8):
                at = slice(STRIP + 8 * g, STRIP + 8 * g + 8)
                right = pltpu.roll(near_ref[at, 0:128], (128 - 4 * origin) % 128, 1)
                left = pltpu.roll(near_ref[at, 128:256], (124 - 4 * origin) % 128, 1)
                side = jnp.where(lane < 4, right, jnp.where(lane >= 124, left, 0.0))
                ext_ref[halves, base + 8 * g : base + 8 * g + 8] = side

    def source_row(x):
        here, after, prior = x * NS, (x + 1) % XR * NS, (x - 1) % XR * NS

        def row_of(start, f):
            return jnp.concatenate(
                [ext_ref[h, start + f : start + f + 8, :] for h in range(halves + 1)], axis=1
            )

        def east(f):
            return row_of(after, f) - row_of(prior, f)

        def north(f):
            value = row_of(here, f)
            return pltpu.roll(value, YR - 1, 1) - pltpu.roll(value, 1, 1)

        out = x * 24
        values = (
            0.5 * east(0) + 0.5 * north(16),
            0.5 * east(8) + 0.5 * north(24),
            0.5 * east(32) + 0.5 * pltpu.roll(north(32), 5, 0),
        )
        for g, value in enumerate(values):
            for h in range(halves + 1):
                source_ref[h, out + 8 * g : out + 8 * g + 8, :] = value[
                    :, 128 * h : 128 * h + 128
                ]

    for x in range(XR):
        source_row(x)

    row_id = lax.broadcasted_iota(jnp.int32, (XR, YR), 0)
    col_id = lax.broadcasted_iota(jnp.int32, (XR, YR), 1)
    row_in = (row_id < 32) | ((row_id < 36) & (gx < last_gx)) | ((row_id >= 36) & (gx > 0))
    col_in = (
        (col_id < 256) | ((col_id < 260) & (gy < last_gy)) | ((col_id >= 380) & (gy > 0))
    )
    inside = jnp.where(row_in & col_in, 1.0, 0.0)
    for layer in range(LZ + DEEP):
        picked = layer if layer < LZ else 23 - layer
        for group in range(XR // 8):
            for h in range(YR // 128):
                at = slice(128 * h, 128 * h + 128)
                x = slice(8 * group, 8 * group + 8)
                if group < 4 and h < 2:
                    if layer < LZ:
                        known = mask_ref[rows * picked + 8 * group : rows * picked + 8 * group + 8, at]
                    else:
                        first = rows * (picked - 5) + 8 * group
                        known = far_mask_ref[first : first + 8, at]
                    known = known.astype(F32)
                else:
                    known = ext_ref[h, pl.ds(8 * group * NS + NF + picked, 8, stride=NS), :]
                full = inside[x, at]
                air = jnp.where(lower, known, full) if layer < LZ else jnp.where(lower, full, known)
                air_ref[layer, x, at] = air
                source = air * source_ref[h, pl.ds(8 * group * 24 + layer, 8, stride=24), :]
                value = source / (14.0 * air + (1.0 - air))
                if layer < LZ + 1:
                    basis_ref[0, layer, x, at] = value
                else:
                    last_ref[0, layer - LZ - 1, x, at] = value

    def read(k, layer):
        if layer < LZ + 1:
            return basis_ref[k, layer]
        return last_ref[k, layer - LZ - 1]

    def advance(k, layer):
        here = read(k, layer)
        beside = read(k, layer + 1)
        if layer > 0:
            beside = beside + read(k, layer - 1)
        return air_ref[layer] * (ring_smooth(here + 0.5 * beside) - here) * (1.0 / 7.0)

    sums = [None] * 6

    def add(at, value):
        value = value[:, 0:128] + value[:, 128:256]
        sums[at] = value if sums[at] is None else sums[at] + value

    for layer in range(LZ + 2):
        value = advance(0, layer)
        if layer < LZ + 1:
            basis_ref[1, layer] = value
        else:
            last_ref[1, layer - LZ - 1] = value
    for layer in range(LZ + 1):
        basis_ref[2, layer] = advance(1, layer)
    for layer in range(LZ):
        third = advance(2, layer)[0:rows, 0:cols]
        first, second, zero = (basis_ref[k, layer, 0:rows, 0:cols] for k in (1, 2, 0))
        air = air_ref[layer, 0:rows, 0:cols]
        scaling = 14.0 * air + (1.0 - air)
        zero_s, first_s, second_s = zero * scaling, first * scaling, second * scaling
        add(0, zero_s * zero)
        add(1, zero_s * first)
        add(2, first_s * first)
        add(3, first_s * second)
        add(4, second_s * second)
        add(5, second_s * third)
    lane_id = lax.broadcasted_iota(jnp.int32, (1, 128), 1)
    packed = jnp.zeros((1, 128), F32)
    for k, value in enumerate(sums):
        value = jnp.sum(jnp.sum(value, axis=0, keepdims=True), axis=1, keepdims=True)
        packed = jnp.where(lane_id == k, value, packed)
    moments_ref[...] = jnp.broadcast_to(packed, moments_ref.shape)


def iterate(nu):
    def inner(a, b):
        total = None
        for i, left in enumerate(a):
            for j, right in enumerate(b):
                term = left * right * nu[i + j]
                total = term if total is None else total + term
        return total

    one = jnp.ones_like(nu[0])
    precond = [one]
    direction = [one]
    potential = []
    current = nu[0]
    for step in range(3):
        applied = (
            [direction[0]]
            + [direction[i] - direction[i - 1] for i in range(1, len(direction))]
            + [-direction[-1]]
        )
        alpha = current / inner(direction, applied)
        potential = [
            (potential[i] + alpha * d) if i < len(potential) else alpha * d
            for i, d in enumerate(direction)
        ]
        if step < 2:
            precond = [
                (precond[i] - alpha * a) if i < len(precond) else -(alpha * a)
                for i, a in enumerate(applied)
            ]
            updated = inner(precond, precond)
            ratio = updated / current
            direction = [
                (p + ratio * direction[i]) if i < len(direction) else p
                for i, p in enumerate(precond)
            ]
            current = updated
    return potential


def wind_kernel(
    gz_ref, moments_ref, basis_ref, edge_ref, middle_0_ref, middle_1_ref, mask_ref,
    potential_ref, wind_ref, speed_ref, balance_ref, p_ref, grid_ref
):
    gz = gz_ref[0]
    rows, cols = speed_ref.shape
    near = 4 * NF
    for h in range(cols // 128):
        grid_ref[h, 0:near] = edge_ref[h, 0:near]
        grid_ref[h, near : SPLIT * NF] = middle_0_ref[h]
        grid_ref[h, SPLIT * NF : (rows - 4) * NF] = middle_1_ref[h]
        grid_ref[h, (rows - 4) * NF :] = edge_ref[h, near:]
    totals = jnp.sum(moments_ref[...], axis=0, keepdims=True)
    factors = iterate([totals[:, k : k + 1] for k in range(6)])
    factors = [jnp.broadcast_to(c, (8, 128)) for c in factors]
    factors = [jnp.tile(c, (XR // 8, YR // 128)) for c in factors]

    def combine(layer):
        return (
            factors[0] * basis_ref[0, layer]
            + factors[1] * basis_ref[1, layer]
            + factors[2] * basis_ref[2, layer]
        )

    for layer in range(LZ + 1):
        p_ref[layer] = combine(layer)
    upward = jnp.where(gz == 0, 0.5, -0.5)

    def wind_of(layer, below):
        here = p_ref[layer]
        slope_up = p_ref[layer + 1][0:rows, 0:cols]
        if below:
            slope_up = slope_up - p_ref[layer - 1][0:rows, 0:cols]
        slope_up = upward * slope_up
        slope_east = 0.5 * (pltpu.roll(here, XR - 1, 0) - pltpu.roll(here, 1, 0))[0:rows, 0:cols]
        slope_north = 0.5 * (pltpu.roll(here, YR - 1, 1) - pltpu.roll(here, 1, 1))[0:rows, 0:cols]
        out = jnp.where(gz == 0, layer, LZ - 1 - layer)
        potential_ref[out] = here[0:rows, 0:cols]
        for group in range(rows // 8):
            x = slice(8 * group, 8 * group + 8)
            for h in range(cols // 128):
                at = slice(128 * h, 128 * h + 128)
                east = grid_ref[h, pl.ds(8 * group * NF + layer, 8, stride=NF), :]
                north = grid_ref[h, pl.ds(8 * group * NF + LZ + layer, 8, stride=NF), :]
                air = mask_ref[out, x, at].astype(F32)
                a = air * (east + slope_east[x, at])
                b = air * (north + slope_north[x, at])
                c = air * slope_up[x, at]
                wind_ref[0, out, x, at] = a
                wind_ref[1, out, x, at] = b
                wind_ref[2, out, x, at] = c
                speed = jnp.sqrt(a * a + b * b + c * c)
                if below:
                    speed = speed_ref[x, at] + speed
                speed_ref[x, at] = speed

    for layer in range(LZ):
        wind_of(layer, layer > 0)
    for group in range(rows // 8):
        x = slice(8 * group, 8 * group + 8)
        for h in range(cols // 128):
            at = slice(128 * h, 128 * h + 128)
            temp = grid_ref[h, pl.ds(8 * group * NF + NF - 2, 8, stride=NF), :] / 32.0
            humid = grid_ref[h, pl.ds(8 * group * NF + NF - 1, 8, stride=NF), :] / 32.0
            balance_ref[x, at] = 1.2 + 0.5 * jnp.tanh(humid) - 0.3 * jnp.tanh(temp)


def fuel_kernel(speed_ref, other_ref, balance_ref, start_ref, out_ref):
    speed_mean = (speed_ref[...] + other_ref[...]) / 32.0
    balance = balance_ref[...]
    for kind, lag in enumerate(LAGS):
        decay_rate = jnp.exp(-(1.0 + 0.5 * speed_mean) / lag)
        moisture = start_ref[kind]
        for hour in range(PASSES):
            goal = balance + 0.3 * math.cos(2.0 * math.pi * hour / 24.0)
            moisture = goal + (moisture - goal) * decay_rate
        out_ref[kind] = moisture


def shifted(block, axis, by):
    count = lax.axis_size(axis)
    pairs = [(i, i + by) for i in range(count) if 0 <= i + by < count]
    return lax.ppermute(block, axis, pairs)


def swapped(block, axis, bit):
    count = lax.axis_size(axis)
    return lax.ppermute(block, axis, [(i, i ^ bit) for i in range(count)])


def shards(
    era5_columns,
    column_owner,
    live_counts,
    vertical_weights,
    stencil_index,
    stencil_weight,
    terrain_mask,
    fuel_start,
):
    gx, gy, gz = (lax.axis_index(a).astype(jnp.int32) for a in ("gx", GY, "gz"))
    gx, gy, gz = gx.reshape(1), gy.reshape(1), gz.reshape(1)
    tiles = lax.axis_size(("gx", *GY))
    rows_in = column_owner.shape[1]
    capacity = rows_in // tiles
    slots = tiles * capacity
    layers, rows, cols = terrain_mask.shape
    halves = cols // 128
    vmem = pl.BlockSpec(memory_space=pltpu.VMEM)
    smem = pl.BlockSpec(memory_space=pltpu.SMEM)

    def kernel(
        body, name, outs, operands, scratch=(), in_smem=0, anywhere=(), tail=None, vmem_mib=28, cost=None
    ):
        inputs = len(operands)
        own_refs = inputs + len(outs) + len(scratch)

        def whole(*refs):
            refs, extra = list(refs[:own_refs]), refs[own_refs:]
            copies = []
            for i, at in enumerate(anywhere):
                from_ref = refs[at]
                if at == tail:
                    from_ref = from_ref.at[pl.ds(from_ref.shape[0] - far_rows, far_rows)]
                copies.append(pltpu.make_async_copy(from_ref, extra[2 * i], extra[2 * i + 1]))
                refs[at] = extra[2 * i]
            for copy in copies:
                copy.start()
            for copy in copies:
                copy.wait()
            body(*refs)

        specs = [smem if at < in_smem else vmem for at in range(inputs)]
        more = []
        for at in anywhere:
            specs[at] = pl.BlockSpec(memory_space=pl.ANY)
            shape = (far_rows, cols) if at == tail else operands[at].shape
            more.append(pltpu.VMEM(shape, operands[at].dtype))
            more.append(pltpu.SemaphoreType.DMA)
        return pl.pallas_call(
            whole,
            out_shape=tuple(jax.ShapeDtypeStruct(shape, dtype) for shape, dtype in outs),
            in_specs=specs,
            out_specs=(vmem,) * len(outs),
            scratch_shapes=[pltpu.VMEM(shape, dtype) for shape, dtype in scratch] + more,
            compiler_params=pltpu.CompilerParams(vmem_limit_bytes=vmem_mib * 1024 * 1024),
            cost_estimate=cost,
            name=name,
        )(*operands)

    near_mask = terrain_mask.reshape(layers * rows, cols)
    far_mask = swapped(terrain_mask, "gz", 1).reshape(layers * rows, cols)
    far_rows = DEEP * rows
    (outgoing,) = kernel(
        functools.partial(route_kernel, tiles=tiles, capacity=capacity),
        "route",
        [((slots // 2, 128), F32)],
        [gz, live_counts, vertical_weights, era5_columns[0], column_owner],
        in_smem=2,
        vmem_mib=60,
        cost=pl.CostEstimate(flops=1_000_000_000, bytes_accessed=1_000_000, transcendentals=0),
    )
    outgoing, far_mask, gx, gy, gz = lax.optimization_barrier((outgoing, far_mask, gx, gy, gz))
    received = lax.all_to_all(
        outgoing.reshape(tiles, capacity // 2, 128),
        ("gx", *GY),
        split_axis=0,
        concat_axis=0,
        tiled=True,
    ).reshape(slots // 2, 128)
    other = swapped(received, "gz", 1)

    table, low_y, high_y = kernel(
        functools.partial(table_kernel, capacity=capacity),
        "table",
        [((slots // 256 * NF, 512), BF16), ((NS, 128), F32), ((NS, 128), F32)],
        [gz, received, other, stencil_index, stencil_weight, near_mask, far_mask],
        scratch=[((halves, layers * rows, 128), F32)],
        in_smem=1,
        anywhere=(2, 6),
        tail=6,
    )
    right = shifted(low_y, GY, -1)
    left = shifted(high_y, GY, 1)
    edge, middle_0, low_x, high_x = kernel(
        functools.partial(edge_kernel, capacity=capacity),
        "edge",
        [
            ((halves, 8, NF, 128), F32),
            ((halves, SPLIT - 4, NF, 128), F32),
            ((STRIP + NS, cols), F32),
            ((STRIP + NS, cols), F32),
        ],
        [gz, table, stencil_index, stencil_weight, near_mask, far_mask],
        scratch=[((halves, layers * rows, 128), F32)],
        in_smem=1,
        anywhere=(5,),
        tail=5,
        cost=pl.CostEstimate(flops=3_000_000_000, bytes_accessed=2_500_000, transcendentals=0),
    )
    corners = jnp.concatenate([right, left], axis=1)
    low_x, high_x = low_x.at[STRIP:].set(corners), high_x.at[STRIP:].set(corners)
    table, low_x, high_x = lax.optimization_barrier((table, low_x, high_x))
    above = shifted(low_x, "gx", -1)
    below = shifted(high_x, "gx", 1)
    (middle_1,) = kernel(
        functools.partial(middle_kernel, first=SPLIT, capacity=capacity),
        "middle",
        [((halves, rows - 4 - SPLIT, NF, 128), F32)],
        [table, stencil_index, stencil_weight],
        cost=pl.CostEstimate(flops=3_000_000_000, bytes_accessed=1_600_000, transcendentals=0),
    )
    middles = (middle_0, middle_1)

    devices = tiles * lax.axis_size("gz")
    basis, moments = kernel(
        functools.partial(
            basis_kernel, last_gx=lax.axis_size("gx") - 1, last_gy=lax.axis_size(GY) - 1
        ),
        "basis",
        [((3, LZ + 1, XR, YR), F32), ((devices, 128), F32)],
        [gx, gy, gz, edge, *middles, near_mask, far_mask, right, left, above, below],
        scratch=[
            ((YR // 128, XR * NS, 128), F32),
            ((YR // 128, XR * 24, 128), F32),
            ((LZ + DEEP, XR, YR), F32),
            ((2, DEEP - 1, XR, YR), F32),
        ],
        in_smem=3,
        anywhere=(7, 8, 9, 10, 11),
        tail=7,
    )
    moments = lax.all_to_all(
        moments, ("gx", *GY, "gz"), split_axis=0, concat_axis=0, tiled=True
    )
    potential, wind_field, speed, balance = kernel(
        wind_kernel,
        "wind",
        [
            ((layers, rows, cols), F32),
            ((3, layers, rows, cols), F32),
            ((rows, cols), F32),
            ((rows, cols), F32),
        ],
        [
            gz,
            moments,
            basis,
            *(piece.reshape(halves, -1, 128) for piece in (edge, *middles)),
            terrain_mask,
        ],
        scratch=[((LZ + 1, XR, YR), F32), ((halves, rows * NF, 128), F32)],
        in_smem=1,
    )
    (fuel_moisture,) = kernel(
        fuel_kernel,
        "fuel",
        [((len(LAGS), rows, cols), F32)],
        [speed, swapped(speed, "gz", 1), balance, fuel_start],
        anywhere=(1,),
    )
    return (potential, wind_field, fuel_moisture)


def solution(mesh):
    placed = (
        P(("gx", *GY), None, "gz"),
        P(("gx", *GY), None),
        P(("gx", *GY)),
        P("gz", None),
        P(None, "gx", GY),
        P(None, "gx", GY),
        P("gz", "gx", GY),
        P(None, "gx", GY),
    )
    return jax.shard_map(
        shards,
        mesh=mesh,
        in_specs=placed,
        out_specs=(P("gz", "gx", GY), P(None, "gz", "gx", GY), P(None, "gx", GY)),
        check_vma=False,
    )
```
